128 devices in a mesh: ctx: 16 (over y, x), shard: 8 (over z, core).
Axes of the slice: x: 4, y: 4, z: 4, core: 2. Of those that a mesh axis runs over, the one named last changes fastest.
Arguments:
- tokens: bfloat16 [16384, 768], P(('ctx', 'shard')), may hold values from -6 to 6
- span_order: int32 [32], replicated, may hold values from 0 to 31, as said below
- first_gain: bfloat16 [768], P('shard'), may hold values from 0.5 to 1.5
- first_shift: bfloat16 [768], P('shard'), may hold values from -3 to 3
- query_weight: bfloat16 [768, 768], P('shard'), may hold values from -0.4375 to 0.4375
- query_bias: bfloat16 [768], P('shard'), may hold values from -3 to 3
- key_weight: bfloat16 [768, 768], P('shard'), may hold values from -0.21875 to 0.21875
- value_weight: bfloat16 [768, 768], P('shard'), may hold values from -0.21875 to 0.21875
- value_bias: bfloat16 [768], P('shard'), may hold values from -3 to 3
- out_weight: bfloat16 [768, 768], P('shard'), may hold values from -3.5 to 3.5
- out_bias: bfloat16 [768], P('shard'), may hold values from -3 to 3
- second_gain: bfloat16 [768], P('shard'), may hold values from 0.5 to 1.5
- second_shift: bfloat16 [768], P('shard'), may hold values from -3 to 3
- up_weight: bfloat16 [768, 3072], P('shard'), may hold values from -0.21875 to 0.21875
- up_bias: bfloat16 [3072], P('shard'), may hold values from -3 to 3
- down_weight: bfloat16 [3072, 768], P('shard'), may hold values from -0.109375 to 0.109375
- down_bias: bfloat16 [768], P('shard'), may hold values from -3 to 3
- cotangent: bfloat16 [16384, 768], P(('ctx', 'shard')), may hold values from -6 to 6
Outputs:
- activations: bfloat16 [16384, 768], P(('ctx', 'shard'))
- input_grad: float32 [16384, 768], P(('ctx', 'shard'))
- grad_first_gain: float32 [768], P('shard')
- grad_first_shift: float32 [768], P('shard')
- grad_query_weight: float32 [768, 768], P('shard')
- grad_query_bias: float32 [768], P('shard')
- grad_key_weight: float32 [768, 768], P('shard')
- grad_value_weight: float32 [768, 768], P('shard')
- grad_value_bias: float32 [768], P('shard')
- grad_out_weight: float32 [768, 768], P('shard')
- grad_out_bias: float32 [768], P('shard')
- grad_second_gain: float32 [768], P('shard')
- grad_second_shift: float32 [768], P('shard')
- grad_up_weight: float32 [768, 3072], P('shard')
- grad_up_bias: float32 [3072], P('shard')
- grad_down_weight: float32 [3072, 768], P('shard')
- grad_down_bias: float32 [768], P('shard')
The draws below stay inside these ranges and needn't reach their ends.
Inputs may be any that keep to these rules, and one draw needn't show every extreme that they name: span_order is a permutation of the 32 span numbers in which entries 2c and 2c + 1 add up to 31.
All inputs are finite; a program needn't handle non-finite values.
Results may differ from the reference program's by a relative error of at most 0.04.
Values may be sent and summed in bfloat16 or wider, within the bound.
No kernel may reach another device: no remote copies, remote signals or barrier semaphores. Data moves between devices by JAX's collectives and lax.ppermute only.
A program may use at most 192 MiB of HBM per device.

```python
import jax
import jax.numpy as jnp
from jax import lax

D = 768
HEADS = 12
HEAD_DIM = 64
FF = 3072
SEQ = 16384
SPANS = 32
SPAN = 512


def draw_span_order(key, part):
    key = jax.random.fold_in(key, 11)
    pair_key, flip_key = jax.random.split(key)
    pair_count = SPANS // 2
    low_half = jax.random.permutation(pair_key, pair_count).astype(jnp.int32)
    flip_bits = jax.random.randint(flip_key, (pair_count,), 0, 2, dtype=jnp.int32)
    leading = jnp.where(flip_bits == 1, SPANS - 1 - low_half, low_half)
    trailing = SPANS - 1 - leading
    return jnp.stack([leading, trailing], axis=1).reshape(SPANS).astype(jnp.int32)


def levels(rng, extent, cuts, low, top_value):
    factor_of = 1.0
    for position, blocks in cuts:
        draws = jax.random.uniform(jax.random.fold_in(jax.random.fold_in(rng, 6), position), (blocks,), jnp.float32, low / len(cuts), top_value / len(cuts))
        factor_of = factor_of * jnp.repeat(jnp.exp(draws), extent[position] // blocks).reshape((-1,) + (1,) * (len(extent) - 1 - position))
    return factor_of


def gaussian(rng, dims, width, reach, shards=(), held_as=jnp.bfloat16):
    drawn = width * jax.random.normal(rng, dims, jnp.float32)
    if shards:
        drawn = drawn * levels(rng, dims, shards, -0.22, 0.18)
    return jnp.clip(drawn, -reach, reach).astype(held_as)


def setup_inputs(seed: int = 0) -> dict:
    arg_keys = jax.random.split(jax.random.key(seed), 19)
    tokens = gaussian(arg_keys[0], (SEQ, D), 1.0, 6.0, ((0, 128),))
    span_order = draw_span_order(jax.random.fold_in(arg_keys[18], 71), 0)
    first_gain = jnp.clip(1.0 + 0.1 * jax.random.normal(arg_keys[2], (D,), jnp.float32), 0.5, 1.5).astype(jnp.bfloat16)
    first_shift = gaussian(arg_keys[3], (D,), 0.3, 3.0, ((0, 8),))
    query_weight = gaussian(arg_keys[4], (D, D), (D // 4) ** -0.5, 0.4375, ((0, 8),))
    query_bias = gaussian(arg_keys[5], (D,), 0.3, 3.0, ((0, 8),))
    key_weight = gaussian(arg_keys[6], (D, D), D ** -0.5, 0.21875, ((0, 8),))
    value_weight = gaussian(arg_keys[7], (D, D), D ** -0.5, 0.21875, ((0, 8),))
    value_bias = gaussian(arg_keys[8], (D,), 0.3, 3.0, ((0, 8),))
    out_weight = gaussian(arg_keys[9], (D, D), (max(1, D // 256)) ** -0.5, 3.5, ((0, 8),))
    out_bias = gaussian(arg_keys[10], (D,), 0.3, 3.0, ((0, 8),))
    second_gain = jnp.clip(1.0 + 0.1 * jax.random.normal(arg_keys[11], (D,), jnp.float32), 0.5, 1.5).astype(jnp.bfloat16)
    second_shift = gaussian(arg_keys[12], (D,), 0.3, 3.0, ((0, 8),))
    up_weight = gaussian(arg_keys[13], (D, FF), D ** -0.5, 0.21875, ((0, 8),))
    up_bias = gaussian(arg_keys[14], (FF,), 0.3, 3.0, ((0, 8),))
    down_weight = gaussian(arg_keys[15], (FF, D), FF ** -0.5, 0.109375, ((0, 8),))
    down_bias = gaussian(arg_keys[16], (D,), 0.3, 3.0, ((0, 8),))
    cotangent = gaussian(arg_keys[17], (SEQ, D), 1.0, 6.0, ((0, 128),))
    return {"tokens": tokens, "span_order": span_order, "first_gain": first_gain, "first_shift": first_shift, "query_weight": query_weight, "query_bias": query_bias, "key_weight": key_weight, "value_weight": value_weight, "value_bias": value_bias, "out_weight": out_weight, "out_bias": out_bias, "second_gain": second_gain, "second_shift": second_shift, "up_weight": up_weight, "up_bias": up_bias, "down_weight": down_weight, "down_bias": down_bias, "cotangent": cotangent}


@jax.custom_vjp
def low(v):
    return lax.optimization_barrier(v.astype(jnp.bfloat16)).astype(jnp.float32)

@jax.custom_vjp
def low_back(v):
    return v

def low_keep(v):
    return (low(v), None)

def low_pass(kept, grad):
    return (grad,)

def back_keep(v):
    return (v, None)

def back_low(kept, grad):
    return (low(grad),)
low.defvjp(low_keep, low_pass)
low_back.defvjp(back_keep, back_low)
norm_eps = 1e-05
highest = lax.Precision.HIGHEST

def norm_rows(values, gain, shift):
    center = values - lax.optimization_barrier(jnp.mean(values, axis=-1, keepdims=True))
    spread = lax.optimization_barrier(jnp.mean(center * center, axis=-1, keepdims=True))
    return center * lax.rsqrt(spread + norm_eps) * gain + shift

def product(left, right):
    return jnp.dot(left, right, precision=highest)

def attention(queries, keyset, valueset):
    block_rows = 256 if SEQ % 256 == 0 else SEQ
    block_count = SEQ // block_rows
    keys_split = keyset.reshape(SEQ, HEADS, HEAD_DIM)
    values_split = valueset.reshape(SEQ, HEADS, HEAD_DIM)
    key_place = jnp.arange(SEQ, dtype=jnp.int32)

    def one_block(block_entry):
        query_blk, query_place = block_entry
        scores = jnp.einsum('qhd,khd->hqk', query_blk, keys_split, precision=highest)
        scores = low_back(scores)
        allowed = key_place[None, None, :] <= query_place[None, :, None]
        scores = jnp.where(allowed, scores, -1e+30)
        weights = jax.nn.softmax(scores, axis=-1)
        return jnp.einsum('hqk,khd->qhd', low(weights), values_split, precision=highest)
    blocks = (queries.reshape(block_count, block_rows, HEADS, HEAD_DIM), key_place.reshape(block_count, block_rows))
    outcome = lax.map(jax.checkpoint(one_block), blocks)
    return outcome.reshape(SEQ, D)

def layer(tokens_f, first_gain, first_shift, query_weight, query_bias, key_weight, value_weight, value_bias, out_weight, out_bias, second_gain, second_shift, up_weight, up_bias, down_weight, down_bias):
    normed = low(norm_rows(tokens_f, first_gain, first_shift))
    queries = low(low_back((product(normed, query_weight) + query_bias) * 0.125))
    keyset = low(low_back(product(normed, key_weight)))
    valueset = low(low_back(product(normed, value_weight) + value_bias))
    context = low(low_back(attention(queries, keyset, valueset)))
    middle = tokens_f + low_back(product(context, out_weight) + out_bias)
    second = low(norm_rows(middle, second_gain, second_shift))
    hidden = low(jax.nn.gelu(low_back(product(second, up_weight) + up_bias)))
    return middle + product(hidden, down_weight) + down_bias

def reference(tokens, span_order, first_gain, first_shift, query_weight, query_bias, key_weight, value_weight, value_bias, out_weight, out_bias, second_gain, second_shift, up_weight, up_bias, down_weight, down_bias, cotangent):
    ranks = jnp.arange(SPANS, dtype=jnp.int32)
    inverse = jnp.zeros((SPANS,), jnp.int32).at[span_order.astype(jnp.int32)].set(ranks)

    def to_sequence(array):
        return array.reshape(SPANS, SPAN, -1)[inverse].reshape(SEQ, -1)

    def to_stored(array):
        return array.reshape(SPANS, SPAN, -1)[span_order.astype(jnp.int32)].reshape(SEQ, -1)
    params = tuple((member.astype(jnp.float32) for member in (first_gain, first_shift, query_weight, query_bias, key_weight, value_weight, value_bias, out_weight, out_bias, second_gain, second_shift, up_weight, up_bias, down_weight, down_bias)))
    start_rows = to_sequence(tokens.astype(jnp.float32))
    outcome, pullback = jax.vjp(layer, start_rows, *params)
    grads = pullback(to_sequence(cotangent.astype(jnp.float32)))
    return (to_stored(outcome).astype(jnp.bfloat16), to_stored(grads[0]), grads[1], grads[2], grads[3], grads[4], grads[5], grads[6], grads[7], grads[8], grads[9], grads[10], grads[11], grads[12], grads[13], grads[14], grads[15])
```

```python
import jax
import jax.numpy as jnp
from jax import lax
from jax.experimental import pallas as pl
from jax.experimental.pallas import tpu as pltpu
from jax.sharding import PartitionSpec as P

HEAD_DIM = 64
RING = 4
CORES = 2
GROUP_HEADS = 3
GROUP_WIDTH = GROUP_HEADS * HEAD_DIM
WIDE = 256
BLOCK = 256

norm_eps = 1e-05
lowest = -1e30
tiny = 1e-30
log2_e = 1.4426950408889634
ln_2 = 0.6931471805599453

bf16 = jnp.bfloat16
f32 = jnp.float32


def norm_rows(values, gain, shift):
    center = values - jnp.mean(values, axis=-1, keepdims=True)
    spread = jnp.mean(center * center, axis=-1, keepdims=True)
    return center * lax.rsqrt(spread + norm_eps) * gain + shift


def dense(left, right):
    return jnp.dot(left, right, preferred_element_type=f32)


def contract_rows(left, right):
    return lax.dot_general(left, right, (((0,), (0,)), ((), ())), preferred_element_type=f32)


def contract_cols(left, right):
    return lax.dot_general(left, right, (((1,), (1,)), ((), ())), preferred_element_type=f32)


def move_z(x, hops):
    size = RING * CORES
    return lax.ppermute(x, "shard", [(r, (r + CORES * hops) % size) for r in range(size)])


def swap_core(x):
    return lax.ppermute(x, "shard", [(r, r ^ 1) for r in range(RING * CORES)])


def move_x(x, hops):
    pairs = [(c, (c // RING) * RING + (c + hops) % RING) for c in range(RING * RING)]
    return lax.ppermute(x, "ctx", pairs)


def move_y(x, hops):
    size = RING * RING
    return lax.ppermute(x, "ctx", [(c, (c + RING * hops) % size) for c in range(size)])


def pick(x, at):
    return lax.dynamic_index_in_dim(x, at % RING, 0, keepdims=False)


def in_order(parts, mine):
    around = jnp.stack([parts[0], parts[3], parts[2], parts[1], parts[0], parts[3], parts[2]])
    return lax.dynamic_slice_in_dim(around, (RING - mine) % RING, RING, 0)


def spread(x, move):
    return [x] + [move(x, k) for k in range(1, RING)]


def exchange(chunks, mine, move):
    return [pick(chunks, mine)] + [move(pick(chunks, mine + k), k) for k in range(1, RING)]


def sum_parts(parts):
    total = parts[0].astype(f32)
    for part in parts[1:]:
        total = total + part.astype(f32)
    return total


def sum_over_ctx(x, y, xq):
    rows, cols = x.shape
    share = sum_parts(exchange(x.reshape(RING, rows // RING, cols), xq, move_x)).astype(bf16)
    share = share.reshape(RING, rows // RING // RING, cols)
    part = sum_parts(exchange(share, y, move_y)).astype(bf16)
    share = in_order(spread(part, move_y), y).reshape(rows // RING, cols)
    return in_order(spread(share, move_x), xq).reshape(rows, cols)


def nt(left, right):
    return lax.dot_general(left, right, (((1,), (1,)), ((), ())), preferred_element_type=f32)


def places(parity, rows, own_first):
    at = rows % BLOCK
    side = jnp.where(rows < BLOCK, parity, 1 - parity) if own_first else parity
    return (at // 128) * 256 + side * 128 + at % 128


def allowed_block(parity):
    key_at = lax.broadcasted_iota(jnp.int32, (BLOCK, 2 * BLOCK), 0)
    query_at = lax.broadcasted_iota(jnp.int32, (BLOCK, 2 * BLOCK), 1)
    return places(parity, key_at, False) <= places(parity, query_at, True)


def split3(value):
    high = value.astype(bf16).astype(f32)
    rest = value - high
    mid = rest.astype(bf16).astype(f32)
    return high, mid, rest - mid


def lanes_of(rows, first, last):
    lane = lax.broadcasted_iota(jnp.int32, (rows, WIDE), 1)
    return jnp.where((lane >= first) & (lane < last), 1.0, 0.0).astype(bf16)


def forward_kernel(meta, q_own, q_oth, kv, o_own, o_oth, k_head, v_turned, best, total, acc):
    parity = meta[16]
    for h in range(GROUP_HEADS):
        mask = lanes_of(BLOCK, HEAD_DIM * h, HEAD_DIM * (h + 1))
        for j in range(8):
            k_head[j, BLOCK * h : BLOCK * (h + 1), :] = kv[j, :, :WIDE] * mask
    for j in range(8):
        v_turned[j] = kv[j, :, 128:].astype(f32).T.astype(bf16)

    def one_span(i, carry):
        best[...] = jnp.full(best.shape, lowest, f32)
        total[...] = jnp.zeros(total.shape, f32)
        acc[...] = jnp.zeros(acc.shape, f32)

        def visit(j, masked):
            query = jnp.concatenate([q_own[i], q_oth[i]], axis=0)
            if masked:
                allowed = allowed_block(parity)
            for h in range(GROUP_HEADS):
                scores = nt(k_head[j, BLOCK * h : BLOCK * (h + 1), :], query)
                if masked:
                    scores = jnp.where(allowed, scores, lowest)
                old = best[h : h + 1, :]
                new = jnp.maximum(old, jnp.max(scores, axis=0, keepdims=True))
                weights = jnp.exp2(scores - new)
                if masked:
                    weights = jnp.where(allowed, weights, 0.0)
                fade = jnp.exp2(old - new)
                best[h : h + 1, :] = new
                total[h : h + 1, :] = total[h : h + 1, :] * fade + jnp.sum(
                    weights, axis=0, keepdims=True
                )
                here = slice(HEAD_DIM * h, HEAD_DIM * (h + 1))
                values = v_turned[j, HEAD_DIM * (h + 1) : HEAD_DIM * (h + 2), :]
                acc[here, :] = acc[here, :] * fade + dense(values, weights.astype(bf16))

        def one_block(j, carry):
            @pl.when(meta[8 + j] < meta[i])
            def _():
                visit(j, False)

            @pl.when(meta[8 + j] == meta[i])
            def _():
                visit(j, True)

            return carry

        lax.fori_loop(0, 8, one_block, 0)
        row = lax.broadcasted_iota(jnp.int32, (HEAD_DIM, 2 * BLOCK), 0)
        pieces = []
        extra = jnp.zeros((HEAD_DIM, 2 * BLOCK), f32)
        for h in range(GROUP_HEADS):
            count = jnp.maximum(total[h : h + 1, :], tiny)
            pieces.append(acc[HEAD_DIM * h : HEAD_DIM * (h + 1), :] / count)
            terms = split3(best[h : h + 1, :] + jnp.log(count) * log2_e)
            for t in range(3):
                extra = jnp.where(row == 3 * h + t, terms[t], extra)
        turned = jnp.concatenate(pieces + [extra], axis=0).T.astype(bf16)
        o_own[i] = turned[:BLOCK]
        o_oth[i] = turned[BLOCK:]
        return carry

    lax.fori_loop(0, 8, one_span, 0)


def forward_call(meta, q_own, q_oth, kv):
    vmem = pl.BlockSpec(memory_space=pltpu.VMEM)
    shape = jax.ShapeDtypeStruct((8, BLOCK, WIDE), bf16)
    return pl.pallas_call(
        forward_kernel,
        out_shape=(shape, shape),
        in_specs=[pl.BlockSpec(memory_space=pltpu.SMEM), vmem, vmem, vmem],
        out_specs=(vmem, vmem),
        scratch_shapes=[
            pltpu.VMEM((8, GROUP_HEADS * BLOCK, WIDE), bf16),
            pltpu.VMEM((8, WIDE, BLOCK), bf16),
            pltpu.VMEM((8, 2 * BLOCK), f32),
            pltpu.VMEM((8, 2 * BLOCK), f32),
            pltpu.VMEM((GROUP_WIDTH, 2 * BLOCK), f32),
        ],
        compiler_params=pltpu.CompilerParams(vmem_limit_bytes=50 * 2**20),
        name="attention_forward",
    )(meta, q_own, q_oth, kv)


def merge_kernel(*refs):
    ins, out = refs[:-1], refs[-1]
    row = lax.broadcasted_iota(jnp.int32, (WIDE, WIDE), 0)
    col = lax.broadcasted_iota(jnp.int32, (WIDE, WIDE), 1)

    def ones_at(where):
        return jnp.where(where, 1.0, 0.0).astype(bf16)

    to_lanes = ones_at((row >= 192) & (row < 201) & (col < 192) & ((row - 192) // 3 == col // 64))
    logs = [dense(x[...], to_lanes) for x in ins]
    best = logs[0]
    for part in logs[1:]:
        best = jnp.maximum(best, part)
    total = jnp.zeros_like(best)
    context = jnp.zeros_like(best)
    for x, part in zip(ins, logs):
        weight = jnp.exp2(part - best)
        total = total + weight
        context = context + weight * x[...].astype(f32)
    context = context / total
    terms = split3(best + jnp.log(total) * log2_e)
    extra = jnp.zeros_like(best)
    for t in range(3):
        back = ones_at((row < 192) & (row % 64 == 0) & (col == 192 + 3 * (row // 64) + t))
        extra = extra + dense(terms[t].astype(bf16), back)
    lane = lax.broadcasted_iota(jnp.int32, best.shape, 1)
    out[...] = jnp.where(lane < 192, context, extra).astype(bf16)


def merge_call(parts):
    rows = parts[0].shape[0]
    block = 512
    spec = pl.BlockSpec((block, WIDE), lambda i: (i, 0))
    return pl.pallas_call(
        merge_kernel,
        out_shape=jax.ShapeDtypeStruct((rows, WIDE), bf16),
        grid=(rows // block,),
        in_specs=[spec] * len(parts),
        out_specs=spec,
        compiler_params=pltpu.CompilerParams(vmem_limit_bytes=50 * 2**20),
        name="merge_partial_attention",
    )(*parts)


def pack_kernel(dcontext, context, out):
    row = lax.broadcasted_iota(jnp.int32, (GROUP_WIDTH, WIDE), 0)
    col = lax.broadcasted_iota(jnp.int32, (GROUP_WIDTH, WIDE), 1)

    def ones_at(where):
        return jnp.where(where, 1.0, 0.0).astype(bf16)

    product = dcontext[...].astype(f32) * context[:, :GROUP_WIDTH].astype(f32)
    by_head = ones_at((col < 9) & (row // 64 == col // 3))
    delta = jnp.zeros(out.shape, f32)
    for term in split3(product):
        delta = delta + dense(term.astype(bf16), by_head)
    high, mid, low = split3(delta)
    lane = lax.broadcasted_iota(jnp.int32, out.shape, 1)
    delta_terms = jnp.where(lane % 3 == 0, high, jnp.where(lane % 3 == 1, mid, low))
    row2 = lax.broadcasted_iota(jnp.int32, (WIDE, WIDE), 0)
    col2 = lax.broadcasted_iota(jnp.int32, (WIDE, WIDE), 1)
    log_terms = dense(
        context[...], ones_at((row2 >= 192) & (row2 < 201) & (col2 == row2 - 183))
    )
    shifted = dense(dcontext[...], ones_at(col == row + 64))
    out[...] = jnp.where(
        lane < 9, -delta_terms, jnp.where(lane < 18, -log_terms, shifted)
    ).astype(bf16)


def pack_call(dcontext, context):
    return pl.pallas_call(
        pack_kernel,
        out_shape=jax.ShapeDtypeStruct(context.shape, bf16),
        compiler_params=pltpu.CompilerParams(vmem_limit_bytes=50 * 2**20),
        name="pack_context_gradient",
    )(dcontext, context)


def backward_kernel(
    meta,
    q_own,
    q_oth,
    d_own,
    d_oth,
    kv,
    dq_own,
    dq_oth,
    dkv,
    k_head,
    v_head,
    k_turned,
    q_full,
    d_full,
    q_head,
    d_head,
    dq_acc,
    dk_acc,
    dv_acc,
):
    parity = meta[16]
    lane = lax.broadcasted_iota(jnp.int32, (BLOCK, 128), 1)

    def prepare_queries(i, carry):
        for side, (q_ref, d_ref) in enumerate(((q_own, d_own), (q_oth, d_oth))):
            rows = slice(BLOCK * side, BLOCK * (side + 1))
            query, grad = q_ref[i], d_ref[i]
            d_full[i, rows, :] = grad
            q_full[i, rows, :128] = query[:, :128]
            logs = pltpu.roll(grad[:, :128].astype(f32), 64, 1)
            q_full[i, rows, 128:] = jnp.where(
                lane < 64, query[:, 128:].astype(f32), logs
            ).astype(bf16)
            for h in range(GROUP_HEADS):
                there = slice(2 * BLOCK * h + BLOCK * side, 2 * BLOCK * h + BLOCK * (side + 1))
                q_head[i, there, :] = query * lanes_of(BLOCK, HEAD_DIM * h, HEAD_DIM * (h + 1))
                d_head[i, there, :] = grad * lanes_of(
                    BLOCK, HEAD_DIM * (h + 1), HEAD_DIM * (h + 2)
                )
        dq_acc[i] = jnp.zeros(dq_acc.shape[1:], f32)
        return carry

    lax.fori_loop(0, 8, prepare_queries, 0)

    def prepare_keys(j, carry):
        keys = kv[j, :, :WIDE]
        values = kv[j, :, 128:]
        for h in range(GROUP_HEADS):
            there = slice(BLOCK * h, BLOCK * (h + 1))
            k_head[j, there, :] = keys * lanes_of(
                BLOCK, HEAD_DIM * h, HEAD_DIM * (h + 1)
            ) + lanes_of(BLOCK, 201 + 3 * h, 204 + 3 * h)
            v_head[j, there, :] = values * lanes_of(
                BLOCK, HEAD_DIM * (h + 1), HEAD_DIM * (h + 2)
            ) + lanes_of(BLOCK, 3 * h, 3 * h + 3)
        k_turned[j] = keys.astype(f32).T.astype(bf16)
        return carry

    lax.fori_loop(0, 8, prepare_keys, 0)

    def one_key_block(j, carry):
        dk_acc[...] = jnp.zeros(dk_acc.shape, f32)
        dv_acc[...] = jnp.zeros(dv_acc.shape, f32)

        def visit(i, masked):
            if masked:
                allowed = allowed_block(parity)
            query = q_full[i]
            grad = d_full[i]
            all_weights = []
            all_dscores = []
            for h in range(GROUP_HEADS):
                there = slice(BLOCK * h, BLOCK * (h + 1))
                weights = jnp.exp2(nt(k_head[j, there, :], query))
                if masked:
                    weights = jnp.where(allowed, weights, 0.0)
                dscores = (weights * nt(v_head[j, there, :], grad)).astype(bf16)
                here = slice(HEAD_DIM * h, HEAD_DIM * (h + 1))
                dq_acc[i, here, :] = dq_acc[i, here, :] + dense(k_turned[j, here, :], dscores)
                all_weights.append(weights.astype(bf16))
                all_dscores.append(dscores)
            dv_acc[...] = dv_acc[...] + dense(jnp.concatenate(all_weights, axis=1), d_head[i])
            dk_acc[...] = dk_acc[...] + dense(jnp.concatenate(all_dscores, axis=1), q_head[i])

        def one_span(i, carry):
            @pl.when(meta[8 + j] < meta[i])
            def _():
                visit(i, False)

            @pl.when(meta[8 + j] == meta[i])
            def _():
                visit(i, True)

            return carry

        lax.fori_loop(0, 8, one_span, 0)
        dk = dk_acc[...] * ln_2
        dv = dv_acc[...]
        dkv[j, :, :128] = dk[:, :128].astype(bf16)
        dkv[j, :, 128:256] = jnp.where(lane < 64, dk[:, 128:], dv[:, :128]).astype(bf16)
        dkv[j, :, 256:] = dv[:, 128:].astype(bf16)
        return carry

    lax.fori_loop(0, 8, one_key_block, 0)

    def finish(i, carry):
        filled = jnp.concatenate(
            [dq_acc[i], jnp.zeros((WIDE - GROUP_WIDTH, 2 * BLOCK), f32)], axis=0
        )
        turned = filled.T.astype(bf16)
        dq_own[i] = turned[:BLOCK]
        dq_oth[i] = turned[BLOCK:]
        return carry

    lax.fori_loop(0, 8, finish, 0)


def backward_call(meta, q_own, q_oth, d_own, d_oth, kv):
    vmem = pl.BlockSpec(memory_space=pltpu.VMEM)
    shape = jax.ShapeDtypeStruct((8, BLOCK, WIDE), bf16)
    heads = GROUP_HEADS
    return pl.pallas_call(
        backward_kernel,
        out_shape=(shape, shape, jax.ShapeDtypeStruct(kv.shape, bf16)),
        in_specs=[pl.BlockSpec(memory_space=pltpu.SMEM)] + [vmem] * 5,
        out_specs=(vmem, vmem, vmem),
        scratch_shapes=[
            pltpu.VMEM((8, heads * BLOCK, WIDE), bf16),
            pltpu.VMEM((8, heads * BLOCK, WIDE), bf16),
            pltpu.VMEM((8, WIDE, BLOCK), bf16),
            pltpu.VMEM((8, 2 * BLOCK, WIDE), bf16),
            pltpu.VMEM((8, 2 * BLOCK, WIDE), bf16),
            pltpu.VMEM((8, heads * 2 * BLOCK, WIDE), bf16),
            pltpu.VMEM((8, heads * 2 * BLOCK, WIDE), bf16),
            pltpu.VMEM((8, GROUP_WIDTH, 2 * BLOCK), f32),
            pltpu.VMEM((BLOCK, WIDE), f32),
            pltpu.VMEM((BLOCK, WIDE), f32),
        ],
        compiler_params=pltpu.CompilerParams(vmem_limit_bytes=56 * 2**20),
        name="attention_backward",
    )(meta, q_own, q_oth, d_own, d_oth, kv)


def on_device(
    tokens,
    span_order,
    first_gain,
    first_shift,
    query_weight,
    query_bias,
    key_weight,
    value_weight,
    value_bias,
    out_weight,
    out_bias,
    second_gain,
    second_shift,
    up_weight,
    up_bias,
    down_weight,
    down_bias,
    cotangent,
):
    shard_at = lax.axis_index("shard")
    z, core = shard_at // CORES, shard_at % CORES
    ctx_at = lax.axis_index("ctx")
    y, xq = ctx_at // RING, ctx_at % RING
    rows, width = tokens.shape
    ranks = RING * CORES
    hidden_width = up_weight.shape[1]
    part_rows = width // ranks

    steps = jnp.arange(RING, dtype=jnp.int32)
    groups = jnp.concatenate([((y - steps) % RING) * RING + xq, y * RING + (xq - steps) % RING])
    stored = (2 * groups[:, None] + jnp.arange(2, dtype=jnp.int32)[None, :]).reshape(-1)
    found = stored[:, None] == jnp.arange(span_order.shape[0], dtype=jnp.int32)[None, :]
    spans = jnp.sum(jnp.where(found, span_order[None, :], 0), axis=1)
    meta = jnp.concatenate([spans, core[None].astype(jnp.int32)])

    vectors = jnp.concatenate(
        [
            first_gain,
            first_shift,
            query_bias,
            value_bias,
            out_bias,
            second_gain,
            second_shift,
            down_bias,
            up_bias,
        ]
    ).reshape(2, 3 * GROUP_WIDTH)
    by_place = jnp.concatenate(
        [w.reshape(part_rows, RING, GROUP_WIDTH) for w in (query_weight, key_weight, value_weight)],
        axis=2,
    ).transpose(1, 0, 2)
    sent = jnp.concatenate(
        [by_place, jnp.broadcast_to(vectors[None], (RING,) + vectors.shape)], axis=1
    )
    token_parts = spread(tokens, move_z)
    own_part = in_order(exchange(sent, z, move_z), z)
    other_part = swap_core(own_part)
    first_core = jnp.where(core == 0, own_part, other_part)
    second_core = jnp.where(core == 0, other_part, own_part)
    joined = jnp.stack([first_core, second_core], axis=1)
    w_qkv = joined[:, :, :part_rows].reshape(width, 3 * GROUP_WIDTH)
    vec = joined[:, :, part_rows:].reshape(ranks, -1)

    def vector(k):
        return vec[:, part_rows * k : part_rows * (k + 1)].reshape(-1).astype(f32)

    gain_one, shift_one, b_query, b_value, b_out, gain_two, shift_two, b_down = (
        vector(k) for k in range(8)
    )
    b_up = vec[:, 8 * part_rows :].reshape(-1).astype(f32)

    w_out = lax.all_gather(out_weight, "shard", axis=0, tiled=True)
    w_up = lax.all_gather(up_weight, "shard", axis=0, tiled=True)
    w_down = lax.all_gather(down_weight, "shard", axis=0, tiled=True)

    span_tokens = in_order(token_parts, z).reshape(RING * rows, width)
    normed_low = norm_rows(span_tokens.astype(f32), gain_one, shift_one).astype(bf16)
    projected = dense(normed_low, w_qkv)
    my_cols = GROUP_WIDTH * z
    bias_q = lax.dynamic_slice_in_dim(b_query, my_cols, GROUP_WIDTH)
    bias_v = lax.dynamic_slice_in_dim(b_value, my_cols, GROUP_WIDTH)
    queries = ((projected[:, :GROUP_WIDTH] + bias_q) * (0.125 * log2_e)).astype(bf16)
    queries = jnp.pad(queries, ((0, 0), (0, WIDE - GROUP_WIDTH)))
    kv_own = jnp.concatenate(
        [
            projected[:, GROUP_WIDTH : 2 * GROUP_WIDTH],
            projected[:, 2 * GROUP_WIDTH :] + bias_v,
        ],
        axis=1,
    ).astype(bf16)

    q_own = jnp.stack(spread(queries, move_y))
    kv_all = jnp.stack(spread(kv_own, move_x))
    q_oth = swap_core(q_own)
    q_own = q_own.reshape(8, BLOCK, WIDE)
    q_oth = q_oth.reshape(8, BLOCK, WIDE)
    kv_all = kv_all.reshape(8, BLOCK, 2 * GROUP_WIDTH)
    out_own, out_oth = forward_call(meta, q_own, q_oth, kv_all)

    swapped = swap_core(out_oth)
    merged = merge_call(
        [out_own.reshape(-1, WIDE), swapped.reshape(-1, WIDE)]
    ).reshape(RING, RING * rows, WIDE)
    context_packed = merge_call([merged[0]] + [move_y(merged[k], -k) for k in range(1, RING)])
    by_token = jnp.stack(
        [merged_part for merged_part in exchange(
            context_packed[:, :GROUP_WIDTH].reshape(RING, rows, GROUP_WIDTH), z, move_z
        )]
    )
    context_low = (
        in_order([by_token[k] for k in range(RING)], z).transpose(1, 0, 2).reshape(rows, width)
    )

    tokens_f = tokens.astype(f32)
    middle = tokens_f + dense(context_low, w_out) + b_out
    second, second_back = jax.vjp(norm_rows, middle, gain_two, shift_two)
    second_low = second.astype(bf16)
    pre_act = dense(second_low, w_up) + b_up
    hidden, gelu_back = jax.vjp(jax.nn.gelu, pre_act)
    hidden_low = hidden.astype(bf16)
    activations = (middle + dense(hidden_low, w_down) + b_down).astype(bf16)
    upstream = cotangent.astype(f32)
    grad_down_bias = jnp.sum(upstream, axis=0)
    dpre = gelu_back(contract_cols(cotangent, w_down))[0].astype(bf16)
    grad_up_bias = jnp.sum(dpre.astype(f32), axis=0)
    dmid_norm, grad_second_gain, grad_second_shift = second_back(contract_cols(dpre, w_up))
    dmiddle = upstream + dmid_norm
    dmid_low = dmiddle.astype(bf16)
    grad_out_bias = jnp.sum(dmid_low.astype(f32), axis=0)
    dcontext = contract_cols(dmid_low, w_out).astype(bf16)

    dcontext_mine = in_order(
        exchange(dcontext.reshape(rows, RING, GROUP_WIDTH).transpose(1, 0, 2), z, move_z), z
    ).reshape(RING * rows, GROUP_WIDTH)
    packed = pack_call(dcontext_mine, context_packed)
    d_own = jnp.stack(spread(packed, move_y))
    d_oth = swap_core(d_own)
    dq_own, dq_oth, dkv = backward_call(
        meta,
        q_own,
        q_oth,
        d_own.reshape(8, BLOCK, WIDE),
        d_oth.reshape(8, BLOCK, WIDE),
        kv_all,
    )

    def columns(x):
        return x.reshape(rows, RING, -1).transpose(1, 0, 2)

    def tokens_joined(parts):
        return in_order(parts, z).reshape(RING * rows, -1)

    cot_z = tokens_joined(spread(cotangent, move_z))
    hidden_z = tokens_joined(exchange(columns(hidden_low), z, move_z))
    second_z = tokens_joined(exchange(columns(second_low), z, move_z))
    dpre_z = tokens_joined(spread(dpre, move_z))
    dmid_z = tokens_joined(spread(dmid_low, move_z))
    grad_down = contract_rows(hidden_z, cot_z)
    grad_up = contract_rows(second_z, dpre_z)
    grad_out = contract_rows(context_packed[:, :GROUP_WIDTH], dmid_z)

    def core_half(x, at):
        half = x.shape[0] // CORES
        return lax.dynamic_slice_in_dim(x, at * half, half, 0)

    def rank_rows(at):
        up = core_half(grad_up, at)
        return jnp.concatenate(
            [core_half(grad_down, at), core_half(grad_out, at)]
            + [up[:, width * k : width * (k + 1)] for k in range(hidden_width // width)],
            axis=0,
        )

    early = rank_rows(core) + swap_core(rank_rows(1 - core).astype(bf16)).astype(f32)
    early = jnp.pad(early.astype(bf16), ((0, 32), (0, 0)))
    early = sum_over_ctx(early, y, xq).astype(f32)
    grad_down_weight = early[: 4 * part_rows]
    grad_out_weight = early[4 * part_rows : 5 * part_rows]
    grad_up_weight = jnp.concatenate(
        [early[(5 + k) * part_rows : (6 + k) * part_rows] for k in range(hidden_width // width)],
        axis=1,
    )

    dq_mine = dq_own.astype(f32) + swap_core(dq_oth).astype(f32)
    dq_mine = dq_mine.astype(bf16).reshape(RING, RING * rows, WIDE)
    dq_sum = sum_parts([dq_mine[0]] + [move_y(dq_mine[k], -k) for k in range(1, RING)])
    dkv_parts = dkv.reshape(RING, RING * rows, 2 * GROUP_WIDTH)
    dkv_sum = sum_parts([dkv_parts[0]] + [move_x(dkv_parts[k], -k) for k in range(1, RING)])
    dq_low = dq_sum[:, :GROUP_WIDTH].astype(bf16) * bf16(0.125)
    dqkv = jnp.concatenate([dq_low, dkv_sum.astype(bf16)], axis=1)
    grad_qkv = contract_rows(normed_low, dqkv).astype(bf16)
    bias_grads = jnp.sum(dqkv.astype(f32), axis=0)

    dnormed_part = contract_cols(dqkv, w_qkv).astype(bf16).reshape(RING, rows, width)
    dnormed = sum_parts(exchange(dnormed_part, z, move_z))
    _, first_back = jax.vjp(norm_rows, tokens_f, gain_one, shift_one)
    dtok_norm, grad_first_gain, grad_first_shift = first_back(dnormed)
    input_grad = dmiddle + dtok_norm

    def placed(x):
        return lax.dynamic_update_slice(jnp.zeros((width,), f32), x, (my_cols,))

    vec_grads = jnp.concatenate(
        [
            v.reshape(ranks, -1)
            for v in (
                grad_first_gain,
                grad_first_shift,
                placed(bias_grads[:GROUP_WIDTH]),
                placed(bias_grads[2 * GROUP_WIDTH :]),
                grad_out_bias,
                grad_second_gain,
                grad_second_shift,
                grad_down_bias,
                grad_up_bias,
            )
        ],
        axis=1,
    )
    vec_rows = vec_grads.astype(bf16).reshape(RING, CORES * 2, 3 * GROUP_WIDTH)
    weight_rows = grad_qkv.reshape(RING, CORES * part_rows, 3 * GROUP_WIDTH)
    late_parts = exchange(jnp.concatenate([weight_rows, vec_rows], axis=1), z, move_z)
    weight_cols = in_order(late_parts, z)[:, : CORES * part_rows].reshape(
        RING, CORES, part_rows, 3 * GROUP_WIDTH
    )
    vec_sum = sum_parts([part[CORES * part_rows :] for part in late_parts]).reshape(
        CORES, 2, 3 * GROUP_WIDTH
    )

    def late_rows(at):
        mine = lax.dynamic_index_in_dim(weight_cols, at, 1, keepdims=False)
        return jnp.concatenate(
            [
                mine.reshape(RING * part_rows, 3 * GROUP_WIDTH),
                lax.dynamic_index_in_dim(vec_sum, at, 0, keepdims=False).astype(bf16),
            ],
            axis=0,
        )

    late = late_rows(core).astype(f32) + swap_core(late_rows(1 - core)).astype(f32)
    late = jnp.pad(late.astype(bf16), ((0, 512 - late.shape[0]), (0, 0)))
    late = sum_over_ctx(late, y, xq).astype(f32)
    late_weights = late[: RING * part_rows].reshape(RING, part_rows, 3, GROUP_WIDTH)
    late_weights = late_weights.transpose(2, 1, 0, 3).reshape(3, part_rows, width)
    late_vec = late[RING * part_rows : RING * part_rows + 2].reshape(-1)

    def late_vector(k):
        return late_vec[part_rows * k : part_rows * (k + 1)]

    return (
        activations,
        input_grad,
        late_vector(0),
        late_vector(1),
        late_weights[0],
        late_vector(2),
        late_weights[1],
        late_weights[2],
        late_vector(3),
        grad_out_weight,
        late_vector(4),
        late_vector(5),
        late_vector(6),
        grad_up_weight,
        late_vec[8 * part_rows :],
        grad_down_weight,
        late_vector(7),
    )


def solution(mesh):
    tokens_spec = P(("ctx", "shard"), None)
    vector_spec = P("shard")
    matrix_spec = P("shard", None)
    return jax.shard_map(
        on_device,
        mesh=mesh,
        in_specs=(
            tokens_spec,
            P(),
            vector_spec,
            vector_spec,
            matrix_spec,
            vector_spec,
            matrix_spec,
            matrix_spec,
            vector_spec,
            matrix_spec,
            vector_spec,
            vector_spec,
            vector_spec,
            matrix_spec,
            vector_spec,
            matrix_spec,
            vector_spec,
            tokens_spec,
        ),
        out_specs=(
            tokens_spec,
            tokens_spec,
            vector_spec,
            vector_spec,
            matrix_spec,
            vector_spec,
            matrix_spec,
            matrix_spec,
            vector_spec,
            matrix_spec,
            vector_spec,
            vector_spec,
            vector_spec,
            matrix_spec,
            vector_spec,
            matrix_spec,
            vector_spec,
        ),
        check_vma=False,
    )
```

```python
import jax
import jax.numpy as jnp
from jax import lax
from jax.experimental import pallas as pl
from jax.experimental.pallas import tpu as pltpu
from jax.sharding import PartitionSpec as P

HEAD_DIM = 64
RING = 4
CORES = 2
GROUP_HEADS = 3
GROUP_WIDTH = GROUP_HEADS * HEAD_DIM
WIDE = 256
BLOCK = 256

norm_eps = 1e-05
lowest = -1e30
tiny = 1e-30
log2_e = 1.4426950408889634
ln_2 = 0.6931471805599453

bf16 = jnp.bfloat16
f32 = jnp.float32


def dense(left, right):
    return jnp.dot(left, right, preferred_element_type=f32)


def nt(left, right):
    return lax.dot_general(left, right, (((1,), (1,)), ((), ())), preferred_element_type=f32)


def tn(left, right):
    return lax.dot_general(left, right, (((0,), (0,)), ((), ())), preferred_element_type=f32)


def move_z(x, hops):
    size = RING * CORES
    return lax.ppermute(x, "shard", [(r, (r + CORES * hops) % size) for r in range(size)])


def swap_core(x):
    return lax.ppermute(x, "shard", [(r, r ^ 1) for r in range(RING * CORES)])


def move_x(x, hops):
    pairs = [(c, (c // RING) * RING + (c + hops) % RING) for c in range(RING * RING)]
    return lax.ppermute(x, "ctx", pairs)


def move_y(x, hops):
    size = RING * RING
    return lax.ppermute(x, "ctx", [(c, (c + RING * hops) % size) for c in range(size)])


def spread(x, move):
    return [x] + [move(x, k) for k in range(1, RING)]


def deliver(chunks, move):
    return [chunks[0]] + [move(chunks[k], k) for k in range(1, RING)]


def give_back(chunks, move):
    return [chunks[0]] + [move(chunks[k], -k) for k in range(1, RING)]


def sum_low(parts):
    total = parts[0].astype(f32)
    for part in parts[1:]:
        total = total + part.astype(f32)
    return total.astype(bf16)


def sum_over_ctx(chunks):
    share = sum_low(deliver(chunks, move_x))
    return spread(sum_low(spread(share, move_y)), move_x)


VM = pl.BlockSpec(memory_space=pltpu.VMEM)
SM = pl.BlockSpec(memory_space=pltpu.SMEM)


def run(kernel, name, outs, args, scratch=(), specs=None, cost=None):
    return pl.pallas_call(
        kernel,
        out_shape=tuple(jax.ShapeDtypeStruct(shape, dtype) for shape, dtype in outs),
        in_specs=specs or [SM] + [VM] * (len(args) - 1),
        out_specs=tuple(VM for _ in outs),
        scratch_shapes=list(scratch),
        cost_estimate=cost,
        compiler_params=pltpu.CompilerParams(vmem_limit_bytes=56 * 2**20),
        name=name,
    )(*args)


def turn(at, size=RING):
    return lax.rem(at + size, size)


def tile(x, k):
    return x[:, 128 * k : 128 * (k + 1)]


def pieces(sources):
    made = []
    rows = next(source for source in sources if source is not None)[0].shape[0]
    for left, right in zip(sources[::2], sources[1::2]):
        sides = []
        for side, source in enumerate((left, right)):
            if source is None:
                sides.append(None)
                continue
            value = tile(source[0], source[1] // 2).astype(f32)
            sides.append(value if source[1] % 2 == side else pltpu.roll(value, 64, 1))
        low, high = (jnp.zeros((rows, 128), f32) if part is None else part for part in sides)
        lane = lax.broadcasted_iota(jnp.int32, (rows, 128), 1)
        made.append(jnp.where(lane < 64, low, high))
    return jnp.concatenate(made, axis=1)


def lanes_of(rows, first, last):
    lane = lax.broadcasted_iota(jnp.int32, (rows, WIDE), 1)
    return jnp.where((lane >= first) & (lane < last), 1.0, 0.0).astype(bf16)


def put_by_distance(refs, place, at, value):
    for k in range(RING):

        @pl.when(turn(at - place) == k)
        def _(k=k):
            refs[k][...] = value


def split3(value):
    high = value.astype(bf16).astype(f32)
    rest = value - high
    mid = rest.astype(bf16).astype(f32)
    return high, mid, rest - mid


def arrange_kernel(meta, wk, wv, wq, vec, *outs):
    for t in range(RING):
        parts = [(w, 3 * t + n) for w in (wk, wv, wq) for n in range(3)] + [None]
        chunk = pieces(parts).astype(bf16)
        filled = jnp.concatenate(
            [chunk, jnp.concatenate([vec[...], jnp.zeros((16, 512), bf16)], axis=1)], axis=0
        )
        put_by_distance(outs, meta[17], t, filled)


def center_rows(values):
    center = values - jnp.mean(values, axis=-1, keepdims=True)
    spread_ = jnp.mean(center * center, axis=-1, keepdims=True)
    scale = lax.rsqrt(spread_ + norm_eps)
    return center * scale, scale


def project_kernel(meta, *refs):
    toks, ws, others = refs[:4], refs[4:8], refs[8:12]
    span_tokens, normed, queries, kv, w_out, vec_out, up_out, vec_in = refs[12:]
    core, z = meta[16], meta[17]
    for k in range(RING):
        place = turn(z - k)
        span_tokens[pl.ds(pl.multiple_of(place * 128, 128), 128), :] = toks[k][...]
        for source, side in ((ws[k], core), (others[k], 1 - core)):
            rank = 2 * place + side
            w_out[pl.ds(pl.multiple_of(rank * 96, 32), 96), :] = source[:96, :]
            vec_in[rank] = source[96:112, :128]
    row = lax.broadcasted_iota(jnp.int32, (128, 768), 0)
    col = lax.broadcasted_iota(jnp.int32, (128, 768), 1)
    vec = jnp.zeros((16, 768), f32)
    for rank in range(2 * RING):
        there = jnp.where((row < 96) & (col == row + 96 * rank), 1.0, 0.0).astype(bf16)
        vec = vec + dense(vec_in[rank], there)
    vec_out[...] = vec
    row = lax.broadcasted_iota(jnp.int32, (128, 384), 0)
    col = lax.broadcasted_iota(jnp.int32, (128, 384), 1)
    for rank in range(2 * RING):
        line = jnp.zeros((1, 384), f32)
        for n in range(4):
            there = jnp.where((row < 96) & (col == row + 96 * n), 1.0, 0.0).astype(bf16)
            line = line + dense(vec_in[rank], there)[8 + n : 9 + n, :]
        up_out[:, 384 * rank : 384 * (rank + 1)] = line
    xhat, _ = center_rows(span_tokens[...].astype(f32))
    low = (xhat * vec[0:1, :] + vec[1:2, :]).astype(bf16)
    normed[...] = low
    bias = jnp.zeros((8, 640), f32)
    bias_q = jnp.broadcast_to(vec[2:3, :], (8, 768))
    bias_v = jnp.broadcast_to(vec[3:4, :], (8, 768))
    for t in range(RING):
        here = pieces(
            [None] * 3
            + [(bias_v, 3 * t + n) for n in range(3)]
            + [(bias_q, 3 * t + n) for n in range(3)]
            + [None]
        )
        bias = jnp.where(z == t, here, bias)
    projected = dense(low, w_out[...]) + bias[0:1, :]
    kv[...] = projected[:, :384].astype(bf16)
    queries[...] = (projected[:, 384:] * (0.125 * log2_e)).astype(bf16)


def places(parity, rows, own_first):
    at = rows % BLOCK
    side = jnp.where(rows < BLOCK, parity, 1 - parity) if own_first else parity
    return (at // 128) * 256 + side * 128 + at % 128


def allowed_block(parity):
    key_at = lax.broadcasted_iota(jnp.int32, (BLOCK, 2 * BLOCK), 0)
    query_at = lax.broadcasted_iota(jnp.int32, (BLOCK, 2 * BLOCK), 1)
    return places(parity, key_at, False) <= places(parity, query_at, True)


def forward_kernel(meta, *refs):
    q_own, q_oth, kvs, o_own, o_oth = (refs[4 * n : 4 * (n + 1)] for n in range(5))
    k_head, v_turned, q_turned, best, acc, out = refs[20:]
    parity = meta[16]
    for h in range(GROUP_HEADS):
        mask = lanes_of(BLOCK, HEAD_DIM * h, HEAD_DIM * (h + 1))
        for j in range(8):
            rows = slice(BLOCK * (j % 2), BLOCK * (j % 2 + 1))
            k_head[j, BLOCK * h : BLOCK * (h + 1), :] = kvs[j // 2][rows, :WIDE] * mask
    for j in range(8):
        rows = slice(BLOCK * (j % 2), BLOCK * (j % 2 + 1))
        turned = kvs[j // 2][rows, 128:].astype(f32).T.astype(bf16)
        for h in range(GROUP_HEADS):
            v_turned[j, 80 * h : 80 * h + 64, :] = turned[64 * (h + 1) : 64 * (h + 2)]
            v_turned[j, 80 * h + 64 : 80 * h + 80, :] = jnp.ones((16, BLOCK), bf16)
        query = jnp.concatenate([q_own[j // 2][rows, :], q_oth[j // 2][rows, :]], axis=0)
        q_turned[j] = query.astype(f32).T.astype(bf16)

    def one_span(i, carry):
        best[...] = jnp.full(best.shape, lowest, f32)
        acc[...] = jnp.zeros(acc.shape, f32)

        def visit(j, masked):
            if masked:
                allowed = allowed_block(parity)
            every = [
                dense(k_head[j, BLOCK * h : BLOCK * (h + 1), :], q_turned[i])
                for h in range(GROUP_HEADS)
            ]
            fades, lows = [], []
            for h in range(GROUP_HEADS):
                scores = every[h]
                if masked:
                    scores = jnp.where(allowed, scores, lowest)
                old = best[h : h + 1, :]
                new = jnp.maximum(old, jnp.max(scores, axis=0, keepdims=True))
                weights = jnp.exp2(scores - new)
                if masked:
                    weights = jnp.where(allowed, weights, 0.0)
                best[h : h + 1, :] = new
                lows.append(weights.astype(bf16))
                fades.append(jnp.exp2(old - new))
            for h in range(GROUP_HEADS):
                here = slice(80 * h, 80 * (h + 1))
                acc[here, :] = acc[here, :] * fades[h] + dense(v_turned[j, here, :], lows[h])

        def one_block(j, carry):
            @pl.when(meta[8 + j] < meta[i])
            def _():
                visit(j, False)

            @pl.when(meta[8 + j] == meta[i])
            def _():
                visit(j, True)

            return carry

        lax.fori_loop(0, 8, one_block, 0)
        row = lax.broadcasted_iota(jnp.int32, (HEAD_DIM, 2 * BLOCK), 0)
        parts = []
        extra = jnp.zeros((HEAD_DIM, 2 * BLOCK), f32)
        for h in range(GROUP_HEADS):
            count = jnp.maximum(acc[80 * h + 64 : 80 * h + 65, :], tiny)
            parts.append(acc[80 * h : 80 * h + 64, :] / count)
            terms = split3(best[h : h + 1, :] + jnp.log(count) * log2_e)
            for t in range(3):
                extra = jnp.where(row == 3 * h + t, terms[t], extra)
        out[i] = jnp.concatenate(parts + [extra], axis=0).T.astype(bf16)
        return carry

    lax.fori_loop(0, 8, one_span, 0)
    for i in range(8):
        rows = slice(BLOCK * (i % 2), BLOCK * (i % 2 + 1))
        o_own[i // 2][rows, :] = out[i, :BLOCK, :]
        o_oth[i // 2][rows, :] = out[i, BLOCK:, :]


def forward_call(meta, q_own, q_oth, kvs):
    outs = run(
        forward_kernel,
        "attention_forward",
        [((2 * BLOCK, WIDE), bf16)] * 8,
        (meta, *q_own, *q_oth, *kvs),
        scratch=[
            pltpu.VMEM((8, GROUP_HEADS * BLOCK, WIDE), bf16),
            pltpu.VMEM((8, 240, BLOCK), bf16),
            pltpu.VMEM((8, WIDE, 2 * BLOCK), bf16),
            pltpu.VMEM((8, 2 * BLOCK), f32),
            pltpu.VMEM((240, 2 * BLOCK), f32),
            pltpu.VMEM((8, 2 * BLOCK, WIDE), bf16),
        ],
        cost=pl.CostEstimate(flops=20 * 10**9, bytes_accessed=10**7, transcendentals=13 * 10**6),
    )
    return outs[:4], outs[4:]


def one_hot(where):
    return jnp.where(where, 1.0, 0.0).astype(bf16)


def merge_rows(parts):
    row = lax.broadcasted_iota(jnp.int32, (WIDE, WIDE), 0)
    col = lax.broadcasted_iota(jnp.int32, (WIDE, WIDE), 1)
    to_lanes = one_hot((row >= 192) & (row < 201) & (col < 192) & ((row - 192) // 3 == col // 64))
    logs = [dense(part, to_lanes) for part in parts]
    best = logs[0]
    for part in logs[1:]:
        best = jnp.maximum(best, part)
    total = jnp.zeros_like(best)
    context = jnp.zeros_like(best)
    for part, log in zip(parts, logs):
        weight = jnp.exp2(log - best)
        total = total + weight
        context = context + weight * part.astype(f32)
    context = context / total
    terms = split3(best + jnp.log(total) * log2_e)
    extra = jnp.zeros_like(best)
    for t in range(3):
        back = one_hot((row < 192) & (row % 64 == 0) & (col == 192 + 3 * (row // 64) + t))
        extra = extra + dense(terms[t].astype(bf16), back)
    lane = lax.broadcasted_iota(jnp.int32, best.shape, 1)
    return jnp.where(lane < 192, context, extra).astype(bf16)


def merge_cores_kernel(meta, *refs):
    for k in range(RING):
        refs[8 + k][...] = merge_rows([refs[k][...], refs[4 + k][...]])


def merge_groups_kernel(meta, *refs):
    whole = refs[4]
    whole[...] = merge_rows([ref[...] for ref in refs[:4]])
    for k in range(RING):
        rows = pl.ds(pl.multiple_of(turn(meta[17] + k - RING) * 128, 128), 128)
        refs[5 + k][...] = whole[rows, :]


def middle_kernel(meta, *refs):
    tokens, cot = refs[:2]
    contexts = refs[2:6]
    w_out, up_far, down_far, vec, b_up = refs[6:11]
    act, dmiddle_out, dmid_out, second_out = refs[11:15]
    hiddens, dpres, dcontexts = refs[15:19], refs[19:23], refs[23:27]
    sums, sum_up, w_up, w_down, up_done, down_done = refs[27:]
    z = meta[17]
    up_copy = pltpu.make_async_copy(up_far, w_up, up_done)
    down_copy = pltpu.make_async_copy(down_far, w_down, down_done)
    up_copy.start()
    down_copy.start()
    middle = tokens[...].astype(f32) + vec[4:5, :]
    for k in range(RING):
        rows = pl.ds(pl.multiple_of(turn(z - k) * GROUP_WIDTH, 64), GROUP_WIDTH)
        middle = middle + dense(contexts[k][:, :GROUP_WIDTH], w_out[rows, :])
    xhat, scale = center_rows(middle)
    gain = vec[5:6, :]
    second = (xhat * gain + vec[6:7, :]).astype(bf16)
    second_out[...] = second
    cot_low = cot[...]
    up_copy.wait()
    down_copy.wait()
    total = middle + vec[7:8, :]
    dsecond = jnp.zeros_like(middle)
    width = 768
    for n in range(RING):
        cols = slice(width * n, width * (n + 1))
        pre = dense(second, w_up[:, cols]) + b_up[:, cols]
        square = pre * pre
        inner = jnp.tanh(0.7978845608028654 * (pre + 0.044715 * (square * pre)))
        half = 0.5 * (1.0 + inner)
        hidden = (pre * half).astype(bf16)
        slope = half + (0.5 * 0.7978845608028654) * pre * (1.0 - inner * inner) * (
            1.0 + 3.0 * 0.044715 * square
        )
        total = total + dense(hidden, w_down[cols, :])
        dpre = (nt(cot_low, w_down[cols, :]) * slope).astype(bf16)
        dsecond = dsecond + nt(dpre, w_up[:, cols])
        sum_up[:, cols] = jnp.sum(dpre.astype(f32), axis=0, keepdims=True)
        put_by_distance(hiddens, z, n, hidden)
        put_by_distance(dpres, z, n, dpre)
    act[...] = total.astype(bf16)
    grad = dsecond * gain
    dnorm = scale * (
        grad
        - jnp.mean(grad, axis=-1, keepdims=True)
        - xhat * jnp.mean(grad * xhat, axis=-1, keepdims=True)
    )
    upstream = cot_low.astype(f32)
    dmiddle = upstream + dnorm
    dmiddle_out[...] = dmiddle
    dmid = dmiddle.astype(bf16)
    dmid_out[...] = dmid
    for t in range(RING):
        rows = slice(GROUP_WIDTH * t, GROUP_WIDTH * (t + 1))
        put_by_distance(dcontexts, z, t, nt(dmid, w_out[rows, :]).astype(bf16))
    row = lax.broadcasted_iota(jnp.int32, (8, width), 0)
    lines = (
        dmid.astype(f32),
        dsecond * xhat,
        dsecond,
        upstream,
    )
    gathered = jnp.zeros((8, width), f32)
    for n, line in enumerate(lines):
        gathered = jnp.where(row == 4 + n, jnp.sum(line, axis=0, keepdims=True), gathered)
    sums[...] = gathered


def pack_kernel(meta, d0, d1, d2, d3, context, out, dcontext):
    for k, part in enumerate((d0, d1, d2, d3)):
        dcontext[pl.ds(pl.multiple_of(turn(meta[17] - k) * 128, 128), 128), :] = part[...]
    row = lax.broadcasted_iota(jnp.int32, (GROUP_WIDTH, WIDE), 0)
    col = lax.broadcasted_iota(jnp.int32, (GROUP_WIDTH, WIDE), 1)
    product = dcontext[...].astype(f32) * context[:, :GROUP_WIDTH].astype(f32)
    by_head = one_hot((col < 9) & (row // 64 == col // 3))
    delta = jnp.zeros(out.shape, f32)
    for term in split3(product):
        delta = delta + dense(term.astype(bf16), by_head)
    high, mid, low = split3(delta)
    lane = lax.broadcasted_iota(jnp.int32, out.shape, 1)
    delta_terms = jnp.where(lane % 3 == 0, high, jnp.where(lane % 3 == 1, mid, low))
    row2 = lax.broadcasted_iota(jnp.int32, (WIDE, WIDE), 0)
    col2 = lax.broadcasted_iota(jnp.int32, (WIDE, WIDE), 1)
    log_terms = dense(context[...], one_hot((row2 >= 192) & (row2 < 201) & (col2 == row2 - 183)))
    shifted = dense(dcontext[...], one_hot(col == row + 64))
    out[...] = jnp.where(
        lane < 9, -delta_terms, jnp.where(lane < 18, -log_terms, shifted)
    ).astype(bf16)


def backward_kernel(first_block, last, meta, *refs):
    q_own, q_oth, d_own, d_oth = (refs[4 * n : 4 * (n + 1)] for n in range(4))
    kvs = refs[16:18]
    if last:
        dq_in = refs[18]
        dq_own, dq_oth, dkvs = refs[19:23], refs[23:27], refs[27:29]
        dq_acc = refs[29]
        scratch = refs[30:]
    else:
        dkvs, dq_acc = refs[18:20], refs[20]
        scratch = refs[21:]
    k_head, v_head, k_turned, q_full, d_full, kv, dkv, dk_acc, dv_acc = scratch
    parity = meta[16]
    lane = lax.broadcasted_iota(jnp.int32, (BLOCK, 128), 1)
    for i in range(8):
        there = slice(BLOCK * (i % 2), BLOCK * (i % 2 + 1))
        for side, (q_refs, d_refs) in enumerate(((q_own, d_own), (q_oth, d_oth))):
            rows = slice(BLOCK * side, BLOCK * (side + 1))
            grad = d_refs[i // 2][there, :]
            d_full[i, rows, :] = grad
            q_full[i, rows, :128] = q_refs[i // 2][there, :128]
            logs = pltpu.roll(grad[:, :128].astype(f32), 64, 1)
            q_full[i, rows, 128:] = jnp.where(
                lane < 64, q_refs[i // 2][there, 128:].astype(f32), logs
            ).astype(bf16)
        dq_acc[i] = dq_in[i] if last else jnp.zeros(dq_acc.shape[1:], f32)
    for j in range(4):
        kv[j] = kvs[j // 2][BLOCK * (j % 2) : BLOCK * (j % 2 + 1), :]

    def one_key_block(j, carry):
        keys = kv[j, :, :WIDE]
        values = kv[j, :, 128:]
        for h in range(GROUP_HEADS):
            there = slice(BLOCK * h, BLOCK * (h + 1))
            k_head[there, :] = keys * lanes_of(
                BLOCK, HEAD_DIM * h, HEAD_DIM * (h + 1)
            ) + lanes_of(BLOCK, 201 + 3 * h, 204 + 3 * h)
            v_head[there, :] = values * lanes_of(
                BLOCK, HEAD_DIM * (h + 1), HEAD_DIM * (h + 2)
            ) + lanes_of(BLOCK, 3 * h, 3 * h + 3)
        k_turned[...] = keys.astype(f32).T.astype(bf16)
        dk_acc[...] = jnp.zeros(dk_acc.shape, f32)
        dv_acc[...] = jnp.zeros(dv_acc.shape, f32)
        key_span = meta[8 + turn(first_block + j - 8, 8)]

        def visit(i, masked):
            if masked:
                allowed = allowed_block(parity)
            query = q_full[i]
            grad = d_full[i]
            heads = [slice(BLOCK * h, BLOCK * (h + 1)) for h in range(GROUP_HEADS)]
            scores = [nt(k_head[there, :], query) for there in heads]
            dprobs = [nt(v_head[there, :], grad) for there in heads]
            all_weights = []
            all_dscores = []
            for h in range(GROUP_HEADS):
                weights = jnp.exp2(scores[h])
                if masked:
                    weights = jnp.where(allowed, weights, 0.0)
                all_weights.append(weights.astype(bf16))
                all_dscores.append((weights * dprobs[h]).astype(bf16))
            d_heads = jnp.concatenate(
                [
                    grad * lanes_of(2 * BLOCK, HEAD_DIM * (h + 1), HEAD_DIM * (h + 2))
                    for h in range(GROUP_HEADS)
                ],
                axis=0,
            )
            q_heads = jnp.concatenate(
                [
                    query * lanes_of(2 * BLOCK, HEAD_DIM * h, HEAD_DIM * (h + 1))
                    for h in range(GROUP_HEADS)
                ],
                axis=0,
            )
            dv_acc[...] = dv_acc[...] + dense(jnp.concatenate(all_weights, axis=1), d_heads)
            dk_acc[...] = dk_acc[...] + dense(jnp.concatenate(all_dscores, axis=1), q_heads)
            for h in range(GROUP_HEADS):
                here = slice(HEAD_DIM * h, HEAD_DIM * (h + 1))
                dq_acc[i, here, :] = dq_acc[i, here, :] + dense(k_turned[here, :], all_dscores[h])

        def one_span(i, carry):
            @pl.when(key_span < meta[i])
            def _():
                visit(i, False)

            @pl.when(key_span == meta[i])
            def _():
                visit(i, True)

            return carry

        lax.fori_loop(0, 8, one_span, 0)
        dk = dk_acc[...] * ln_2
        dv = dv_acc[...]
        dkv[j, :, :128] = dk[:, :128].astype(bf16)
        dkv[j, :, 128:256] = jnp.where(lane < 64, dk[:, 128:], dv[:, :128]).astype(bf16)
        dkv[j, :, 256:] = dv[:, 128:].astype(bf16)
        return carry

    lax.fori_loop(0, 4, one_key_block, 0)
    for j in range(4):
        dkvs[j // 2][BLOCK * (j % 2) : BLOCK * (j % 2 + 1), :] = dkv[j]
    if last:
        for i in range(8):
            there = slice(BLOCK * (i % 2), BLOCK * (i % 2 + 1))
            filled = jnp.concatenate(
                [dq_acc[i], jnp.zeros((WIDE - GROUP_WIDTH, 2 * BLOCK), f32)], axis=0
            )
            turned = filled.T.astype(bf16)
            dq_own[i // 2][there, :] = turned[:BLOCK]
            dq_oth[i // 2][there, :] = turned[BLOCK:]


def backward_call(first_block, last, meta, q_own, q_oth, d_own, d_oth, kvs, dq_in=None):
    part = ((2 * BLOCK, WIDE), bf16)
    kv_part = ((2 * BLOCK, 2 * GROUP_WIDTH), bf16)
    dq_shape = (8, GROUP_WIDTH, 2 * BLOCK)
    if last:
        outs, extra, accs = [part] * 8 + [kv_part] * 2, (dq_in,), [pltpu.VMEM(dq_shape, f32)]
    else:
        outs, extra, accs = [kv_part] * 2 + [(dq_shape, f32)], (), []
    return run(
        lambda *refs: backward_kernel(first_block, last, *refs),
        "attention_backward_rest" if last else "attention_backward",
        outs,
        (meta, *q_own, *q_oth, *d_own, *d_oth, *kvs, *extra),
        scratch=accs
        + [
            pltpu.VMEM((GROUP_HEADS * BLOCK, WIDE), bf16),
            pltpu.VMEM((GROUP_HEADS * BLOCK, WIDE), bf16),
            pltpu.VMEM((WIDE, BLOCK), bf16),
            pltpu.VMEM((8, 2 * BLOCK, WIDE), bf16),
            pltpu.VMEM((8, 2 * BLOCK, WIDE), bf16),
            pltpu.VMEM((4, BLOCK, 2 * GROUP_WIDTH), bf16),
            pltpu.VMEM((4, BLOCK, 2 * GROUP_WIDTH), bf16),
            pltpu.VMEM((BLOCK, WIDE), f32),
            pltpu.VMEM((BLOCK, WIDE), f32),
        ],
        cost=pl.CostEstimate(flops=20 * 10**9, bytes_accessed=10**7, transcendentals=7 * 10**6),
    )


def early_kernel(meta, *refs):
    hiddens, cots, dpres, seconds, dmids = (refs[4 * n : 4 * (n + 1)] for n in range(5))
    context = refs[20]
    keep, send = refs[21:23]
    ups = refs[23:27]
    grad = refs[27]
    core, z = meta[16], meta[17]
    grad[...] = sum(tn(a[...], b[...]) for a, b in zip(hiddens, cots))
    keep[:384, :] = grad[pl.ds(pl.multiple_of(core * 384, 128), 384), :].astype(bf16)
    send[:384, :] = grad[pl.ds(pl.multiple_of((1 - core) * 384, 128), 384), :].astype(bf16)
    total = jnp.zeros((GROUP_WIDTH, 768), f32)
    for k in range(RING):
        rows = pl.ds(pl.multiple_of(turn(z - k) * 128, 128), 128)
        total = total + tn(context[rows, :], dmids[k][...])[:GROUP_WIDTH]
    grad[:GROUP_WIDTH, :] = total
    keep[384:, :] = grad[pl.ds(pl.multiple_of(core * 96, 32), 96), :].astype(bf16)
    send[384:, :] = grad[pl.ds(pl.multiple_of((1 - core) * 96, 32), 96), :].astype(bf16)
    up = sum(tn(a[...], b[...]) for a, b in zip(seconds, dpres))
    for t in range(RING):
        put_by_distance(ups, z, t, up[GROUP_WIDTH * t : GROUP_WIDTH * (t + 1), :].astype(bf16))


def early_up_kernel(meta, *refs):
    parts, keep, send = refs[:4], refs[4], refs[5]
    core, z = meta[16], meta[17]
    for k in range(RING):
        to = pl.ds(pl.multiple_of(turn(z - k) * 96, 32), 96)
        keep[to, :] = parts[k][pl.ds(pl.multiple_of(core * 96, 32), 96), :]
        send[to, :] = parts[k][pl.ds(pl.multiple_of((1 - core) * 96, 32), 96), :]


def by_x(outs, whole, meta):
    rows = outs[0].shape[0]
    for k in range(RING):
        there = pl.ds(pl.multiple_of(turn(meta[18] + k - RING) * rows, 16), rows)
        outs[k][...] = whole[there, :].astype(bf16)


def from_x(whole, parts, meta):
    rows = parts[0].shape[0]
    for k in range(RING):
        there = pl.ds(pl.multiple_of(turn(meta[18] - k) * rows, 16), rows)
        whole[there, :] = parts[k][...]


def early_sum_kernel(meta, keep, got, up_keep, up_got, *refs):
    whole = refs[4]
    whole[:480, :] = keep[...].astype(f32) + got[...].astype(f32)
    whole[480:864, :] = up_keep[...].astype(f32) + up_got[...].astype(f32)
    whole[864:, :] = jnp.zeros((32, 768), f32)
    by_x(refs[:4], whole, meta)


def early_end_kernel(meta, *refs):
    down, out, up, whole = refs[4:]
    from_x(whole, refs[:4], meta)
    down[...] = whole[:384, :].astype(f32)
    out[...] = whole[384:480, :].astype(f32)
    for t in range(RING):
        up[:, 768 * t : 768 * (t + 1)] = whole[480 + 96 * t : 576 + 96 * t, :].astype(f32)


def collect_kernel(meta, *refs):
    dqs, dkvs = refs[:5], refs[5:9]
    normed, span_tokens, w_qkv, sums, sum_up = refs[9:14]
    dnormeds, lates = refs[14:18], refs[18:22]
    dqkv, grad = refs[22:]
    z = meta[17]
    dq = sum(part[...].astype(f32) for part in dqs)
    dqkv[:, 384:] = (dq.astype(bf16).astype(f32) * 0.125).astype(bf16)
    dqkv[:, :384] = sum(part[...].astype(f32) for part in dkvs).astype(bf16)
    grads = dqkv[...]
    dnormed = nt(grads, w_qkv[...])
    for t in range(RING):
        put_by_distance(dnormeds, z, t, dnormed[128 * t : 128 * (t + 1), :].astype(bf16))
    xhat, _ = center_rows(span_tokens[...].astype(f32))
    gain_grad = jnp.sum(dnormed * xhat, axis=0, keepdims=True)
    shift_grad = jnp.sum(dnormed, axis=0, keepdims=True)
    ones = jnp.ones((8, 512), bf16)
    bias = dense(ones, grads)
    row = lax.broadcasted_iota(jnp.int32, (8, 768), 0)
    vec = sums[...]
    vec = jnp.where(row == 0, gain_grad, jnp.where(row == 1, shift_grad, vec))
    weight = tn(normed[...], grads).astype(bf16)
    for t in range(RING):
        top = pieces([(vec, 3 * t + n) for n in range(3)] + [None])
        mine = z == t
        from_q = pieces([(bias, 6 + n) for n in range(3)] + [None])
        from_v = pieces([(bias, 3 + n) for n in range(3)] + [None])
        row8 = lax.broadcasted_iota(jnp.int32, (8, WIDE), 0)
        top = jnp.where(mine & (row8 == 2), from_q, jnp.where(mine & (row8 == 3), from_v, top))
        lines = jnp.zeros((8, WIDE), f32)
        up = jnp.broadcast_to(sum_up[:, 768 * t : 768 * (t + 1)], (8, 768))
        for q in range(4):
            line = pieces([(up, 3 * q + n) for n in range(3)] + [None])
            lines = jnp.where(row8 == q, line, lines)
        bottom = jnp.concatenate(
            [jnp.concatenate([top, lines], axis=0), jnp.zeros((16, 384), f32)], axis=1
        ).astype(bf16)
        value = jnp.concatenate(
            [weight[GROUP_WIDTH * t : GROUP_WIDTH * (t + 1), :], bottom], axis=0
        )
        put_by_distance(lates, z, t, value)


def end_norm_kernel(meta, n0, n1, n2, n3, tokens, vec, dmiddle, out):
    dnormed = sum(part[...].astype(f32) for part in (n0, n1, n2, n3))
    xhat, scale = center_rows(tokens[...].astype(f32))
    grad = dnormed * vec[0:1, :]
    out[...] = dmiddle[...] + scale * (
        grad
        - jnp.mean(grad, axis=-1, keepdims=True)
        - xhat * jnp.mean(grad * xhat, axis=-1, keepdims=True)
    )


def late_kernel(meta, *refs):
    parts, keep, send = refs[:4], refs[4], refs[5]
    core, z = meta[16], meta[17]
    for k in range(RING):
        to = pl.ds(pl.multiple_of(turn(z - k) * 96, 32), 96)
        keep[to, :] = parts[k][pl.ds(pl.multiple_of(core * 96, 32), 96), :]
        send[to, :] = parts[k][pl.ds(pl.multiple_of((1 - core) * 96, 32), 96), :]
    vec = sum(part[192:, :].astype(f32) for part in parts).astype(bf16)
    keep[384:, :] = vec
    send[384:, :] = vec


def late_sum_kernel(meta, keep, got, *refs):
    whole = refs[4]
    whole[:400, :] = keep[...].astype(f32) + got[...].astype(f32)
    whole[400:, :] = jnp.zeros((48, 640), f32)
    by_x(refs[:4], whole, meta)


def late_end_kernel(meta, *refs):
    key_grad, value_grad, query_grad, vec_out, whole = refs[4:]
    from_x(whole, refs[:4], meta)
    parts = [whole[96 * t : 96 * (t + 1), :].astype(f32) for t in range(RING)]
    for n, out in enumerate((key_grad, value_grad, query_grad)):
        out[...] = pieces([(parts[t], 3 * n + m) for t in range(RING) for m in range(3)])
    vec = whole[384:400, :WIDE].astype(f32)
    row = lax.broadcasted_iota(jnp.int32, (16, WIDE), 0)
    vec_out[...] = jnp.where((meta[16] == 0) | (row >= 8), vec, pltpu.roll(vec, WIDE - 96, 1))


def on_device(
    tokens,
    span_order,
    first_gain,
    first_shift,
    query_weight,
    query_bias,
    key_weight,
    value_weight,
    value_bias,
    out_weight,
    out_bias,
    second_gain,
    second_shift,
    up_weight,
    up_bias,
    down_weight,
    down_bias,
    cotangent,
):
    shard_at = lax.axis_index("shard")
    z, core = shard_at // CORES, shard_at % CORES
    ctx_at = lax.axis_index("ctx")
    y, xq = ctx_at // RING, ctx_at % RING
    rows, width = tokens.shape
    low = ((rows, width), bf16)

    token_parts = spread(tokens, move_z)

    steps = jnp.arange(RING, dtype=jnp.int32)
    groups = jnp.concatenate([((y - steps) % RING) * RING + xq, y * RING + (xq - steps) % RING])
    stored = (2 * groups[:, None] + jnp.arange(2, dtype=jnp.int32)[None, :]).reshape(-1)
    found = stored[:, None] == jnp.arange(span_order.shape[0], dtype=jnp.int32)[None, :]
    spans = jnp.sum(jnp.where(found, span_order[None, :], 0), axis=1)
    meta = jnp.concatenate([spans, jnp.stack([core, z, xq]).astype(jnp.int32)])

    vectors = (
        first_gain,
        first_shift,
        query_bias,
        value_bias,
        out_bias,
        second_gain,
        second_shift,
        down_bias,
        up_bias,
    )
    vec_own = jnp.pad(jnp.concatenate(vectors).reshape(12, 96), ((0, 4), (0, 32)))
    chunks = run(
        arrange_kernel,
        "arrange_weights",
        [((112, 640), bf16)] * 4,
        (meta, key_weight, value_weight, query_weight, vec_own),
    )
    w_parts = deliver(chunks, move_z)
    w_others = [swap_core(part) for part in w_parts]
    span_tokens, normed, queries, kv_own, w_qkv, vec, b_up = run(
        project_kernel,
        "project",
        [
            ((512, width), bf16),
            ((512, width), bf16),
            ((512, WIDE), bf16),
            ((512, 384), bf16),
            ((width, 640), bf16),
            ((16, width), f32),
            ((1, 4 * width), f32),
        ],
        (meta, *token_parts, *w_parts, *w_others),
        scratch=[pltpu.VMEM((8, 16, 128), bf16)],
    )
    w_out = lax.all_gather(out_weight, "shard", axis=0, tiled=True)
    w_up = lax.all_gather(up_weight, "shard", axis=0, tiled=True)
    w_down = lax.all_gather(down_weight, "shard", axis=0, tiled=True)

    kvs = spread(kv_own, move_x)
    q_own = spread(queries, move_y)
    q_oth = [swap_core(part) for part in q_own]
    out_own, out_oth = forward_call(meta, q_own, q_oth, kvs)

    merged = run(
        merge_cores_kernel,
        "merge_cores",
        [((512, WIDE), bf16)] * 4,
        (meta, *out_own, *[swap_core(part) for part in out_oth]),
    )
    context, *context_chunks = run(
        merge_groups_kernel,
        "merge_groups",
        [((512, WIDE), bf16)] + [((128, WIDE), bf16)] * 4,
        (meta, *give_back(merged, move_y)),
    )
    far = pl.BlockSpec(memory_space=pl.ANY)
    middle = run(
        middle_kernel,
        "feed_forward",
        [low, ((rows, width), f32), low, low]
        + [low] * 8
        + [((128, GROUP_WIDTH), bf16)] * 4
        + [((8, width), f32), ((1, 4 * width), f32)],
        (
            meta,
            tokens,
            cotangent,
            *deliver(context_chunks, move_z),
            w_out,
            w_up,
            w_down,
            vec,
            b_up,
        ),
        specs=[SM] + [VM] * 7 + [far, far, VM, VM],
        scratch=[
            pltpu.VMEM((width, 4 * width), bf16),
            pltpu.VMEM((4 * width, width), bf16),
            pltpu.SemaphoreType.DMA,
            pltpu.SemaphoreType.DMA,
        ],
    )
    activations, dmiddle, dmid_low, second_low = middle[:4]
    hiddens, dpres, dcontexts = middle[4:8], middle[8:12], middle[12:16]
    sums, sum_up = middle[16:]

    (packed,) = run(
        pack_kernel,
        "pack_context_gradient",
        [((512, WIDE), bf16)],
        (meta, *deliver(dcontexts, move_z), context),
        scratch=[pltpu.VMEM((512, GROUP_WIDTH), bf16)],
    )
    d_own = spread(packed, move_y)
    d_oth = [swap_core(part) for part in d_own]
    early_parts = [
        *deliver(hiddens, move_z),
        *spread(cotangent, move_z),
        *deliver(dpres, move_z),
        *spread(second_low, move_z),
        *spread(dmid_low, move_z),
    ]
    dkv1, dkv2, dq_half = backward_call(2, False, meta, q_own, q_oth, d_own, d_oth, kvs[1:3])

    dkv1, dkv2, dq_half, early_parts = lax.optimization_barrier(
        (dkv1, dkv2, dq_half, early_parts)
    )
    keep, send, *ups = run(
        early_kernel,
        "early_gradients",
        [((480, width), bf16)] * 2 + [((192, width), bf16)] * 4,
        (meta, *early_parts, context),
        scratch=[pltpu.VMEM((width, width), f32)],
    )
    got = swap_core(send)
    up_parts = deliver(ups, move_z)
    dkv_arrived = [move_x(dkv1, -1), move_x(dkv2, -2)]
    dq_half, keep = lax.optimization_barrier((dq_half, keep))
    last = backward_call(
        6, True, meta, q_own, q_oth, d_own, d_oth, (kvs[3], kvs[0]), dq_half
    )
    dq_own, dq_oth, dkv3, dkv0 = last[:4], last[4:8], last[8], last[9]
    dkv_arrived.append(move_x(dkv3, -3))
    dq_got = [swap_core(part) for part in dq_oth]
    dq_sums = [sum_low([dq_own[k], dq_got[k]]) for k in range(1, RING)]
    dq_arrived = [move_y(dq_sums[k - 1], -k) for k in range(1, RING)]

    dq_own0, up_parts = lax.optimization_barrier((dq_own[0], up_parts))
    up_keep, up_send = run(
        early_up_kernel,
        "early_up",
        [((384, width), bf16)] * 2,
        (meta, *up_parts),
    )
    early_chunks = run(
        early_sum_kernel,
        "early_sum",
        [((224, width), bf16)] * 4,
        (meta, keep, got, up_keep, swap_core(up_send)),
        scratch=[pltpu.VMEM((896, width), f32)],
    )
    early_sums = sum_over_ctx(early_chunks)

    collected = run(
        collect_kernel,
        "collect",
        [low] * 4 + [((208, 640), bf16)] * 4,
        (
            meta,
            dq_own0,
            dq_got[0],
            *dq_arrived,
            dkv0,
            *dkv_arrived,
            normed,
            span_tokens,
            w_qkv,
            sums,
            sum_up,
        ),
        scratch=[pltpu.VMEM((512, 640), bf16), pltpu.VMEM((8, 128), f32)],
    )
    late_parts = deliver(collected[4:], move_z)
    (input_grad,) = run(
        end_norm_kernel,
        "end_norm",
        [((rows, width), f32)],
        (meta, *deliver(collected[:4], move_z), tokens, vec, dmiddle),
    )
    late_keep, late_send = run(
        late_kernel, "late", [((400, 640), bf16)] * 2, (meta, *late_parts)
    )
    late_chunks = run(
        late_sum_kernel,
        "late_sum",
        [((112, 640), bf16)] * 4,
        (meta, late_keep, swap_core(late_send)),
        scratch=[pltpu.VMEM((448, 640), f32)],
    )
    late_sums = sum_over_ctx(late_chunks)
    grad_down, grad_out, grad_up = run(
        early_end_kernel,
        "early_end",
        [((384, width), f32), ((96, width), f32), ((96, 4 * width), f32)],
        (meta, *early_sums),
        scratch=[pltpu.VMEM((896, width), bf16)],
    )
    key_grad, value_grad, query_grad, vec_grad = run(
        late_end_kernel,
        "late_end",
        [((96, width), f32)] * 3 + [((16, WIDE), f32)],
        (meta, *late_sums),
        scratch=[pltpu.VMEM((448, 640), bf16)],
    )
    up_lines = jnp.where(core == 0, vec_grad[8:10], vec_grad[10:12])
    grad_up_bias = up_lines[:, :GROUP_WIDTH].reshape(-1)

    def line(k):
        return vec_grad[k, :96]

    return (
        activations,
        input_grad,
        line(0),
        line(1),
        query_grad,
        line(2),
        key_grad,
        value_grad,
        line(3),
        grad_out,
        line(4),
        line(5),
        line(6),
        grad_up,
        grad_up_bias,
        grad_down,
        line(7),
    )


def solution(mesh):
    tokens_spec = P(("ctx", "shard"), None)
    vector_spec = P("shard")
    matrix_spec = P("shard", None)
    return jax.shard_map(
        on_device,
        mesh=mesh,
        in_specs=(
            tokens_spec,
            P(),
            vector_spec,
            vector_spec,
            matrix_spec,
            vector_spec,
            matrix_spec,
            matrix_spec,
            vector_spec,
            matrix_spec,
            vector_spec,
            vector_spec,
            vector_spec,
            matrix_spec,
            vector_spec,
            matrix_spec,
            vector_spec,
            tokens_spec,
        ),
        out_specs=(
            tokens_spec,
            tokens_spec,
            vector_spec,
            vector_spec,
            matrix_spec,
            vector_spec,
            matrix_spec,
            matrix_spec,
            vector_spec,
            matrix_spec,
            vector_spec,
            vector_spec,
            vector_spec,
            matrix_spec,
            vector_spec,
            matrix_spec,
            vector_spec,
        ),
        check_vma=False,
    )
```

```python
import jax
import jax.numpy as jnp
from jax import lax
from jax.experimental import pallas as pl
from jax.experimental.pallas import tpu as pltpu
from jax.sharding import PartitionSpec as P

HEAD_DIM = 64
RING = 4
CORES = 2
GROUP_HEADS = 3
GROUP_WIDTH = GROUP_HEADS * HEAD_DIM
WIDE = 256
BLOCK = 256

norm_eps = 1e-05
lowest = -1e30
tiny = 1e-30
log2_e = 1.4426950408889634
ln_2 = 0.6931471805599453

bf16 = jnp.bfloat16
f32 = jnp.float32


def dense(left, right):
    return jnp.dot(left, right, preferred_element_type=f32)


def nt(left, right):
    return lax.dot_general(left, right, (((1,), (1,)), ((), ())), preferred_element_type=f32)


def tn(left, right):
    return lax.dot_general(left, right, (((0,), (0,)), ((), ())), preferred_element_type=f32)


def move_z(x, hops):
    size = RING * CORES
    return lax.ppermute(x, "shard", [(r, (r + CORES * hops) % size) for r in range(size)])


def swap_core(x):
    return lax.ppermute(x, "shard", [(r, r ^ 1) for r in range(RING * CORES)])


def move_x(x, hops):
    pairs = [(c, (c // RING) * RING + (c + hops) % RING) for c in range(RING * RING)]
    return lax.ppermute(x, "ctx", pairs)


def move_y(x, hops):
    size = RING * RING
    return lax.ppermute(x, "ctx", [(c, (c + RING * hops) % size) for c in range(size)])


def spread(x, move):
    return [x] + [move(x, k) for k in range(1, RING)]


def deliver(chunks, move):
    return [chunks[0]] + [move(chunks[k], k) for k in range(1, RING)]


def give_back(chunks, move):
    return [chunks[0]] + [move(chunks[k], -k) for k in range(1, RING)]


def sum_low(parts):
    total = parts[0].astype(f32)
    for part in parts[1:]:
        total = total + part.astype(f32)
    return total.astype(bf16)


COLUMN_GROUPS = [[RING * j + i for j in range(RING)] for i in range(RING)]


VM = pl.BlockSpec(memory_space=pltpu.VMEM)
SM = pl.BlockSpec(memory_space=pltpu.SMEM)


def run(kernel, name, outs, args, scratch=(), specs=None, cost=None):
    return pl.pallas_call(
        kernel,
        out_shape=tuple(jax.ShapeDtypeStruct(shape, dtype) for shape, dtype in outs),
        in_specs=specs or [SM] + [VM] * (len(args) - 1),
        out_specs=tuple(VM for _ in outs),
        scratch_shapes=list(scratch),
        cost_estimate=cost,
        compiler_params=pltpu.CompilerParams(vmem_limit_bytes=56 * 2**20),
        name=name,
    )(*args)


def turn(at, size=RING):
    return lax.rem(at + size, size)


def tile(x, k):
    return x[:, 128 * k : 128 * (k + 1)]


def pieces(sources):
    made = []
    rows = next(source for source in sources if source is not None)[0].shape[0]
    for left, right in zip(sources[::2], sources[1::2]):
        sides = []
        for side, source in enumerate((left, right)):
            if source is None:
                sides.append(None)
                continue
            value = tile(source[0], source[1] // 2).astype(f32)
            sides.append(value if source[1] % 2 == side else pltpu.roll(value, 64, 1))
        low, high = (jnp.zeros((rows, 128), f32) if part is None else part for part in sides)
        lane = lax.broadcasted_iota(jnp.int32, (rows, 128), 1)
        made.append(jnp.where(lane < 64, low, high))
    return jnp.concatenate(made, axis=1)


def lanes_of(rows, first, last):
    lane = lax.broadcasted_iota(jnp.int32, (rows, WIDE), 1)
    return jnp.where((lane >= first) & (lane < last), 1.0, 0.0).astype(bf16)


def put_by_distance(refs, place, at, value):
    for k in range(RING):

        @pl.when(turn(at - place) == k)
        def _(k=k):
            refs[k][...] = value


def split3(value):
    high = value.astype(bf16).astype(f32)
    rest = value - high
    mid = rest.astype(bf16).astype(f32)
    return high, mid, rest - mid


def arrange_kernel(meta, tokens, wk, wv, wq, *refs):
    vectors, outs, vec = refs[:9], refs[9:13], refs[13]
    for ref in outs:
        ref[:128, :] = tokens[...]
    vec[...] = jnp.zeros(vec.shape, f32)
    for n in range(8):
        vec[n : n + 1, :96] = vectors[n][...].astype(f32).reshape(1, 96)
    for n in range(3):
        vec[8 + n : 9 + n, :] = vectors[8][128 * n : 128 * (n + 1)].astype(f32).reshape(1, 128)
    lines = jnp.concatenate([vec[...].astype(bf16), jnp.zeros((16, 512), bf16)], axis=1)
    for t in range(RING):
        parts = [(w, 3 * t + n) for w in (wk, wv, wq) for n in range(3)] + [None]
        chunk = pieces(parts).astype(bf16)
        put_by_distance(
            [ref.at[128:, :640] for ref in outs],
            meta[17],
            t,
            jnp.concatenate([chunk, lines], axis=0),
        )


def center_rows(values):
    center = values - jnp.mean(values, axis=-1, keepdims=True)
    spread_ = jnp.mean(center * center, axis=-1, keepdims=True)
    scale = lax.rsqrt(spread_ + norm_eps)
    return center * scale, scale


def project_kernel(meta, *refs):
    parts, others = refs[:4], refs[4:8]
    span_tokens, normed, queries, kv, w_out, vec_out, up_out, vec_in = refs[8:]
    core, z = meta[16], meta[17]
    for k in range(RING):
        place = turn(z - k)
        span_tokens[pl.ds(pl.multiple_of(place * 128, 128), 128), :] = parts[k][:128, :]
        for source, side in ((parts[k], core), (others[k], 1 - core)):
            rank = 2 * place + side
            w_out[pl.ds(pl.multiple_of(rank * 96, 32), 96), :] = source[128:224, :640]
            vec_in[rank] = source[224:240, :128]
    row = lax.broadcasted_iota(jnp.int32, (128, 768), 0)
    col = lax.broadcasted_iota(jnp.int32, (128, 768), 1)
    vec = jnp.zeros((16, 768), f32)
    for rank in range(2 * RING):
        there = jnp.where((row < 96) & (col == row + 96 * rank), 1.0, 0.0).astype(bf16)
        vec = vec + dense(vec_in[rank], there)
    vec_out[...] = vec
    for rank in range(2 * RING):
        for n in range(3):
            at = 384 * rank + 128 * n
            up_out[:, at : at + 128] = vec_in[rank, 8 + n : 9 + n, :].astype(f32)
    xhat, _ = center_rows(span_tokens[...].astype(f32))
    low = (xhat * vec[0:1, :] + vec[1:2, :]).astype(bf16)
    normed[...] = low
    bias = jnp.zeros((8, 640), f32)
    bias_q = jnp.broadcast_to(vec[2:3, :], (8, 768))
    bias_v = jnp.broadcast_to(vec[3:4, :], (8, 768))
    for t in range(RING):
        here = pieces(
            [None] * 3
            + [(bias_v, 3 * t + n) for n in range(3)]
            + [(bias_q, 3 * t + n) for n in range(3)]
            + [None]
        )
        bias = jnp.where(z == t, here, bias)
    projected = dense(low, w_out[...]) + bias[0:1, :]
    kv[...] = projected[:, :384].astype(bf16)
    queries[...] = (projected[:, 384:] * (0.125 * log2_e)).astype(bf16)


def places(parity, rows):
    at = rows % BLOCK
    side = jnp.where(rows < BLOCK, parity, 1 - parity)
    return (at // 128) * 256 + side * 128 + at % 128


def allowed_block(parity):
    key_at = lax.broadcasted_iota(jnp.int32, (2 * BLOCK, BLOCK), 0)
    query_at = lax.broadcasted_iota(jnp.int32, (2 * BLOCK, BLOCK), 1)
    return places(parity, key_at) <= places(parity, query_at)


def forward_kernel(meta, *refs):
    queries, kv_own, kv_oth, outs = (refs[4 * n : 4 * (n + 1)] for n in range(4))
    kv, v_turned, q_turned, best, acc, out = refs[16:]
    parity = meta[16]
    keys = 2 * BLOCK
    row = lax.broadcasted_iota(jnp.int32, (128, BLOCK), 0)
    for j in range(8):
        rows = slice(BLOCK * (j % 2), BLOCK * (j % 2 + 1))
        for side, kvs in enumerate((kv_own, kv_oth)):
            cols = slice(BLOCK * side, BLOCK * (side + 1))
            kv[j, cols, :] = kvs[j // 2][rows, :WIDE]
            turned = kvs[j // 2][rows, 128:].astype(f32).T.astype(bf16)
            for h in range(GROUP_HEADS):
                v_turned[j, 80 * h : 80 * h + 64, cols] = turned[64 * (h + 1) : 64 * (h + 2)]
                v_turned[j, 80 * h + 64 : 80 * h + 80, cols] = jnp.ones((16, BLOCK), bf16)
        query = queries[j // 2][rows, :].astype(f32).T
        q_turned[j, 0] = jnp.where(row < 64, query[:128], 0.0).astype(bf16)
        q_turned[j, 1] = jnp.where(row < 64, 0.0, query[:128]).astype(bf16)
        q_turned[j, 2] = query[128:].astype(bf16)

    def one_span(i, carry):
        best[...] = jnp.full(best.shape, lowest, f32)
        acc[...] = jnp.zeros(acc.shape, f32)

        def visit(j, masked):
            if masked:
                allowed = allowed_block(parity)
            every = [
                dense(kv[j, :, 128 * (h // 2) : 128 * (h // 2 + 1)], q_turned[i, h])
                for h in range(GROUP_HEADS)
            ]
            fades, lows = [], []
            for h in range(GROUP_HEADS):
                scores = every[h]
                if masked:
                    scores = jnp.where(allowed, scores, lowest)
                old = best[h : h + 1, :]
                new = jnp.maximum(old, jnp.max(scores, axis=0, keepdims=True))
                weights = jnp.exp2(scores - new)
                if masked:
                    weights = jnp.where(allowed, weights, 0.0)
                best[h : h + 1, :] = new
                lows.append(weights.astype(bf16))
                fades.append(jnp.exp2(old - new))
            for h in range(GROUP_HEADS):
                here = slice(80 * h, 80 * (h + 1))
                acc[here, :] = acc[here, :] * fades[h] + dense(v_turned[j, here, :], lows[h])

        def one_block(j, carry):
            @pl.when(meta[8 + j] < meta[i])
            def _():
                visit(j, False)

            @pl.when(meta[8 + j] == meta[i])
            def _():
                visit(j, True)

            return carry

        lax.fori_loop(0, 8, one_block, 0)
        row = lax.broadcasted_iota(jnp.int32, (HEAD_DIM, BLOCK), 0)
        parts = []
        extra = jnp.zeros((HEAD_DIM, BLOCK), f32)
        for h in range(GROUP_HEADS):
            count = jnp.maximum(acc[80 * h + 64 : 80 * h + 65, :], tiny)
            parts.append(acc[80 * h : 80 * h + 64, :] / count)
            terms = split3(best[h : h + 1, :] + jnp.log(count) * log2_e)
            for t in range(3):
                extra = jnp.where(row == 3 * h + t, terms[t], extra)
        out[i] = jnp.concatenate(parts + [extra], axis=0).T.astype(bf16)
        return carry

    lax.fori_loop(0, 8, one_span, 0)
    for i in range(8):
        outs[i // 2][BLOCK * (i % 2) : BLOCK * (i % 2 + 1), :] = out[i]


def forward_call(meta, queries, kv_own, kv_oth):
    return run(
        forward_kernel,
        "attention_forward",
        [((2 * BLOCK, WIDE), bf16)] * 4,
        (meta, *queries, *kv_own, *kv_oth),
        scratch=[
            pltpu.VMEM((8, 2 * BLOCK, WIDE), bf16),
            pltpu.VMEM((8, 240, 2 * BLOCK), bf16),
            pltpu.VMEM((8, GROUP_HEADS, 128, BLOCK), bf16),
            pltpu.VMEM((8, BLOCK), f32),
            pltpu.VMEM((240, BLOCK), f32),
            pltpu.VMEM((8, BLOCK, WIDE), bf16),
        ],
        cost=pl.CostEstimate(flops=20 * 10**9, bytes_accessed=10**7, transcendentals=13 * 10**6),
    )


def one_hot(where):
    return jnp.where(where, 1.0, 0.0).astype(bf16)


def merge_rows(parts):
    row = lax.broadcasted_iota(jnp.int32, (WIDE, WIDE), 0)
    col = lax.broadcasted_iota(jnp.int32, (WIDE, WIDE), 1)
    to_lanes = one_hot((row >= 192) & (row < 201) & (col < 192) & ((row - 192) // 3 == col // 64))
    logs = [dense(part, to_lanes) for part in parts]
    best = logs[0]
    for part in logs[1:]:
        best = jnp.maximum(best, part)
    total = jnp.zeros_like(best)
    context = jnp.zeros_like(best)
    for part, log in zip(parts, logs):
        weight = jnp.exp2(log - best)
        total = total + weight
        context = context + weight * part.astype(f32)
    context = context / total
    terms = split3(best + jnp.log(total) * log2_e)
    extra = jnp.zeros_like(best)
    for t in range(3):
        back = one_hot((row < 192) & (row % 64 == 0) & (col == 192 + 3 * (row // 64) + t))
        extra = extra + dense(terms[t].astype(bf16), back)
    lane = lax.broadcasted_iota(jnp.int32, best.shape, 1)
    return jnp.where(lane < 192, context, extra).astype(bf16)


def merge_groups_kernel(meta, *refs):
    whole = refs[4]
    whole[...] = merge_rows([ref[...] for ref in refs[:4]])
    for k in range(RING):
        rows = pl.ds(pl.multiple_of(turn(meta[17] + k - RING) * 128, 128), 128)
        refs[5 + k][...] = whole[rows, :]


def middle_kernel(meta, *refs):
    tokens, cot = refs[:2]
    contexts = refs[2:6]
    w_out, up_far, down_far, vec, b_up = refs[6:11]
    act, dmiddle_out = refs[11:13]
    early, dcontexts = refs[13:17], refs[17:21]
    sums, sum_up, w_up, w_down, up_done, down_done = refs[21:]
    z = meta[17]
    up_copy = pltpu.make_async_copy(up_far, w_up, up_done)
    down_copy = pltpu.make_async_copy(down_far, w_down, down_done)
    up_copy.start()
    down_copy.start()
    middle = tokens[...].astype(f32) + vec[4:5, :]
    for k in range(RING):
        rows = pl.ds(pl.multiple_of(turn(z - k) * GROUP_WIDTH, 64), GROUP_WIDTH)
        middle = middle + dense(contexts[k][:, :GROUP_WIDTH], w_out[rows, :])
    xhat, scale = center_rows(middle)
    gain = vec[5:6, :]
    second = (xhat * gain + vec[6:7, :]).astype(bf16)
    for ref in early:
        ref[256:384, :] = second
    cot_low = cot[...]
    up_copy.wait()
    down_copy.wait()
    total = middle + vec[7:8, :]
    dsecond = jnp.zeros_like(middle)
    width = 768
    for n in range(RING):
        cols = slice(width * n, width * (n + 1))
        pre = dense(second, w_up[:, cols]) + b_up[:, cols]
        square = pre * pre
        inner = jnp.tanh(0.7978845608028654 * (pre + 0.044715 * (square * pre)))
        half = 0.5 * (1.0 + inner)
        hidden = (pre * half).astype(bf16)
        slope = half + (0.5 * 0.7978845608028654) * pre * (1.0 - inner * inner) * (
            1.0 + 3.0 * 0.044715 * square
        )
        total = total + dense(hidden, w_down[cols, :])
        dpre = (nt(cot_low, w_down[cols, :]) * slope).astype(bf16)
        dsecond = dsecond + nt(dpre, w_up[:, cols])
        sum_up[:, cols] = jnp.sum(dpre.astype(f32), axis=0, keepdims=True)
        put_by_distance([ref.at[:128, :] for ref in early], z, n, hidden)
        put_by_distance([ref.at[128:256, :] for ref in early], z, n, dpre)
    act[...] = total.astype(bf16)
    grad = dsecond * gain
    dnorm = scale * (
        grad
        - jnp.mean(grad, axis=-1, keepdims=True)
        - xhat * jnp.mean(grad * xhat, axis=-1, keepdims=True)
    )
    upstream = cot_low.astype(f32)
    dmiddle = upstream + dnorm
    dmiddle_out[...] = dmiddle
    dmid = dmiddle.astype(bf16)
    for ref in early:
        ref[384:512, :] = dmid
    for t in range(RING):
        rows = slice(GROUP_WIDTH * t, GROUP_WIDTH * (t + 1))
        put_by_distance(dcontexts, z, t, nt(dmid, w_out[rows, :]).astype(bf16))
    row = lax.broadcasted_iota(jnp.int32, (8, width), 0)
    lines = (
        dmid.astype(f32),
        dsecond * xhat,
        dsecond,
        upstream,
    )
    gathered = jnp.zeros((8, width), f32)
    for n, line in enumerate(lines):
        gathered = jnp.where(row == 4 + n, jnp.sum(line, axis=0, keepdims=True), gathered)
    sums[...] = gathered


def pack_kernel(meta, d0, d1, d2, d3, context, out, dcontext):
    for k, part in enumerate((d0, d1, d2, d3)):
        dcontext[pl.ds(pl.multiple_of(turn(meta[17] - k) * 128, 128), 128), :] = part[...]
    row = lax.broadcasted_iota(jnp.int32, (GROUP_WIDTH, WIDE), 0)
    col = lax.broadcasted_iota(jnp.int32, (GROUP_WIDTH, WIDE), 1)
    product = dcontext[...].astype(f32) * context[:, :GROUP_WIDTH].astype(f32)
    by_head = one_hot((col < 9) & (row // 64 == col // 3))
    delta = jnp.zeros(out.shape, f32)
    for term in split3(product):
        delta = delta + dense(term.astype(bf16), by_head)
    high, mid, low = split3(delta)
    lane = lax.broadcasted_iota(jnp.int32, out.shape, 1)
    delta_terms = jnp.where(lane % 3 == 0, high, jnp.where(lane % 3 == 1, mid, low))
    row2 = lax.broadcasted_iota(jnp.int32, (WIDE, WIDE), 0)
    col2 = lax.broadcasted_iota(jnp.int32, (WIDE, WIDE), 1)
    log_terms = dense(context[...], one_hot((row2 >= 192) & (row2 < 201) & (col2 == row2 - 183)))
    shifted = dense(dcontext[...], one_hot(col == row + 64))
    out[...] = jnp.where(
        lane < 9, -delta_terms, jnp.where(lane < 18, -log_terms, shifted)
    ).astype(bf16)


def backward_kernel(group, count, first, last, meta, *refs):
    queries, grads = refs[:4], refs[4:8]
    kv_own, kv_oth = refs[8 : 8 + count], refs[8 + count : 8 + 2 * count]
    refs = refs[8 + 2 * count :]
    if not first:
        dq_in, refs = refs[0], refs[1:]
    dkv_own, dkv_oth, refs = refs[:count], refs[count], refs[count + 1 :]
    if last:
        dqs, refs = refs[:4], refs[4:]
    dq_acc, stats, k_turned, q_full, d_full, kv, dkv, dk_acc, dv_acc = refs
    parity = meta[16]
    keys_rows = 2 * BLOCK
    lane = lax.broadcasted_iota(jnp.int32, (BLOCK, 128), 1)
    left = jnp.where(lane < 64, 1.0, 0.0).astype(bf16)
    right = jnp.where(lane < 64, 0.0, 1.0).astype(bf16)
    wide_lane = lax.broadcasted_iota(jnp.int32, (keys_rows, 128), 1)
    for i in range(8):
        there = slice(BLOCK * (i % 2), BLOCK * (i % 2 + 1))
        grad = grads[i // 2][there, :]
        d_full[i] = grad
        q_full[i] = queries[i // 2][there, :]
        lines = grad[:, :128].astype(f32).T
        for n in range(6):
            stats[i, n : n + 1, :] = (
                lines[3 * n : 3 * n + 1] + lines[3 * n + 1 : 3 * n + 2] + lines[3 * n + 2 : 3 * n + 3]
            )
        dq_acc[i] = jnp.zeros(dq_acc.shape[1:], f32) if first else dq_in[i]
    for j in range(2 * count):
        there = slice(BLOCK * (j % 2), BLOCK * (j % 2 + 1))
        kv[j, :BLOCK, :] = kv_own[j // 2][there, :]
        kv[j, BLOCK:, :] = kv_oth[j // 2][there, :]

    def one_key_block(j, carry):
        keys = kv[j, :, :WIDE]
        k_turned[...] = keys.astype(f32).T.astype(bf16)
        dk_acc[...] = jnp.zeros(dk_acc.shape, f32)
        dv_acc[...] = jnp.zeros(dv_acc.shape, f32)
        key_span = meta[8 + 2 * group + j]

        def visit(i, masked):
            if masked:
                allowed = allowed_block(parity)
            query = q_full[i]
            grad = d_full[i]
            first_key, mid_key, last_key = (kv[j, :, 128 * n : 128 * (n + 1)] for n in range(3))
            scores = [
                nt(first_key, query[:, :128] * left),
                nt(first_key, query[:, :128] * right),
                nt(mid_key, query[:, 128:]),
            ]
            dprobs = [
                nt(mid_key, grad[:, :128] * right),
                nt(last_key, grad[:, 128:] * left),
                nt(last_key, grad[:, 128:] * right),
            ]
            all_weights = []
            all_dscores = []
            for h in range(GROUP_HEADS):
                weights = jnp.exp2(scores[h] + stats[i, 3 + h : 4 + h, :])
                if masked:
                    weights = jnp.where(allowed, weights, 0.0)
                all_weights.append(weights.astype(bf16))
                all_dscores.append((weights * (dprobs[h] + stats[i, h : h + 1, :])).astype(bf16))
            d_heads = jnp.concatenate(
                [
                    grad * lanes_of(BLOCK, HEAD_DIM * (h + 1), HEAD_DIM * (h + 2))
                    for h in range(GROUP_HEADS)
                ],
                axis=0,
            )
            q_heads = jnp.concatenate(
                [
                    query * lanes_of(BLOCK, HEAD_DIM * h, HEAD_DIM * (h + 1))
                    for h in range(GROUP_HEADS)
                ],
                axis=0,
            )
            dv_acc[...] = dv_acc[...] + dense(jnp.concatenate(all_weights, axis=1), d_heads)
            dk_acc[...] = dk_acc[...] + dense(jnp.concatenate(all_dscores, axis=1), q_heads)
            for h in range(GROUP_HEADS):
                here = slice(HEAD_DIM * h, HEAD_DIM * (h + 1))
                dq_acc[i, here, :] = dq_acc[i, here, :] + dense(k_turned[here, :], all_dscores[h])

        def one_span(i, carry):
            @pl.when(key_span < meta[i])
            def _():
                visit(i, False)

            @pl.when(key_span == meta[i])
            def _():
                visit(i, True)

            return carry

        lax.fori_loop(0, 8, one_span, 0)
        dk = dk_acc[...] * ln_2
        dv = dv_acc[...]
        dkv[j, :, :128] = dk[:, :128].astype(bf16)
        dkv[j, :, 128:256] = jnp.where(wide_lane < 64, dk[:, 128:], dv[:, :128]).astype(bf16)
        dkv[j, :, 256:] = dv[:, 128:].astype(bf16)
        return carry

    lax.fori_loop(0, 2 * count, one_key_block, 0)
    for j in range(2 * count):
        there = slice(BLOCK * (j % 2), BLOCK * (j % 2 + 1))
        dkv_own[j // 2][there, :] = dkv[j, :BLOCK, :]
        dkv_oth[BLOCK * j : BLOCK * (j + 1), :] = dkv[j, BLOCK:, :]
    if last:
        for i in range(8):
            there = slice(BLOCK * (i % 2), BLOCK * (i % 2 + 1))
            filled = jnp.concatenate(
                [dq_acc[i], jnp.zeros((WIDE - GROUP_WIDTH, BLOCK), f32)], axis=0
            )
            dqs[i // 2][there, :] = filled.T.astype(bf16)


def backward_call(group, meta, queries, grads, kv_own, kv_oth, dq_in=None, last=False):
    count = len(kv_own)
    first = dq_in is None
    kv_outs = [((2 * BLOCK, 2 * GROUP_WIDTH), bf16)] * count
    kv_outs.append(((count * 2 * BLOCK, 2 * GROUP_WIDTH), bf16))
    dq_shape = (8, GROUP_WIDTH, BLOCK)
    if last:
        dq_outs, accs = [((2 * BLOCK, WIDE), bf16)] * 4, [pltpu.VMEM(dq_shape, f32)]
    else:
        dq_outs, accs = [(dq_shape, f32)], []
    outs = run(
        lambda *refs: backward_kernel(group, count, first, last, *refs),
        f"attention_backward_{group}",
        kv_outs + dq_outs,
        (meta, *queries, *grads, *kv_own, *kv_oth) + (() if first else (dq_in,)),
        scratch=accs
        + [
            pltpu.VMEM((8, 8, BLOCK), f32),
            pltpu.VMEM((WIDE, 2 * BLOCK), bf16),
            pltpu.VMEM((8, BLOCK, WIDE), bf16),
            pltpu.VMEM((8, BLOCK, WIDE), bf16),
            pltpu.VMEM((2 * count, 2 * BLOCK, 2 * GROUP_WIDTH), bf16),
            pltpu.VMEM((2 * count, 2 * BLOCK, 2 * GROUP_WIDTH), bf16),
            pltpu.VMEM((2 * BLOCK, WIDE), f32),
            pltpu.VMEM((2 * BLOCK, WIDE), f32),
        ],
        cost=pl.CostEstimate(
            flops=10 * count * 10**9, bytes_accessed=10**7, transcendentals=4 * count * 10**6
        ),
    )
    return outs[:count], outs[count], outs[count + 1 :]


def early_kernel(meta, *refs):
    parts, context, cot_far, out, cots, done = refs[:4], *refs[4:]
    core, z = meta[16], meta[17]
    copies = []
    for k in range(RING):
        there = pl.ds(pl.multiple_of((2 * turn(z - k) + core) * 128, 128), 128)
        copies.append(pltpu.make_async_copy(cot_far.at[there, :], cots.at[k], done.at[k]))
    for copy in copies:
        copy.start()
    up = sum(tn(a[256:384, :], a[128:256, :]) for a in parts)
    out_grad = jnp.zeros((GROUP_WIDTH, 768), f32)
    for k in range(RING):
        rows = pl.ds(pl.multiple_of(turn(z - k) * 128, 128), 128)
        out_grad = out_grad + tn(context[rows, :GROUP_WIDTH], parts[k][384:, :])
    for copy in copies:
        copy.wait()
    down = sum(tn(a[:128, :], cots[k]) for k, a in enumerate(parts))
    for i in range(RING):
        made = []
        for c in range(CORES):
            made.append(down[384 * c + 96 * i : 384 * c + 96 * i + 96])
            made.append(out_grad[96 * c + 24 * i : 96 * c + 24 * i + 24])
        for r in range(RING * CORES):
            made.append(up[96 * r + 24 * i : 96 * r + 24 * i + 24])
        out[432 * i : 432 * (i + 1), :] = jnp.concatenate(made, axis=0).astype(bf16)


def cut_up(outs, whole, place):
    rows = outs[0].shape[0]
    for k in range(RING):
        there = pl.ds(pl.multiple_of(turn(place + k - RING) * rows, 8), rows)
        outs[k][...] = whole[there, :].astype(bf16)


def put_together(whole, parts, place):
    rows = parts[0].shape[0]
    for k in range(RING):
        there = pl.ds(pl.multiple_of(turn(place - k) * rows, 8), rows)
        whole[there, :] = parts[k][...].astype(f32)


def early_end_kernel(meta, total, down, out, up):
    whole = total[...].astype(f32)
    for i in range(RING):
        at = 224 * i
        down[96 * i : 96 * (i + 1), :] = whole[at : at + 96]
        out[24 * i : 24 * (i + 1), :] = whole[at + 96 : at + 120]
        for t in range(RING):
            up[24 * i : 24 * (i + 1), 768 * t : 768 * (t + 1)] = whole[
                at + 120 + 24 * t : at + 144 + 24 * t
            ]


def collect_kernel(meta, *refs):
    dqs, dkvs = refs[:4], refs[4:9]
    normed, span_tokens, w_qkv, sums, sum_up, early = refs[9:15]
    dnormeds, lates = refs[15:19], refs[19:23]
    dqkv = refs[23]
    z = meta[17]
    dq = sum(part[...].astype(f32) for part in dqs)
    dqkv[:, 384:] = (dq.astype(bf16).astype(f32) * 0.125).astype(bf16)
    dqkv[:, :384] = sum(part[...].astype(f32) for part in dkvs).astype(bf16)
    grads = dqkv[...]
    dnormed = nt(grads, w_qkv[...])
    for t in range(RING):
        put_by_distance(dnormeds, z, t, dnormed[128 * t : 128 * (t + 1), :].astype(bf16))
    xhat, _ = center_rows(span_tokens[...].astype(f32))
    gain_grad = jnp.sum(dnormed * xhat, axis=0, keepdims=True)
    shift_grad = jnp.sum(dnormed, axis=0, keepdims=True)
    ones = jnp.ones((8, 512), bf16)
    bias = dense(ones, grads)
    row = lax.broadcasted_iota(jnp.int32, (8, 768), 0)
    vec = sums[...]
    vec = jnp.where(row == 0, gain_grad, jnp.where(row == 1, shift_grad, vec))
    weight = tn(normed[...], grads).astype(bf16)
    for t in range(RING):
        top = pieces([(vec, 3 * t + n) for n in range(3)] + [None])
        mine = z == t
        from_q = pieces([(bias, 6 + n) for n in range(3)] + [None])
        from_v = pieces([(bias, 3 + n) for n in range(3)] + [None])
        row8 = lax.broadcasted_iota(jnp.int32, (8, WIDE), 0)
        top = jnp.where(mine & (row8 == 2), from_q, jnp.where(mine & (row8 == 3), from_v, top))
        lines = jnp.zeros((8, WIDE), f32)
        up = jnp.broadcast_to(sum_up[:, 768 * t : 768 * (t + 1)], (8, 768))
        for q in range(4):
            line = pieces([(up, 3 * q + n) for n in range(3)] + [None])
            lines = jnp.where(row8 == q, line, lines)
        bottom = jnp.concatenate(
            [jnp.concatenate([top, lines], axis=0), jnp.zeros((16, 384), f32)], axis=1
        ).astype(bf16)
        value = jnp.concatenate(
            [weight[GROUP_WIDTH * t : GROUP_WIDTH * (t + 1), :], bottom], axis=0
        )
        put_by_distance([ref.at[:208, :640] for ref in lates], z, t, value)
        put_by_distance(
            [ref.at[208:, :] for ref in lates], z, t, early[240 + 48 * t : 288 + 48 * t, :]
        )


def end_norm_kernel(meta, n0, n1, n2, n3, tokens, vec, dmiddle, out):
    dnormed = sum(part[...].astype(f32) for part in (n0, n1, n2, n3))
    xhat, scale = center_rows(tokens[...].astype(f32))
    grad = dnormed * vec[0:1, :]
    out[...] = dmiddle[...] + scale * (
        grad
        - jnp.mean(grad, axis=-1, keepdims=True)
        - xhat * jnp.mean(grad * xhat, axis=-1, keepdims=True)
    )


def late_kernel(meta, *refs):
    parts, early = refs[:4], refs[4]
    keep, send, wide, ups = refs[5:]
    core, z = meta[16], meta[17]
    vec = sum(part[192:208, :640].astype(f32) for part in parts).astype(bf16)
    wide[...] = early[:240, :].astype(f32)
    for k in range(RING):
        place = turn(z - k)
        ups[pl.ds(pl.multiple_of(place * 48, 16), 48), :] = parts[k][208:, :].astype(f32)
        to = pl.ds(pl.multiple_of(place * 96, 32), 96)
        for ref, side in ((keep, core), (send, 1 - core)):
            ref[to, :] = parts[k][pl.ds(pl.multiple_of(side * 96, 32), 96), :]
    for ref, side in ((keep, core), (send, 1 - core)):
        ref[384:400, :640] = vec
        ref[384:400, 640:] = jnp.zeros((16, 128), bf16)
        made = [wide[pl.ds(pl.multiple_of(side * 120, 8), 120), :]]
        for t in range(RING):
            made.append(ups[pl.ds(pl.multiple_of(48 * t + side * 24, 8), 24), :])
        made.append(jnp.zeros((8, 768), f32))
        ref[400:, :] = jnp.concatenate(made, axis=0).astype(bf16)


def late_sum_kernel(meta, keep, got, *refs):
    early, whole = refs[4], refs[5]
    whole[:400, :] = keep[:400, :640].astype(f32) + got[:400, :640].astype(f32)
    whole[400:, :] = jnp.zeros((48, 640), f32)
    cut_up(refs[:4], whole, meta[19])
    early[...] = (keep[400:, :].astype(f32) + got[400:, :].astype(f32)).astype(bf16)


def late_end_kernel(meta, *refs):
    key_grad, value_grad, query_grad = refs[4:7]
    lines, up_line, whole = refs[7:15], refs[15], refs[16]
    put_together(whole, refs[:4], meta[19])
    parts = [whole[96 * t : 96 * (t + 1), :] for t in range(RING)]
    for n, out in enumerate((key_grad, value_grad, query_grad)):
        out[...] = pieces([(parts[t], 3 * n + m) for t in range(RING) for m in range(3)])
    vec = whole[384:400, :WIDE]
    core = meta[16]
    turned = pltpu.roll(vec, WIDE - 96, 1)
    mine = jnp.where(core == 0, vec, turned)
    for n in range(8):
        lines[n][...] = mine[n, :96]
    first = jnp.where(core == 0, vec[8:9, :], vec[10:11, :])
    second = jnp.where(core == 0, vec[9:10, :], vec[11:12, :])
    spread_line = pieces(
        [(first, 0), (first, 1), (first, 2), (second, 0), (second, 1), (second, 2)]
    )
    up_line[...] = spread_line[0, :]


def on_device(
    tokens,
    span_order,
    first_gain,
    first_shift,
    query_weight,
    query_bias,
    key_weight,
    value_weight,
    value_bias,
    out_weight,
    out_bias,
    second_gain,
    second_shift,
    up_weight,
    up_bias,
    down_weight,
    down_bias,
    cotangent,
):
    shard_at = lax.axis_index("shard")
    z, core = shard_at // CORES, shard_at % CORES
    ctx_at = lax.axis_index("ctx")
    y, xq = ctx_at // RING, ctx_at % RING
    rows, width = tokens.shape
    low = ((rows, width), bf16)

    steps = jnp.arange(RING, dtype=jnp.int32)
    groups = jnp.concatenate([((y - steps) % RING) * RING + xq, y * RING + (xq - steps) % RING])
    stored = (2 * groups[:, None] + jnp.arange(2, dtype=jnp.int32)[None, :]).reshape(-1)
    found = stored[:, None] == jnp.arange(span_order.shape[0], dtype=jnp.int32)[None, :]
    spans = jnp.sum(jnp.where(found, span_order[None, :], 0), axis=1)
    meta = jnp.concatenate([spans, jnp.stack([core, z, xq, y]).astype(jnp.int32)])

    vectors = (
        first_gain,
        first_shift,
        query_bias,
        value_bias,
        out_bias,
        second_gain,
        second_shift,
        down_bias,
        up_bias,
    )
    chunks = run(
        arrange_kernel,
        "arrange_weights",
        [((240, width), bf16)] * 4,
        (meta, tokens, key_weight, value_weight, query_weight, *vectors),
        scratch=[pltpu.VMEM((16, 128), f32)],
    )
    arrived = deliver(chunks, move_z)
    arrived_others = [swap_core(part) for part in arrived]
    span_tokens, normed, queries, kv_own, w_qkv, vec, b_up = run(
        project_kernel,
        "project",
        [
            ((512, width), bf16),
            ((512, width), bf16),
            ((512, WIDE), bf16),
            ((512, 384), bf16),
            ((width, 640), bf16),
            ((16, width), f32),
            ((1, 4 * width), f32),
        ],
        (meta, *arrived, *arrived_others),
        scratch=[pltpu.VMEM((8, 16, 128), bf16)],
    )
    w_out = lax.all_gather(out_weight, "shard", axis=0, tiled=True)
    w_up = lax.all_gather(up_weight, "shard", axis=0, tiled=True)
    w_down = lax.all_gather(down_weight, "shard", axis=0, tiled=True)
    cot_all = lax.all_gather(cotangent, "shard", axis=0, tiled=True)

    kv_parts = spread(kv_own, move_x)
    queries_all = spread(queries, move_y)
    kv_parts, queries_all = lax.optimization_barrier((kv_parts, queries_all))
    kv_others = [swap_core(part) for part in kv_parts]
    partial = forward_call(meta, queries_all, kv_parts, kv_others)

    context, *context_chunks = run(
        merge_groups_kernel,
        "merge_groups",
        [((512, WIDE), bf16)] + [((128, WIDE), bf16)] * 4,
        (meta, *give_back(partial, move_y)),
    )
    far = pl.BlockSpec(memory_space=pl.ANY)
    middle = run(
        middle_kernel,
        "feed_forward",
        [low, ((rows, width), f32)]
        + [((4 * rows, width), bf16)] * 4
        + [((128, GROUP_WIDTH), bf16)] * 4
        + [((8, width), f32), ((1, 4 * width), f32)],
        (
            meta,
            tokens,
            cotangent,
            *deliver(context_chunks, move_z),
            w_out,
            w_up,
            w_down,
            vec,
            b_up,
        ),
        specs=[SM] + [VM] * 7 + [far, far, VM, VM],
        scratch=[
            pltpu.VMEM((width, 4 * width), bf16),
            pltpu.VMEM((4 * width, width), bf16),
            pltpu.SemaphoreType.DMA,
            pltpu.SemaphoreType.DMA,
        ],
    )
    activations, dmiddle = middle[:2]
    early_sent, dcontexts = middle[2:6], middle[6:10]
    sums, sum_up = middle[10:]

    (packed,) = run(
        pack_kernel,
        "pack_context_gradient",
        [((512, WIDE), bf16)],
        (meta, *deliver(dcontexts, move_z), context),
        scratch=[pltpu.VMEM((512, GROUP_WIDTH), bf16)],
    )
    packed, early_sent = lax.optimization_barrier((packed, early_sent))
    grads_all = spread(packed, move_y)
    early_parts = deliver(early_sent, move_z)
    dkv_own, dkv_oth, dq_so_far = backward_call(
        1, meta, queries_all, grads_all, kv_parts[1:], kv_others[1:]
    )

    dkv_oth, dq_so_far, early_parts = lax.optimization_barrier((dkv_oth, dq_so_far, early_parts))
    (early,) = run(
        early_kernel,
        "early_gradients",
        [((1728, width), bf16)],
        (meta, *early_parts, context, cot_all),
        specs=[SM] + [VM] * 5 + [far],
        scratch=[
            pltpu.VMEM((RING, rows, width), bf16),
            pltpu.SemaphoreType.DMA((RING,)),
        ],
    )
    dkv_got = swap_core(dkv_oth)
    dq_so_far, early, dkv_got = lax.optimization_barrier((dq_so_far, early, dkv_got))
    early = lax.psum_scatter(
        early, "ctx", axis_index_groups=COLUMN_GROUPS, scatter_dimension=0, tiled=True
    )
    dkv_sums = [sum_low([dkv_own[k], dkv_got[512 * k : 512 * (k + 1)]]) for k in range(3)]
    dkv_arrived = [move_x(dkv_sums[k], -1 - k) for k in range(3)]
    dkv_own0, dkv_oth0, dqs = backward_call(
        0, meta, queries_all, grads_all, kv_parts[:1], kv_others[:1], *dq_so_far, last=True
    )
    dqs, dkv_oth0, dkv_arrived = lax.optimization_barrier((dqs, dkv_oth0, dkv_arrived))
    dq_arrived = give_back(dqs, move_y)
    dkv_got0 = swap_core(dkv_oth0)

    collected = run(
        collect_kernel,
        "collect",
        [low] * 4 + [((256, width), bf16)] * 4,
        (
            meta,
            *dq_arrived,
            dkv_own0[0],
            dkv_got0,
            *dkv_arrived,
            normed,
            span_tokens,
            w_qkv,
            sums,
            sum_up,
            early,
        ),
        scratch=[pltpu.VMEM((512, 640), bf16)],
    )
    late_parts = deliver(collected[4:], move_z)
    late_parts, dnormed_sent = lax.optimization_barrier((late_parts, collected[:4]))
    dnormed_parts = deliver(dnormed_sent, move_z)
    late_keep, late_send = run(
        late_kernel,
        "late",
        [((624, width), bf16)] * 2,
        (meta, *late_parts, early),
        scratch=[pltpu.VMEM((240, width), f32), pltpu.VMEM((192, width), f32)],
    )
    *late_chunks, early = run(
        late_sum_kernel,
        "late_sum",
        [((112, 640), bf16)] * 4 + [((224, width), bf16)],
        (meta, late_keep, swap_core(late_send)),
        scratch=[pltpu.VMEM((448, 640), f32)],
    )
    late_arrived = deliver(late_chunks, move_y)
    early_parts = spread(early, move_x)
    late_arrived, early_parts, dnormed_parts = lax.optimization_barrier(
        (late_arrived, early_parts, dnormed_parts)
    )
    early_total = lax.all_gather(
        sum_low(early_parts), "ctx", axis_index_groups=COLUMN_GROUPS, axis=0, tiled=True
    )
    late_parts = spread(sum_low(late_arrived), move_x)
    (input_grad,) = run(
        end_norm_kernel,
        "end_norm",
        [((rows, width), f32)],
        (meta, *dnormed_parts, tokens, vec, dmiddle),
    )
    late_sums = spread(sum_low(late_parts), move_y)
    grad_down, grad_out, grad_up = run(
        early_end_kernel,
        "early_end",
        [((384, width), f32), ((96, width), f32), ((96, 4 * width), f32)],
        (meta, early_total),
    )
    key_grad, value_grad, query_grad, *vec_grads = run(
        late_end_kernel,
        "late_end",
        [((96, width), f32)] * 3 + [((96,), f32)] * 8 + [((384,), f32)],
        (meta, *late_sums),
        scratch=[pltpu.VMEM((448, 640), f32)],
    )
    return (
        activations,
        input_grad,
        vec_grads[0],
        vec_grads[1],
        query_grad,
        vec_grads[2],
        key_grad,
        value_grad,
        vec_grads[3],
        grad_out,
        vec_grads[4],
        vec_grads[5],
        vec_grads[6],
        grad_up,
        vec_grads[8],
        grad_down,
        vec_grads[7],
    )


def solution(mesh):
    tokens_spec = P(("ctx", "shard"), None)
    vector_spec = P("shard")
    matrix_spec = P("shard", None)
    return jax.shard_map(
        on_device,
        mesh=mesh,
        in_specs=(
            tokens_spec,
            P(),
            vector_spec,
            vector_spec,
            matrix_spec,
            vector_spec,
            matrix_spec,
            matrix_spec,
            vector_spec,
            matrix_spec,
            vector_spec,
            vector_spec,
            vector_spec,
            matrix_spec,
            vector_spec,
            matrix_spec,
            vector_spec,
            tokens_spec,
        ),
        out_specs=(
            tokens_spec,
            tokens_spec,
            vector_spec,
            vector_spec,
            matrix_spec,
            vector_spec,
            matrix_spec,
            matrix_spec,
            vector_spec,
            matrix_spec,
            vector_spec,
            vector_spec,
            vector_spec,
            matrix_spec,
            vector_spec,
            matrix_spec,
            vector_spec,
        ),
        check_vma=False,
    )
```

```python
import jax
import jax.numpy as jnp
from jax import lax
from jax.experimental import pallas as pl
from jax.experimental.pallas import tpu as pltpu
from jax.sharding import PartitionSpec as P

HEAD_DIM = 64
RING = 4
CORES = 2
GROUP_HEADS = 3
GROUP_WIDTH = GROUP_HEADS * HEAD_DIM
WIDE = 256
BLOCK = 256

norm_eps = 1e-05
lowest = -1e30
tiny = 1e-30
log2_e = 1.4426950408889634
ln_2 = 0.6931471805599453

bf16 = jnp.bfloat16
f32 = jnp.float32


def dense(left, right):
    return jnp.dot(left, right, preferred_element_type=f32)


def nt(left, right):
    return lax.dot_general(left, right, (((1,), (1,)), ((), ())), preferred_element_type=f32)


def tn(left, right):
    return lax.dot_general(left, right, (((0,), (0,)), ((), ())), preferred_element_type=f32)


def move_z(x, hops):
    size = RING * CORES
    return lax.ppermute(x, "shard", [(r, (r + CORES * hops) % size) for r in range(size)])


def swap_core(x):
    return lax.ppermute(x, "shard", [(r, r ^ 1) for r in range(RING * CORES)])


def move_x(x, hops):
    pairs = [(c, (c // RING) * RING + (c + hops) % RING) for c in range(RING * RING)]
    return lax.ppermute(x, "ctx", pairs)


def move_y(x, hops):
    size = RING * RING
    return lax.ppermute(x, "ctx", [(c, (c + RING * hops) % size) for c in range(size)])


def spread(x, move):
    return [x] + [move(x, k) for k in range(1, RING)]


def deliver(chunks, move):
    return [chunks[0]] + [move(chunks[k], k) for k in range(1, RING)]


def give_back(chunks, move):
    return [chunks[0]] + [move(chunks[k], -k) for k in range(1, RING)]


def sum_low(parts):
    total = parts[0].astype(f32)
    for part in parts[1:]:
        total = total + part.astype(f32)
    return total.astype(bf16)


COLUMN_GROUPS = [[RING * j + i for j in range(RING)] for i in range(RING)]


VM = pl.BlockSpec(memory_space=pltpu.VMEM)
SM = pl.BlockSpec(memory_space=pltpu.SMEM)


def run(kernel, name, outs, args, scratch=(), specs=None, cost=None):
    return pl.pallas_call(
        kernel,
        out_shape=tuple(jax.ShapeDtypeStruct(shape, dtype) for shape, dtype in outs),
        in_specs=specs or [SM] + [VM] * (len(args) - 1),
        out_specs=tuple(VM for _ in outs),
        scratch_shapes=list(scratch),
        cost_estimate=cost,
        compiler_params=pltpu.CompilerParams(vmem_limit_bytes=56 * 2**20),
        name=name,
    )(*args)


def turn(at, size=RING):
    return lax.rem(at + size, size)


def tile(x, k):
    return x[:, 128 * k : 128 * (k + 1)]


def pieces(sources):
    made = []
    rows = next(source for source in sources if source is not None)[0].shape[0]
    for left, right in zip(sources[::2], sources[1::2]):
        sides = []
        for side, source in enumerate((left, right)):
            if source is None:
                sides.append(None)
                continue
            value = tile(source[0], source[1] // 2).astype(f32)
            sides.append(value if source[1] % 2 == side else pltpu.roll(value, 64, 1))
        low, high = (jnp.zeros((rows, 128), f32) if part is None else part for part in sides)
        lane = lax.broadcasted_iota(jnp.int32, (rows, 128), 1)
        made.append(jnp.where(lane < 64, low, high))
    return jnp.concatenate(made, axis=1)


def lanes_of(rows, first, last):
    lane = lax.broadcasted_iota(jnp.int32, (rows, WIDE), 1)
    return jnp.where((lane >= first) & (lane < last), 1.0, 0.0).astype(bf16)


def put_by_distance(refs, place, at, value):
    for k in range(RING):

        @pl.when(turn(at - place) == k)
        def _(k=k):
            refs[k][...] = value


def split3(value):
    high = value.astype(bf16).astype(f32)
    rest = value - high
    mid = rest.astype(bf16).astype(f32)
    return high, mid, rest - mid


def arrange_kernel(meta, tokens, wk, wv, wq, *refs):
    vectors, outs, vec = refs[:9], refs[9:13], refs[13]
    for ref in outs:
        ref[:128, :] = tokens[...]
    vec[...] = jnp.zeros(vec.shape, f32)
    for n in range(8):
        vec[n : n + 1, :96] = vectors[n][...].astype(f32).reshape(1, 96)
    for n in range(3):
        vec[8 + n : 9 + n, :] = vectors[8][128 * n : 128 * (n + 1)].astype(f32).reshape(1, 128)
    lines = jnp.concatenate([vec[...].astype(bf16), jnp.zeros((16, 512), bf16)], axis=1)
    for t in range(RING):
        parts = [(w, 3 * t + n) for w in (wk, wv, wq) for n in range(3)] + [None]
        chunk = pieces(parts).astype(bf16)
        put_by_distance(
            [ref.at[128:, :640] for ref in outs],
            meta[17],
            t,
            jnp.concatenate([chunk, lines], axis=0),
        )


def center_rows(values):
    center = values - jnp.mean(values, axis=-1, keepdims=True)
    spread_ = jnp.mean(center * center, axis=-1, keepdims=True)
    scale = lax.rsqrt(spread_ + norm_eps)
    return center * scale, scale


def project_kernel(meta, *refs):
    parts, others = refs[:4], refs[4:8]
    span_tokens, normed, queries, kv, w_out, vec_out, up_out, vec_in = refs[8:]
    core, z = meta[16], meta[17]
    for k in range(RING):
        place = turn(z - k)
        span_tokens[pl.ds(pl.multiple_of(place * 128, 128), 128), :] = parts[k][:128, :]
        for source, side in ((parts[k], core), (others[k], 1 - core)):
            rank = 2 * place + side
            w_out[pl.ds(pl.multiple_of(rank * 96, 32), 96), :] = source[128:224, :640]
            vec_in[rank] = source[224:240, :128]
    row = lax.broadcasted_iota(jnp.int32, (128, 768), 0)
    col = lax.broadcasted_iota(jnp.int32, (128, 768), 1)
    vec = jnp.zeros((16, 768), f32)
    for rank in range(2 * RING):
        there = jnp.where((row < 96) & (col == row + 96 * rank), 1.0, 0.0).astype(bf16)
        vec = vec + dense(vec_in[rank], there)
    vec_out[...] = vec
    for rank in range(2 * RING):
        for n in range(3):
            at = 384 * rank + 128 * n
            up_out[:, at : at + 128] = vec_in[rank, 8 + n : 9 + n, :].astype(f32)
    xhat, _ = center_rows(span_tokens[...].astype(f32))
    low = (xhat * vec[0:1, :] + vec[1:2, :]).astype(bf16)
    normed[...] = low
    bias = jnp.zeros((8, 640), f32)
    bias_q = jnp.broadcast_to(vec[2:3, :], (8, 768))
    bias_v = jnp.broadcast_to(vec[3:4, :], (8, 768))
    for t in range(RING):
        here = pieces(
            [None] * 3
            + [(bias_v, 3 * t + n) for n in range(3)]
            + [(bias_q, 3 * t + n) for n in range(3)]
            + [None]
        )
        bias = jnp.where(z == t, here, bias)
    projected = dense(low, w_out[...]) + bias[0:1, :]
    kv[...] = projected[:, :384].astype(bf16)
    queries[...] = (projected[:, 384:] * (0.125 * log2_e)).astype(bf16)


def places(parity, rows):
    at = rows % BLOCK
    side = jnp.where(rows < BLOCK, parity, 1 - parity)
    return (at // 128) * 256 + side * 128 + at % 128


def allowed_block(parity):
    key_at = lax.broadcasted_iota(jnp.int32, (2 * BLOCK, BLOCK), 0)
    query_at = lax.broadcasted_iota(jnp.int32, (2 * BLOCK, BLOCK), 1)
    return places(parity, key_at) <= places(parity, query_at)


def forward_kernel(meta, *refs):
    queries, kv_own, kv_oth, outs = (refs[4 * n : 4 * (n + 1)] for n in range(4))
    kv, v_turned, q_turned, best, acc, out = refs[16:]
    parity = meta[16]
    keys = 2 * BLOCK
    row = lax.broadcasted_iota(jnp.int32, (128, BLOCK), 0)
    for j in range(8):
        rows = slice(BLOCK * (j % 2), BLOCK * (j % 2 + 1))
        for side, kvs in enumerate((kv_own, kv_oth)):
            cols = slice(BLOCK * side, BLOCK * (side + 1))
            kv[j, cols, :] = kvs[j // 2][rows, :WIDE]
            turned = kvs[j // 2][rows, 128:].astype(f32).T.astype(bf16)
            for h in range(GROUP_HEADS):
                v_turned[j, 80 * h : 80 * h + 64, cols] = turned[64 * (h + 1) : 64 * (h + 2)]
                v_turned[j, 80 * h + 64 : 80 * h + 80, cols] = jnp.ones((16, BLOCK), bf16)
        query = queries[j // 2][rows, :].astype(f32).T
        q_turned[j, 0] = jnp.where(row < 64, query[:128], 0.0).astype(bf16)
        q_turned[j, 1] = jnp.where(row < 64, 0.0, query[:128]).astype(bf16)
        q_turned[j, 2] = query[128:].astype(bf16)

    def one_span(i, carry):
        best[...] = jnp.full(best.shape, lowest, f32)
        acc[...] = jnp.zeros(acc.shape, f32)

        def visit(j, masked):
            if masked:
                allowed = allowed_block(parity)
            every = [
                dense(kv[j, :, 128 * (h // 2) : 128 * (h // 2 + 1)], q_turned[i, h])
                for h in range(GROUP_HEADS)
            ]
            fades, lows = [], []
            for h in range(GROUP_HEADS):
                scores = every[h]
                if masked:
                    scores = jnp.where(allowed, scores, lowest)
                old = best[h : h + 1, :]
                new = jnp.maximum(old, jnp.max(scores, axis=0, keepdims=True))
                weights = jnp.exp2(scores - new)
                if masked:
                    weights = jnp.where(allowed, weights, 0.0)
                best[h : h + 1, :] = new
                lows.append(weights.astype(bf16))
                fades.append(jnp.exp2(old - new))
            for h in range(GROUP_HEADS):
                here = slice(80 * h, 80 * (h + 1))
                acc[here, :] = acc[here, :] * fades[h] + dense(v_turned[j, here, :], lows[h])

        def one_block(j, carry):
            @pl.when(meta[8 + j] < meta[i])
            def _():
                visit(j, False)

            @pl.when(meta[8 + j] == meta[i])
            def _():
                visit(j, True)

            return carry

        lax.fori_loop(0, 8, one_block, 0)
        row = lax.broadcasted_iota(jnp.int32, (HEAD_DIM, BLOCK), 0)
        parts = []
        extra = jnp.zeros((HEAD_DIM, BLOCK), f32)
        for h in range(GROUP_HEADS):
            count = jnp.maximum(acc[80 * h + 64 : 80 * h + 65, :], tiny)
            parts.append(acc[80 * h : 80 * h + 64, :] / count)
            terms = split3(best[h : h + 1, :] + jnp.log(count) * log2_e)
            for t in range(3):
                extra = jnp.where(row == 3 * h + t, terms[t], extra)
        out[i] = jnp.concatenate(parts + [extra], axis=0).T.astype(bf16)
        return carry

    lax.fori_loop(0, 8, one_span, 0)
    for i in range(8):
        outs[i // 2][BLOCK * (i % 2) : BLOCK * (i % 2 + 1), :] = out[i]


def forward_call(meta, queries, kv_own, kv_oth):
    return run(
        forward_kernel,
        "attention_forward",
        [((2 * BLOCK, WIDE), bf16)] * 4,
        (meta, *queries, *kv_own, *kv_oth),
        scratch=[
            pltpu.VMEM((8, 2 * BLOCK, WIDE), bf16),
            pltpu.VMEM((8, 240, 2 * BLOCK), bf16),
            pltpu.VMEM((8, GROUP_HEADS, 128, BLOCK), bf16),
            pltpu.VMEM((8, BLOCK), f32),
            pltpu.VMEM((240, BLOCK), f32),
            pltpu.VMEM((8, BLOCK, WIDE), bf16),
        ],
        cost=pl.CostEstimate(flops=20 * 10**9, bytes_accessed=10**7, transcendentals=13 * 10**6),
    )


def one_hot(where):
    return jnp.where(where, 1.0, 0.0).astype(bf16)


def merge_rows(parts):
    row = lax.broadcasted_iota(jnp.int32, (WIDE, WIDE), 0)
    col = lax.broadcasted_iota(jnp.int32, (WIDE, WIDE), 1)
    to_lanes = one_hot((row >= 192) & (row < 201) & (col < 192) & ((row - 192) // 3 == col // 64))
    logs = [dense(part, to_lanes) for part in parts]
    best = logs[0]
    for part in logs[1:]:
        best = jnp.maximum(best, part)
    total = jnp.zeros_like(best)
    context = jnp.zeros_like(best)
    for part, log in zip(parts, logs):
        weight = jnp.exp2(log - best)
        total = total + weight
        context = context + weight * part.astype(f32)
    context = context / total
    terms = split3(best + jnp.log(total) * log2_e)
    extra = jnp.zeros_like(best)
    for t in range(3):
        back = one_hot((row < 192) & (row % 64 == 0) & (col == 192 + 3 * (row // 64) + t))
        extra = extra + dense(terms[t].astype(bf16), back)
    lane = lax.broadcasted_iota(jnp.int32, best.shape, 1)
    return jnp.where(lane < 192, context, extra).astype(bf16)


def merge_groups_kernel(meta, *refs):
    whole = refs[4]
    whole[...] = merge_rows([ref[...] for ref in refs[:4]])
    for k in range(RING):
        rows = pl.ds(pl.multiple_of(turn(meta[17] + k - RING) * 128, 128), 128)
        refs[5 + k][...] = whole[rows, :]


def middle_kernel(meta, *refs):
    tokens, cot = refs[:2]
    contexts = refs[2:6]
    out_down_far, up_far, vec, b_up = refs[6:10]
    act, dmiddle_out = refs[10:12]
    early, dcontexts = refs[12:16], refs[16:20]
    sums, sum_up, w_out, w_up, w_down, up_done, done = refs[20:]
    z = meta[17]
    up_copy = pltpu.make_async_copy(up_far, w_up, up_done)
    out_copies, down_copies = [], []
    for r in range(2 * RING):
        at = 480 * r
        out_copies.append(
            pltpu.make_async_copy(
                out_down_far.at[at : at + 96, :], w_out.at[96 * r : 96 * (r + 1), :], done.at[r, 0]
            )
        )
        down_copies.append(
            pltpu.make_async_copy(
                out_down_far.at[at + 96 : at + 480, :],
                w_down.at[384 * r : 384 * (r + 1), :],
                done.at[r, 1],
            )
        )
    for copy in out_copies:
        copy.start()
    up_copy.start()
    for copy in down_copies:
        copy.start()
    for copy in out_copies:
        copy.wait()
    middle = tokens[...].astype(f32) + vec[4:5, :]
    for k in range(RING):
        rows = pl.ds(pl.multiple_of(turn(z - k) * GROUP_WIDTH, 64), GROUP_WIDTH)
        middle = middle + dense(contexts[k][:, :GROUP_WIDTH], w_out[rows, :])
    xhat, scale = center_rows(middle)
    gain = vec[5:6, :]
    second = (xhat * gain + vec[6:7, :]).astype(bf16)
    for ref in early:
        ref[256:384, :] = second
    cot_low = cot[...]
    up_copy.wait()
    for copy in down_copies:
        copy.wait()
    total = middle + vec[7:8, :]
    dsecond = jnp.zeros_like(middle)
    width = 768
    for n in range(RING):
        cols = slice(width * n, width * (n + 1))
        pre = dense(second, w_up[:, cols]) + b_up[:, cols]
        square = pre * pre
        inner = jnp.tanh(0.7978845608028654 * (pre + 0.044715 * (square * pre)))
        half = 0.5 * (1.0 + inner)
        hidden = (pre * half).astype(bf16)
        slope = half + (0.5 * 0.7978845608028654) * pre * (1.0 - inner * inner) * (
            1.0 + 3.0 * 0.044715 * square
        )
        total = total + dense(hidden, w_down[cols, :])
        dpre = (nt(cot_low, w_down[cols, :]) * slope).astype(bf16)
        dsecond = dsecond + nt(dpre, w_up[:, cols])
        sum_up[:, cols] = jnp.sum(dpre.astype(f32), axis=0, keepdims=True)
        put_by_distance([ref.at[:128, :] for ref in early], z, n, hidden)
        put_by_distance([ref.at[128:256, :] for ref in early], z, n, dpre)
    act[...] = total.astype(bf16)
    grad = dsecond * gain
    dnorm = scale * (
        grad
        - jnp.mean(grad, axis=-1, keepdims=True)
        - xhat * jnp.mean(grad * xhat, axis=-1, keepdims=True)
    )
    upstream = cot_low.astype(f32)
    dmiddle = upstream + dnorm
    dmiddle_out[...] = dmiddle
    dmid = dmiddle.astype(bf16)
    for ref in early:
        ref[384:512, :] = dmid
    for t in range(RING):
        rows = slice(GROUP_WIDTH * t, GROUP_WIDTH * (t + 1))
        put_by_distance(dcontexts, z, t, nt(dmid, w_out[rows, :]).astype(bf16))
    row = lax.broadcasted_iota(jnp.int32, (8, width), 0)
    lines = (
        dmid.astype(f32),
        dsecond * xhat,
        dsecond,
        upstream,
    )
    gathered = jnp.zeros((8, width), f32)
    for n, line in enumerate(lines):
        gathered = jnp.where(row == 4 + n, jnp.sum(line, axis=0, keepdims=True), gathered)
    sums[...] = gathered


def pack_kernel(meta, d0, d1, d2, d3, context, out, dcontext):
    for k, part in enumerate((d0, d1, d2, d3)):
        dcontext[pl.ds(pl.multiple_of(turn(meta[17] - k) * 128, 128), 128), :] = part[...]
    row = lax.broadcasted_iota(jnp.int32, (GROUP_WIDTH, WIDE), 0)
    col = lax.broadcasted_iota(jnp.int32, (GROUP_WIDTH, WIDE), 1)
    product = dcontext[...].astype(f32) * context[:, :GROUP_WIDTH].astype(f32)
    by_head = one_hot((col < 9) & (row // 64 == col // 3))
    delta = jnp.zeros(out.shape, f32)
    for term in split3(product):
        delta = delta + dense(term.astype(bf16), by_head)
    high, mid, low = split3(delta)
    lane = lax.broadcasted_iota(jnp.int32, out.shape, 1)
    delta_terms = jnp.where(lane % 3 == 0, high, jnp.where(lane % 3 == 1, mid, low))
    row2 = lax.broadcasted_iota(jnp.int32, (WIDE, WIDE), 0)
    col2 = lax.broadcasted_iota(jnp.int32, (WIDE, WIDE), 1)
    log_terms = dense(context[...], one_hot((row2 >= 192) & (row2 < 201) & (col2 == row2 - 183)))
    shifted = dense(dcontext[...], one_hot(col == row + 64))
    out[...] = jnp.where(
        lane < 9, -delta_terms, jnp.where(lane < 18, -log_terms, shifted)
    ).astype(bf16)


def backward_kernel(group, count, first, last, meta, *refs):
    queries, grads = refs[:4], refs[4:8]
    kv_own, kv_oth = refs[8 : 8 + count], refs[8 + count : 8 + 2 * count]
    refs = refs[8 + 2 * count :]
    if not first:
        dq_in, refs = refs[0], refs[1:]
    dkv_own, dkv_oth, refs = refs[:count], refs[count], refs[count + 1 :]
    if last:
        dqs, refs = refs[:4], refs[4:]
    dq_acc, stats, k_turned, q_full, d_full, kv, dkv, dk_acc, dv_acc = refs
    parity = meta[16]
    keys_rows = 2 * BLOCK
    lane = lax.broadcasted_iota(jnp.int32, (BLOCK, 128), 1)
    left = jnp.where(lane < 64, 1.0, 0.0).astype(bf16)
    right = jnp.where(lane < 64, 0.0, 1.0).astype(bf16)
    wide_lane = lax.broadcasted_iota(jnp.int32, (keys_rows, 128), 1)
    for i in range(8):
        there = slice(BLOCK * (i % 2), BLOCK * (i % 2 + 1))
        grad = grads[i // 2][there, :]
        d_full[i] = grad
        q_full[i] = queries[i // 2][there, :]
        lines = grad[:, :128].astype(f32).T
        for n in range(6):
            stats[i, n : n + 1, :] = (
                lines[3 * n : 3 * n + 1] + lines[3 * n + 1 : 3 * n + 2] + lines[3 * n + 2 : 3 * n + 3]
            )
        dq_acc[i] = jnp.zeros(dq_acc.shape[1:], f32) if first else dq_in[i]
    for j in range(2 * count):
        there = slice(BLOCK * (j % 2), BLOCK * (j % 2 + 1))
        kv[j, :BLOCK, :] = kv_own[j // 2][there, :]
        kv[j, BLOCK:, :] = kv_oth[j // 2][there, :]

    def one_key_block(j, carry):
        keys = kv[j, :, :WIDE]
        k_turned[...] = keys.astype(f32).T.astype(bf16)
        dk_acc[...] = jnp.zeros(dk_acc.shape, f32)
        dv_acc[...] = jnp.zeros(dv_acc.shape, f32)
        key_span = meta[8 + 2 * group + j]

        def visit(i, masked):
            if masked:
                allowed = allowed_block(parity)
            query = q_full[i]
            grad = d_full[i]
            first_key, mid_key, last_key = (kv[j, :, 128 * n : 128 * (n + 1)] for n in range(3))
            scores = [
                nt(first_key, query[:, :128] * left),
                nt(first_key, query[:, :128] * right),
                nt(mid_key, query[:, 128:]),
            ]
            dprobs = [
                nt(mid_key, grad[:, :128] * right),
                nt(last_key, grad[:, 128:] * left),
                nt(last_key, grad[:, 128:] * right),
            ]
            all_weights = []
            all_dscores = []
            for h in range(GROUP_HEADS):
                weights = jnp.exp2(scores[h] + stats[i, 3 + h : 4 + h, :])
                if masked:
                    weights = jnp.where(allowed, weights, 0.0)
                all_weights.append(weights.astype(bf16))
                all_dscores.append((weights * (dprobs[h] + stats[i, h : h + 1, :])).astype(bf16))
            d_heads = jnp.concatenate(
                [
                    grad * lanes_of(BLOCK, HEAD_DIM * (h + 1), HEAD_DIM * (h + 2))
                    for h in range(GROUP_HEADS)
                ],
                axis=0,
            )
            q_heads = jnp.concatenate(
                [
                    query * lanes_of(BLOCK, HEAD_DIM * h, HEAD_DIM * (h + 1))
                    for h in range(GROUP_HEADS)
                ],
                axis=0,
            )
            dv_acc[...] = dv_acc[...] + dense(jnp.concatenate(all_weights, axis=1), d_heads)
            dk_acc[...] = dk_acc[...] + dense(jnp.concatenate(all_dscores, axis=1), q_heads)
            for h in range(GROUP_HEADS):
                here = slice(HEAD_DIM * h, HEAD_DIM * (h + 1))
                dq_acc[i, here, :] = dq_acc[i, here, :] + dense(k_turned[here, :], all_dscores[h])

        def one_span(i, carry):
            @pl.when(key_span < meta[i])
            def _():
                visit(i, False)

            @pl.when(key_span == meta[i])
            def _():
                visit(i, True)

            return carry

        lax.fori_loop(0, 8, one_span, 0)
        dk = dk_acc[...] * ln_2
        dv = dv_acc[...]
        dkv[j, :, :128] = dk[:, :128].astype(bf16)
        dkv[j, :, 128:256] = jnp.where(wide_lane < 64, dk[:, 128:], dv[:, :128]).astype(bf16)
        dkv[j, :, 256:] = dv[:, 128:].astype(bf16)
        return carry

    lax.fori_loop(0, 2 * count, one_key_block, 0)
    for j in range(2 * count):
        there = slice(BLOCK * (j % 2), BLOCK * (j % 2 + 1))
        dkv_own[j // 2][there, :] = dkv[j, :BLOCK, :]
        dkv_oth[BLOCK * j : BLOCK * (j + 1), :] = dkv[j, BLOCK:, :]
    if last:
        for i in range(8):
            there = slice(BLOCK * (i % 2), BLOCK * (i % 2 + 1))
            filled = jnp.concatenate(
                [dq_acc[i], jnp.zeros((WIDE - GROUP_WIDTH, BLOCK), f32)], axis=0
            )
            dqs[i // 2][there, :] = filled.T.astype(bf16)


def backward_call(group, meta, queries, grads, kv_own, kv_oth, dq_in=None, last=False):
    count = len(kv_own)
    first = dq_in is None
    kv_outs = [((2 * BLOCK, 2 * GROUP_WIDTH), bf16)] * count
    kv_outs.append(((count * 2 * BLOCK, 2 * GROUP_WIDTH), bf16))
    dq_shape = (8, GROUP_WIDTH, BLOCK)
    if last:
        dq_outs, accs = [((2 * BLOCK, WIDE), bf16)] * 4, [pltpu.VMEM(dq_shape, f32)]
    else:
        dq_outs, accs = [(dq_shape, f32)], []
    outs = run(
        lambda *refs: backward_kernel(group, count, first, last, *refs),
        f"attention_backward_{group}",
        kv_outs + dq_outs,
        (meta, *queries, *grads, *kv_own, *kv_oth) + (() if first else (dq_in,)),
        scratch=accs
        + [
            pltpu.VMEM((8, 8, BLOCK), f32),
            pltpu.VMEM((WIDE, 2 * BLOCK), bf16),
            pltpu.VMEM((8, BLOCK, WIDE), bf16),
            pltpu.VMEM((8, BLOCK, WIDE), bf16),
            pltpu.VMEM((2 * count, 2 * BLOCK, 2 * GROUP_WIDTH), bf16),
            pltpu.VMEM((2 * count, 2 * BLOCK, 2 * GROUP_WIDTH), bf16),
            pltpu.VMEM((2 * BLOCK, WIDE), f32),
            pltpu.VMEM((2 * BLOCK, WIDE), f32),
        ],
        cost=pl.CostEstimate(
            flops=10 * count * 10**9, bytes_accessed=10**7, transcendentals=4 * count * 10**6
        ),
    )
    return outs[:count], outs[count], outs[count + 1 :]


def early_kernel(meta, *refs):
    parts, context, cot_far, out, cots, done = refs[:4], *refs[4:]
    core, z = meta[16], meta[17]
    copies = []
    for k in range(RING):
        there = pl.ds(pl.multiple_of((2 * turn(z - k) + core) * 128, 128), 128)
        copies.append(pltpu.make_async_copy(cot_far.at[there, :], cots.at[k], done.at[k]))
    for copy in copies:
        copy.start()
    up = sum(tn(a[256:384, :], a[128:256, :]) for a in parts)
    out_grad = jnp.zeros((GROUP_WIDTH, 768), f32)
    for k in range(RING):
        rows = pl.ds(pl.multiple_of(turn(z - k) * 128, 128), 128)
        out_grad = out_grad + tn(context[rows, :GROUP_WIDTH], parts[k][384:, :])
    for copy in copies:
        copy.wait()
    down = sum(tn(a[:128, :], cots[k]) for k, a in enumerate(parts))
    for i in range(RING):
        made = []
        for c in range(CORES):
            made.append(down[384 * c + 96 * i : 384 * c + 96 * i + 96])
            made.append(out_grad[96 * c + 24 * i : 96 * c + 24 * i + 24])
        for r in range(RING * CORES):
            made.append(up[96 * r + 24 * i : 96 * r + 24 * i + 24])
        out[432 * i : 432 * (i + 1), :] = jnp.concatenate(made, axis=0).astype(bf16)


def cut_up(outs, whole, place):
    rows = outs[0].shape[0]
    for k in range(RING):
        there = pl.ds(pl.multiple_of(turn(place + k - RING) * rows, 8), rows)
        outs[k][...] = whole[there, :].astype(bf16)


def put_together(whole, parts, place):
    rows = parts[0].shape[0]
    for k in range(RING):
        there = pl.ds(pl.multiple_of(turn(place - k) * rows, 8), rows)
        whole[there, :] = parts[k][...].astype(f32)


def early_end_kernel(meta, total, down, out, up):
    whole = total[...].astype(f32)
    for i in range(RING):
        at = 224 * i
        down[96 * i : 96 * (i + 1), :] = whole[at : at + 96]
        out[24 * i : 24 * (i + 1), :] = whole[at + 96 : at + 120]
        for t in range(RING):
            up[24 * i : 24 * (i + 1), 768 * t : 768 * (t + 1)] = whole[
                at + 120 + 24 * t : at + 144 + 24 * t
            ]


def collect_kernel(meta, *refs):
    dqs, dkvs = refs[:4], refs[4:9]
    normed, span_tokens, w_qkv, sums, sum_up, early = refs[9:15]
    dnormeds, lates = refs[15:19], refs[19:23]
    dqkv = refs[23]
    z = meta[17]
    dq = sum(part[...].astype(f32) for part in dqs)
    dqkv[:, 384:] = (dq.astype(bf16).astype(f32) * 0.125).astype(bf16)
    dqkv[:, :384] = sum(part[...].astype(f32) for part in dkvs).astype(bf16)
    grads = dqkv[...]
    dnormed = nt(grads, w_qkv[...])
    for t in range(RING):
        put_by_distance(dnormeds, z, t, dnormed[128 * t : 128 * (t + 1), :].astype(bf16))
    xhat, _ = center_rows(span_tokens[...].astype(f32))
    gain_grad = jnp.sum(dnormed * xhat, axis=0, keepdims=True)
    shift_grad = jnp.sum(dnormed, axis=0, keepdims=True)
    ones = jnp.ones((8, 512), bf16)
    bias = dense(ones, grads)
    row = lax.broadcasted_iota(jnp.int32, (8, 768), 0)
    vec = sums[...]
    vec = jnp.where(row == 0, gain_grad, jnp.where(row == 1, shift_grad, vec))
    weight = tn(normed[...], grads)
    for t in range(RING):
        top = pieces([(vec, 3 * t + n) for n in range(3)] + [None])
        mine = z == t
        from_q = pieces([(bias, 6 + n) for n in range(3)] + [None])
        from_v = pieces([(bias, 3 + n) for n in range(3)] + [None])
        row8 = lax.broadcasted_iota(jnp.int32, (8, WIDE), 0)
        top = jnp.where(mine & (row8 == 2), from_q, jnp.where(mine & (row8 == 3), from_v, top))
        lines = jnp.zeros((8, WIDE), f32)
        up = jnp.broadcast_to(sum_up[:, 768 * t : 768 * (t + 1)], (8, 768))
        for q in range(4):
            line = pieces([(up, 3 * q + n) for n in range(3)] + [None])
            lines = jnp.where(row8 == q, line, lines)
        bottom = jnp.concatenate(
            [jnp.concatenate([top, lines], axis=0), jnp.zeros((16, 512), f32)], axis=1
        )
        mine = weight[GROUP_WIDTH * t : GROUP_WIDTH * (t + 1), :]
        made = []
        for n in range(3):
            block = mine[48 * n : 48 * (n + 1), :]
            side = [(block, 8)] + [(mine[144:, :], 3 * n + m) for m in range(3)]
            made.append(jnp.concatenate([block[:, :512], pieces(side)], axis=1))
        value = jnp.concatenate(made + [bottom], axis=0).astype(bf16)
        put_by_distance([ref.at[:160, :] for ref in lates], z, t, value)
        put_by_distance(
            [ref.at[160:, :] for ref in lates], z, t, early[240 + 48 * t : 288 + 48 * t, :]
        )


def end_norm_kernel(meta, n0, n1, n2, n3, tokens, vec, dmiddle, out):
    dnormed = sum(part[...].astype(f32) for part in (n0, n1, n2, n3))
    xhat, scale = center_rows(tokens[...].astype(f32))
    grad = dnormed * vec[0:1, :]
    out[...] = dmiddle[...] + scale * (
        grad
        - jnp.mean(grad, axis=-1, keepdims=True)
        - xhat * jnp.mean(grad * xhat, axis=-1, keepdims=True)
    )


def late_kernel(meta, *refs):
    parts, early = refs[:4], refs[4]
    keep, send, wide, ups, weight = refs[5:]
    core, z = meta[16], meta[17]
    vec = sum(part[144:160, :640].astype(f32) for part in parts).astype(bf16)
    wide[...] = early[:240, :].astype(f32)
    for k in range(RING):
        place = turn(z - k)
        ups[pl.ds(pl.multiple_of(place * 48, 16), 48), :] = parts[k][160:, :].astype(f32)
        weight[k, :144, :512] = parts[k][:144, :512]
        weight[k, :144, 512:] = pieces([(parts[k][:144, :], 8), None]).astype(bf16)
        tail = [(parts[k][48 * n : 48 * (n + 1), :], 9 + m) for n in range(3) for m in range(3)]
        weight[k, 144:, :] = pieces(tail + [None]).astype(bf16)
        to = pl.ds(pl.multiple_of(place * 96, 32), 96)
        for ref, side in ((keep, core), (send, 1 - core)):
            ref[to, :640] = weight[k, pl.ds(pl.multiple_of(side * 96, 32), 96), :]
            ref[to, 640:] = jnp.zeros((96, 128), bf16)
    for ref, side in ((keep, core), (send, 1 - core)):
        ref[384:400, :640] = vec
        ref[384:400, 640:] = jnp.zeros((16, 128), bf16)
        made = [wide[pl.ds(pl.multiple_of(side * 120, 8), 120), :]]
        for t in range(RING):
            made.append(ups[pl.ds(pl.multiple_of(48 * t + side * 24, 8), 24), :])
        made.append(jnp.zeros((8, 768), f32))
        ref[400:, :] = jnp.concatenate(made, axis=0).astype(bf16)


def late_sum_kernel(meta, keep, got, *refs):
    early, whole = refs[4], refs[5]
    whole[:400, :] = keep[:400, :640].astype(f32) + got[:400, :640].astype(f32)
    whole[400:, :] = jnp.zeros((48, 640), f32)
    cut_up(refs[:4], whole, meta[19])
    early[...] = (keep[400:, :].astype(f32) + got[400:, :].astype(f32)).astype(bf16)


def late_end_kernel(meta, *refs):
    key_grad, value_grad, query_grad = refs[4:7]
    lines, up_line, whole = refs[7:15], refs[15], refs[16]
    put_together(whole, refs[:4], meta[19])
    parts = [whole[96 * t : 96 * (t + 1), :] for t in range(RING)]
    for n, out in enumerate((key_grad, value_grad, query_grad)):
        out[...] = pieces([(parts[t], 3 * n + m) for t in range(RING) for m in range(3)])
    vec = whole[384:400, :WIDE]
    core = meta[16]
    turned = pltpu.roll(vec, WIDE - 96, 1)
    mine = jnp.where(core == 0, vec, turned)
    for n in range(8):
        lines[n][...] = mine[n, :96]
    first = jnp.where(core == 0, vec[8:9, :], vec[10:11, :])
    second = jnp.where(core == 0, vec[9:10, :], vec[11:12, :])
    spread_line = pieces(
        [(first, 0), (first, 1), (first, 2), (second, 0), (second, 1), (second, 2)]
    )
    up_line[...] = spread_line[0, :]


def on_device(
    tokens,
    span_order,
    first_gain,
    first_shift,
    query_weight,
    query_bias,
    key_weight,
    value_weight,
    value_bias,
    out_weight,
    out_bias,
    second_gain,
    second_shift,
    up_weight,
    up_bias,
    down_weight,
    down_bias,
    cotangent,
):
    shard_at = lax.axis_index("shard")
    z, core = shard_at // CORES, shard_at % CORES
    ctx_at = lax.axis_index("ctx")
    y, xq = ctx_at // RING, ctx_at % RING
    rows, width = tokens.shape
    low = ((rows, width), bf16)

    steps = jnp.arange(RING, dtype=jnp.int32)
    groups = jnp.concatenate([((y - steps) % RING) * RING + xq, y * RING + (xq - steps) % RING])
    stored = (2 * groups[:, None] + jnp.arange(2, dtype=jnp.int32)[None, :]).reshape(-1)
    found = stored[:, None] == jnp.arange(span_order.shape[0], dtype=jnp.int32)[None, :]
    spans = jnp.sum(jnp.where(found, span_order[None, :], 0), axis=1)
    meta = jnp.concatenate([spans, jnp.stack([core, z, xq, y]).astype(jnp.int32)])

    vectors = (
        first_gain,
        first_shift,
        query_bias,
        value_bias,
        out_bias,
        second_gain,
        second_shift,
        down_bias,
        up_bias,
    )
    chunks = run(
        arrange_kernel,
        "arrange_weights",
        [((240, width), bf16)] * 4,
        (meta, tokens, key_weight, value_weight, query_weight, *vectors),
        scratch=[pltpu.VMEM((16, 128), f32)],
    )
    arrived = deliver(chunks, move_z)
    out_down = jnp.concatenate([out_weight, down_weight], axis=0)
    arrived, out_down, up_own, cot_own = lax.optimization_barrier(
        (arrived, out_down, up_weight, cotangent)
    )
    arrived_others = [swap_core(part) for part in arrived]
    w_out_down = lax.all_gather(out_down, "shard", axis=0, tiled=True)
    w_up = lax.all_gather(up_own, "shard", axis=0, tiled=True)
    cot_all = lax.all_gather(cot_own, "shard", axis=0, tiled=True)
    span_tokens, normed, queries, kv_own, w_qkv, vec, b_up = run(
        project_kernel,
        "project",
        [
            ((512, width), bf16),
            ((512, width), bf16),
            ((512, WIDE), bf16),
            ((512, 384), bf16),
            ((width, 640), bf16),
            ((16, width), f32),
            ((1, 4 * width), f32),
        ],
        (meta, *arrived, *arrived_others),
        scratch=[pltpu.VMEM((8, 16, 128), bf16)],
    )
    kv_parts = spread(kv_own, move_x)
    queries_all = spread(queries, move_y)
    kv_parts, queries_all = lax.optimization_barrier((kv_parts, queries_all))
    kv_others = [swap_core(part) for part in kv_parts]
    partial = forward_call(meta, queries_all, kv_parts, kv_others)

    context, *context_chunks = run(
        merge_groups_kernel,
        "merge_groups",
        [((512, WIDE), bf16)] + [((128, WIDE), bf16)] * 4,
        (meta, *give_back(partial, move_y)),
    )
    far = pl.BlockSpec(memory_space=pl.ANY)
    middle = run(
        middle_kernel,
        "feed_forward",
        [low, ((rows, width), f32)]
        + [((4 * rows, width), bf16)] * 4
        + [((128, GROUP_WIDTH), bf16)] * 4
        + [((8, width), f32), ((1, 4 * width), f32)],
        (
            meta,
            tokens,
            cotangent,
            *deliver(context_chunks, move_z),
            w_out_down,
            w_up,
            vec,
            b_up,
        ),
        specs=[SM] + [VM] * 6 + [far, far, VM, VM],
        scratch=[
            pltpu.VMEM((width, width), bf16),
            pltpu.VMEM((width, 4 * width), bf16),
            pltpu.VMEM((4 * width, width), bf16),
            pltpu.SemaphoreType.DMA,
            pltpu.SemaphoreType.DMA((2 * RING, 2)),
        ],
    )
    activations, dmiddle = middle[:2]
    early_sent, dcontexts = middle[2:6], middle[6:10]
    sums, sum_up = middle[10:]

    (packed,) = run(
        pack_kernel,
        "pack_context_gradient",
        [((512, WIDE), bf16)],
        (meta, *deliver(dcontexts, move_z), context),
        scratch=[pltpu.VMEM((512, GROUP_WIDTH), bf16)],
    )
    packed, early_sent = lax.optimization_barrier((packed, early_sent))
    grads_all = spread(packed, move_y)
    early_parts = deliver(early_sent, move_z)
    dkv_own, dkv_oth, dq_so_far = backward_call(
        1, meta, queries_all, grads_all, kv_parts[1:], kv_others[1:]
    )

    dkv_oth, dq_so_far, early_parts = lax.optimization_barrier((dkv_oth, dq_so_far, early_parts))
    (early,) = run(
        early_kernel,
        "early_gradients",
        [((1728, width), bf16)],
        (meta, *early_parts, context, cot_all),
        specs=[SM] + [VM] * 5 + [far],
        scratch=[
            pltpu.VMEM((RING, rows, width), bf16),
            pltpu.SemaphoreType.DMA((RING,)),
        ],
    )
    dkv_got = swap_core(dkv_oth)
    dq_so_far, early, dkv_got = lax.optimization_barrier((dq_so_far, early, dkv_got))
    early = lax.psum_scatter(
        early, "ctx", axis_index_groups=COLUMN_GROUPS, scatter_dimension=0, tiled=True
    )
    dkv_sums = [sum_low([dkv_own[k], dkv_got[512 * k : 512 * (k + 1)]]) for k in range(3)]
    dkv_arrived = [move_x(dkv_sums[k], -1 - k) for k in range(3)]
    dkv_own0, dkv_oth0, dqs = backward_call(
        0, meta, queries_all, grads_all, kv_parts[:1], kv_others[:1], *dq_so_far, last=True
    )
    dqs, dkv_oth0, dkv_arrived = lax.optimization_barrier((dqs, dkv_oth0, dkv_arrived))
    dq_arrived = give_back(dqs, move_y)
    dkv_got0 = swap_core(dkv_oth0)

    collected = run(
        collect_kernel,
        "collect",
        [low] * 4 + [((208, width), bf16)] * 4,
        (
            meta,
            *dq_arrived,
            dkv_own0[0],
            dkv_got0,
            *dkv_arrived,
            normed,
            span_tokens,
            w_qkv,
            sums,
            sum_up,
            early,
        ),
        scratch=[pltpu.VMEM((512, 640), bf16)],
    )
    late_parts = deliver(collected[4:], move_z)
    late_keep, late_send = run(
        late_kernel,
        "late",
        [((624, width), bf16)] * 2,
        (meta, *late_parts, early),
        scratch=[
            pltpu.VMEM((240, width), f32),
            pltpu.VMEM((192, width), f32),
            pltpu.VMEM((RING, GROUP_WIDTH, 640), bf16),
        ],
    )
    *late_chunks, early = run(
        late_sum_kernel,
        "late_sum",
        [((112, 640), bf16)] * 4 + [((224, width), bf16)],
        (meta, late_keep, swap_core(late_send)),
        scratch=[pltpu.VMEM((448, 640), f32)],
    )
    late_arrived = deliver(late_chunks, move_y)
    early_parts = spread(early, move_x)
    late_arrived, early_parts = lax.optimization_barrier((late_arrived, early_parts))
    early_total = lax.all_gather(
        sum_low(early_parts), "ctx", axis_index_groups=COLUMN_GROUPS, axis=0, tiled=True
    )
    late_parts = spread(sum_low(late_arrived), move_x)
    late_parts, dnormed_sent = lax.optimization_barrier((late_parts, collected[:4]))
    dnormed_parts = deliver(dnormed_sent, move_z)
    (input_grad,) = run(
        end_norm_kernel,
        "end_norm",
        [((rows, width), f32)],
        (meta, *dnormed_parts, tokens, vec, dmiddle),
    )
    late_sums = spread(sum_low(late_parts), move_y)
    grad_down, grad_out, grad_up = run(
        early_end_kernel,
        "early_end",
        [((384, width), f32), ((96, width), f32), ((96, 4 * width), f32)],
        (meta, early_total),
    )
    key_grad, value_grad, query_grad, *vec_grads = run(
        late_end_kernel,
        "late_end",
        [((96, width), f32)] * 3 + [((96,), f32)] * 8 + [((384,), f32)],
        (meta, *late_sums),
        scratch=[pltpu.VMEM((448, 640), f32)],
    )
    return (
        activations,
        input_grad,
        vec_grads[0],
        vec_grads[1],
        query_grad,
        vec_grads[2],
        key_grad,
        value_grad,
        vec_grads[3],
        grad_out,
        vec_grads[4],
        vec_grads[5],
        vec_grads[6],
        grad_up,
        vec_grads[8],
        grad_down,
        vec_grads[7],
    )


def solution(mesh):
    tokens_spec = P(("ctx", "shard"), None)
    vector_spec = P("shard")
    matrix_spec = P("shard", None)
    return jax.shard_map(
        on_device,
        mesh=mesh,
        in_specs=(
            tokens_spec,
            P(),
            vector_spec,
            vector_spec,
            matrix_spec,
            vector_spec,
            matrix_spec,
            matrix_spec,
            vector_spec,
            matrix_spec,
            vector_spec,
            vector_spec,
            vector_spec,
            matrix_spec,
            vector_spec,
            matrix_spec,
            vector_spec,
            tokens_spec,
        ),
        out_specs=(
            tokens_spec,
            tokens_spec,
            vector_spec,
            vector_spec,
            matrix_spec,
            vector_spec,
            matrix_spec,
            matrix_spec,
            vector_spec,
            matrix_spec,
            vector_spec,
            vector_spec,
            vector_spec,
            matrix_spec,
            vector_spec,
            matrix_spec,
            vector_spec,
        ),
        check_vma=False,
    )
```

```python
import jax
import jax.numpy as jnp
from jax import lax
from jax.experimental import pallas as pl
from jax.experimental.pallas import tpu as pltpu
from jax.sharding import PartitionSpec as P

HEAD_DIM = 64
RING = 4
CORES = 2
GROUP_HEADS = 3
GROUP_WIDTH = GROUP_HEADS * HEAD_DIM
WIDE = 256
BLOCK = 256

norm_eps = 1e-05
lowest = -1e30
tiny = 1e-30
log2_e = 1.4426950408889634
ln_2 = 0.6931471805599453

bf16 = jnp.bfloat16
f32 = jnp.float32


def dense(left, right):
    return jnp.dot(left, right, preferred_element_type=f32)


def nt(left, right):
    return lax.dot_general(left, right, (((1,), (1,)), ((), ())), preferred_element_type=f32)


def tn(left, right):
    return lax.dot_general(left, right, (((0,), (0,)), ((), ())), preferred_element_type=f32)


def move_z(x, hops):
    size = RING * CORES
    return lax.ppermute(x, "shard", [(r, (r + CORES * hops) % size) for r in range(size)])


def swap_core(x):
    return lax.ppermute(x, "shard", [(r, r ^ 1) for r in range(RING * CORES)])


def move_x(x, hops):
    pairs = [(c, (c // RING) * RING + (c + hops) % RING) for c in range(RING * RING)]
    return lax.ppermute(x, "ctx", pairs)


def move_y(x, hops):
    size = RING * RING
    return lax.ppermute(x, "ctx", [(c, (c + RING * hops) % size) for c in range(size)])


def spread(x, move):
    return [x] + [move(x, k) for k in range(1, RING)]


def deliver(chunks, move):
    return [chunks[0]] + [move(chunks[k], k) for k in range(1, RING)]


def give_back(chunks, move):
    return [chunks[0]] + [move(chunks[k], -k) for k in range(1, RING)]


def sum_low(parts):
    total = parts[0].astype(f32)
    for part in parts[1:]:
        total = total + part.astype(f32)
    return total.astype(bf16)


COLUMN_GROUPS = [[RING * j + i for j in range(RING)] for i in range(RING)]


VM = pl.BlockSpec(memory_space=pltpu.VMEM)
SM = pl.BlockSpec(memory_space=pltpu.SMEM)


def run(kernel, name, outs, args, scratch=(), specs=None, cost=None):
    return pl.pallas_call(
        kernel,
        out_shape=tuple(jax.ShapeDtypeStruct(shape, dtype) for shape, dtype in outs),
        in_specs=specs or [SM] + [VM] * (len(args) - 1),
        out_specs=tuple(VM for _ in outs),
        scratch_shapes=list(scratch),
        cost_estimate=cost,
        compiler_params=pltpu.CompilerParams(vmem_limit_bytes=56 * 2**20),
        name=name,
    )(*args)


def turn(at, size=RING):
    return lax.rem(at + size, size)


def tile(x, k):
    return x[:, 128 * k : 128 * (k + 1)]


def pieces(sources):
    made = []
    rows = next(source for source in sources if source is not None)[0].shape[0]
    for left, right in zip(sources[::2], sources[1::2]):
        sides = []
        for side, source in enumerate((left, right)):
            if source is None:
                sides.append(None)
                continue
            value = tile(source[0], source[1] // 2).astype(f32)
            sides.append(value if source[1] % 2 == side else pltpu.roll(value, 64, 1))
        low, high = (jnp.zeros((rows, 128), f32) if part is None else part for part in sides)
        lane = lax.broadcasted_iota(jnp.int32, (rows, 128), 1)
        made.append(jnp.where(lane < 64, low, high))
    return jnp.concatenate(made, axis=1)


def lanes_of(rows, first, last):
    lane = lax.broadcasted_iota(jnp.int32, (rows, WIDE), 1)
    return jnp.where((lane >= first) & (lane < last), 1.0, 0.0).astype(bf16)


def put_by_distance(refs, place, at, value):
    for k in range(RING):

        @pl.when(turn(at - place) == k)
        def _(k=k):
            refs[k][...] = value


def split3(value):
    high = value.astype(bf16).astype(f32)
    rest = value - high
    mid = rest.astype(bf16).astype(f32)
    return high, mid, rest - mid


def arrange_kernel(meta, tokens, wk, wv, wq, *refs):
    vectors, outs, vec = refs[:9], refs[9:13], refs[13]
    for ref in outs:
        ref[:128, :] = tokens[...]
    vec[...] = jnp.zeros(vec.shape, f32)
    for n in range(8):
        vec[n : n + 1, :96] = vectors[n][...].astype(f32).reshape(1, 96)
    for n in range(3):
        vec[8 + n : 9 + n, :] = vectors[8][128 * n : 128 * (n + 1)].astype(f32).reshape(1, 128)
    lines = jnp.concatenate([vec[...].astype(bf16), jnp.zeros((16, 512), bf16)], axis=1)
    for t in range(RING):
        parts = [(w, 3 * t + n) for w in (wk, wv, wq) for n in range(3)] + [None]
        chunk = pieces(parts).astype(bf16)
        put_by_distance(
            [ref.at[128:, :640] for ref in outs],
            meta[17],
            t,
            jnp.concatenate([chunk, lines], axis=0),
        )


def center_rows(values):
    center = values - jnp.mean(values, axis=-1, keepdims=True)
    spread_ = jnp.mean(center * center, axis=-1, keepdims=True)
    scale = lax.rsqrt(spread_ + norm_eps)
    return center * scale, scale


def project_kernel(meta, *refs):
    parts, others = refs[:4], refs[4:8]
    span_tokens, normed, queries, kv, w_out, vec_out, up_out, vec_in = refs[8:]
    core, z = meta[16], meta[17]
    for k in range(RING):
        place = turn(z - k)
        span_tokens[pl.ds(pl.multiple_of(place * 128, 128), 128), :] = parts[k][:128, :]
        for source, side in ((parts[k], core), (others[k], 1 - core)):
            rank = 2 * place + side
            w_out[pl.ds(pl.multiple_of(rank * 96, 32), 96), :] = source[128:224, :640]
            vec_in[rank] = source[224:240, :128]
    row = lax.broadcasted_iota(jnp.int32, (128, 768), 0)
    col = lax.broadcasted_iota(jnp.int32, (128, 768), 1)
    vec = jnp.zeros((16, 768), f32)
    for rank in range(2 * RING):
        there = jnp.where((row < 96) & (col == row + 96 * rank), 1.0, 0.0).astype(bf16)
        vec = vec + dense(vec_in[rank], there)
    vec_out[...] = vec
    for rank in range(2 * RING):
        for n in range(3):
            at = 384 * rank + 128 * n
            up_out[:, at : at + 128] = vec_in[rank, 8 + n : 9 + n, :].astype(f32)
    xhat, _ = center_rows(span_tokens[...].astype(f32))
    low = (xhat * vec[0:1, :] + vec[1:2, :]).astype(bf16)
    normed[...] = low
    bias = jnp.zeros((8, 640), f32)
    bias_q = jnp.broadcast_to(vec[2:3, :], (8, 768))
    bias_v = jnp.broadcast_to(vec[3:4, :], (8, 768))
    for t in range(RING):
        here = pieces(
            [None] * 3
            + [(bias_v, 3 * t + n) for n in range(3)]
            + [(bias_q, 3 * t + n) for n in range(3)]
            + [None]
        )
        bias = jnp.where(z == t, here, bias)
    projected = dense(low, w_out[...]) + bias[0:1, :]
    kv[...] = projected[:, :384].astype(bf16)
    queries[...] = (projected[:, 384:] * (0.125 * log2_e)).astype(bf16)


def places(parity, rows):
    at = rows % BLOCK
    side = jnp.where(rows < BLOCK, parity, 1 - parity)
    return (at // 128) * 256 + side * 128 + at % 128


def allowed_block(parity):
    key_at = lax.broadcasted_iota(jnp.int32, (2 * BLOCK, BLOCK), 0)
    query_at = lax.broadcasted_iota(jnp.int32, (2 * BLOCK, BLOCK), 1)
    return places(parity, key_at) <= places(parity, query_at)


def forward_kernel(meta, *refs):
    queries, kv_own, kv_oth, outs = (refs[4 * n : 4 * (n + 1)] for n in range(4))
    kv, v_turned, q_turned, best, acc, out = refs[16:]
    parity = meta[16]
    keys = 2 * BLOCK
    row = lax.broadcasted_iota(jnp.int32, (128, BLOCK), 0)
    for j in range(8):
        rows = slice(BLOCK * (j % 2), BLOCK * (j % 2 + 1))
        for side, kvs in enumerate((kv_own, kv_oth)):
            cols = slice(BLOCK * side, BLOCK * (side + 1))
            kv[j, cols, :] = kvs[j // 2][rows, :WIDE]
            turned = kvs[j // 2][rows, 128:].astype(f32).T.astype(bf16)
            for h in range(GROUP_HEADS):
                v_turned[j, 80 * h : 80 * h + 64, cols] = turned[64 * (h + 1) : 64 * (h + 2)]
                v_turned[j, 80 * h + 64 : 80 * h + 80, cols] = jnp.ones((16, BLOCK), bf16)
        query = queries[j // 2][rows, :].astype(f32).T
        q_turned[j, 0] = jnp.where(row < 64, query[:128], 0.0).astype(bf16)
        q_turned[j, 1] = jnp.where(row < 64, 0.0, query[:128]).astype(bf16)
        q_turned[j, 2] = query[128:].astype(bf16)

    def one_span(i, carry):
        best[...] = jnp.full(best.shape, lowest, f32)
        acc[...] = jnp.zeros(acc.shape, f32)

        def visit(j, masked):
            if masked:
                allowed = allowed_block(parity)
            every = [
                dense(kv[j, :, 128 * (h // 2) : 128 * (h // 2 + 1)], q_turned[i, h])
                for h in range(GROUP_HEADS)
            ]
            fades, lows = [], []
            for h in range(GROUP_HEADS):
                scores = every[h]
                if masked:
                    scores = jnp.where(allowed, scores, lowest)
                old = best[h : h + 1, :]
                new = jnp.maximum(old, jnp.max(scores, axis=0, keepdims=True))
                weights = jnp.exp2(scores - new)
                if masked:
                    weights = jnp.where(allowed, weights, 0.0)
                best[h : h + 1, :] = new
                lows.append(weights.astype(bf16))
                fades.append(jnp.exp2(old - new))
            for h in range(GROUP_HEADS):
                here = slice(80 * h, 80 * (h + 1))
                acc[here, :] = acc[here, :] * fades[h] + dense(v_turned[j, here, :], lows[h])

        def one_block(j, carry):
            @pl.when(meta[8 + j] < meta[i])
            def _():
                visit(j, False)

            @pl.when(meta[8 + j] == meta[i])
            def _():
                visit(j, True)

            return carry

        lax.fori_loop(0, 8, one_block, 0)
        row = lax.broadcasted_iota(jnp.int32, (HEAD_DIM, BLOCK), 0)
        parts = []
        extra = jnp.zeros((HEAD_DIM, BLOCK), f32)
        for h in range(GROUP_HEADS):
            count = jnp.maximum(acc[80 * h + 64 : 80 * h + 65, :], tiny)
            parts.append(acc[80 * h : 80 * h + 64, :] / count)
            terms = split3(best[h : h + 1, :] + jnp.log(count) * log2_e)
            for t in range(3):
                extra = jnp.where(row == 3 * h + t, terms[t], extra)
        out[i] = jnp.concatenate(parts + [extra], axis=0).T.astype(bf16)
        return carry

    lax.fori_loop(0, 8, one_span, 0)
    for i in range(8):
        outs[i // 2][BLOCK * (i % 2) : BLOCK * (i % 2 + 1), :] = out[i]


def forward_call(meta, queries, kv_own, kv_oth):
    return run(
        forward_kernel,
        "attention_forward",
        [((2 * BLOCK, WIDE), bf16)] * 4,
        (meta, *queries, *kv_own, *kv_oth),
        scratch=[
            pltpu.VMEM((8, 2 * BLOCK, WIDE), bf16),
            pltpu.VMEM((8, 240, 2 * BLOCK), bf16),
            pltpu.VMEM((8, GROUP_HEADS, 128, BLOCK), bf16),
            pltpu.VMEM((8, BLOCK), f32),
            pltpu.VMEM((240, BLOCK), f32),
            pltpu.VMEM((8, BLOCK, WIDE), bf16),
        ],
        cost=pl.CostEstimate(flops=20 * 10**9, bytes_accessed=10**7, transcendentals=13 * 10**6),
    )


def one_hot(where):
    return jnp.where(where, 1.0, 0.0).astype(bf16)


def merge_rows(parts):
    row = lax.broadcasted_iota(jnp.int32, (WIDE, WIDE), 0)
    col = lax.broadcasted_iota(jnp.int32, (WIDE, WIDE), 1)
    to_lanes = one_hot((row >= 192) & (row < 201) & (col < 192) & ((row - 192) // 3 == col // 64))
    logs = [dense(part, to_lanes) for part in parts]
    best = logs[0]
    for part in logs[1:]:
        best = jnp.maximum(best, part)
    total = jnp.zeros_like(best)
    context = jnp.zeros_like(best)
    for part, log in zip(parts, logs):
        weight = jnp.exp2(log - best)
        total = total + weight
        context = context + weight * part.astype(f32)
    context = context / total
    terms = split3(best + jnp.log(total) * log2_e)
    extra = jnp.zeros_like(best)
    for t in range(3):
        back = one_hot((row < 192) & (row % 64 == 0) & (col == 192 + 3 * (row // 64) + t))
        extra = extra + dense(terms[t].astype(bf16), back)
    lane = lax.broadcasted_iota(jnp.int32, best.shape, 1)
    return jnp.where(lane < 192, context, extra).astype(bf16)


def merge_groups_kernel(meta, *refs):
    whole = refs[4]
    whole[...] = merge_rows([ref[...] for ref in refs[:4]])
    for k in range(RING):
        rows = pl.ds(pl.multiple_of(turn(meta[17] + k - RING) * 128, 128), 128)
        refs[5 + k][...] = whole[rows, :]


def middle_kernel(meta, *refs):
    tokens, cot = refs[:2]
    contexts = refs[2:6]
    out_down_far, up_far, vec, b_up = refs[6:10]
    act, dmiddle_out = refs[10:12]
    early, dcontexts = refs[12:16], refs[16:20]
    sums, sum_up, w_out, w_up, w_down, up_done, done = refs[20:]
    z = meta[17]
    up_copy = pltpu.make_async_copy(up_far, w_up, up_done)
    out_copies, down_copies = [], []
    for r in range(2 * RING):
        at = 480 * r
        out_copies.append(
            pltpu.make_async_copy(
                out_down_far.at[at : at + 96, :], w_out.at[96 * r : 96 * (r + 1), :], done.at[r, 0]
            )
        )
        down_copies.append(
            pltpu.make_async_copy(
                out_down_far.at[at + 96 : at + 480, :],
                w_down.at[384 * r : 384 * (r + 1), :],
                done.at[r, 1],
            )
        )
    for copy in out_copies:
        copy.start()
    up_copy.start()
    for copy in down_copies:
        copy.start()
    for copy in out_copies:
        copy.wait()
    middle = tokens[...].astype(f32) + vec[4:5, :]
    for k in range(RING):
        rows = pl.ds(pl.multiple_of(turn(z - k) * GROUP_WIDTH, 64), GROUP_WIDTH)
        middle = middle + dense(contexts[k][:, :GROUP_WIDTH], w_out[rows, :])
    xhat, scale = center_rows(middle)
    gain = vec[5:6, :]
    second = (xhat * gain + vec[6:7, :]).astype(bf16)
    for ref in early:
        ref[256:384, :] = second
    cot_low = cot[...]
    up_copy.wait()
    for copy in down_copies:
        copy.wait()
    total = middle + vec[7:8, :]
    dsecond = jnp.zeros_like(middle)
    width = 768
    for n in range(RING):
        cols = slice(width * n, width * (n + 1))
        pre = dense(second, w_up[:, cols]) + b_up[:, cols]
        square = pre * pre
        inner = jnp.tanh(0.7978845608028654 * (pre + 0.044715 * (square * pre)))
        half = 0.5 * (1.0 + inner)
        hidden = (pre * half).astype(bf16)
        slope = half + (0.5 * 0.7978845608028654) * pre * (1.0 - inner * inner) * (
            1.0 + 3.0 * 0.044715 * square
        )
        total = total + dense(hidden, w_down[cols, :])
        dpre = (nt(cot_low, w_down[cols, :]) * slope).astype(bf16)
        dsecond = dsecond + nt(dpre, w_up[:, cols])
        sum_up[:, cols] = jnp.sum(dpre.astype(f32), axis=0, keepdims=True)
        put_by_distance([ref.at[:128, :] for ref in early], z, n, hidden)
        put_by_distance([ref.at[128:256, :] for ref in early], z, n, dpre)
    act[...] = total.astype(bf16)
    grad = dsecond * gain
    dnorm = scale * (
        grad
        - jnp.mean(grad, axis=-1, keepdims=True)
        - xhat * jnp.mean(grad * xhat, axis=-1, keepdims=True)
    )
    upstream = cot_low.astype(f32)
    dmiddle = upstream + dnorm
    dmiddle_out[...] = dmiddle
    dmid = dmiddle.astype(bf16)
    for ref in early:
        ref[384:512, :] = dmid
    for t in range(RING):
        rows = slice(GROUP_WIDTH * t, GROUP_WIDTH * (t + 1))
        put_by_distance(dcontexts, z, t, nt(dmid, w_out[rows, :]).astype(bf16))
    row = lax.broadcasted_iota(jnp.int32, (8, width), 0)
    lines = (
        dmid.astype(f32),
        dsecond * xhat,
        dsecond,
        upstream,
    )
    gathered = jnp.zeros((8, width), f32)
    for n, line in enumerate(lines):
        gathered = jnp.where(row == 4 + n, jnp.sum(line, axis=0, keepdims=True), gathered)
    sums[...] = gathered


def pack_kernel(meta, d0, d1, d2, d3, context, out, dcontext):
    for k, part in enumerate((d0, d1, d2, d3)):
        dcontext[pl.ds(pl.multiple_of(turn(meta[17] - k) * 128, 128), 128), :] = part[...]
    row = lax.broadcasted_iota(jnp.int32, (GROUP_WIDTH, WIDE), 0)
    col = lax.broadcasted_iota(jnp.int32, (GROUP_WIDTH, WIDE), 1)
    product = dcontext[...].astype(f32) * context[:, :GROUP_WIDTH].astype(f32)
    by_head = one_hot((col < 9) & (row // 64 == col // 3))
    delta = jnp.zeros(out.shape, f32)
    for term in split3(product):
        delta = delta + dense(term.astype(bf16), by_head)
    high, mid, low = split3(delta)
    lane = lax.broadcasted_iota(jnp.int32, out.shape, 1)
    delta_terms = jnp.where(lane % 3 == 0, high, jnp.where(lane % 3 == 1, mid, low))
    row2 = lax.broadcasted_iota(jnp.int32, (WIDE, WIDE), 0)
    col2 = lax.broadcasted_iota(jnp.int32, (WIDE, WIDE), 1)
    log_terms = dense(context[...], one_hot((row2 >= 192) & (row2 < 201) & (col2 == row2 - 183)))
    shifted = dense(dcontext[...], one_hot(col == row + 64))
    out[...] = jnp.where(
        lane < 9, -delta_terms, jnp.where(lane < 18, -log_terms, shifted)
    ).astype(bf16)


def backward_kernel(group, count, first, last, meta, *refs):
    queries, grads = refs[:4], refs[4:8]
    kv_own, kv_oth = refs[8 : 8 + count], refs[8 + count : 8 + 2 * count]
    refs = refs[8 + 2 * count :]
    if not first:
        dq_in, refs = refs[0], refs[1:]
    dkv_own, dkv_oth, refs = refs[:count], refs[count], refs[count + 1 :]
    if last:
        dqs, refs = refs[:4], refs[4:]
    dq_acc, stats, k_turned, q_full, d_full, kv, dkv, dk_acc, dv_acc = refs
    parity = meta[16]
    keys_rows = 2 * BLOCK
    lane = lax.broadcasted_iota(jnp.int32, (BLOCK, 128), 1)
    left = jnp.where(lane < 64, 1.0, 0.0).astype(bf16)
    right = jnp.where(lane < 64, 0.0, 1.0).astype(bf16)
    wide_lane = lax.broadcasted_iota(jnp.int32, (keys_rows, 128), 1)
    for i in range(8):
        there = slice(BLOCK * (i % 2), BLOCK * (i % 2 + 1))
        grad = grads[i // 2][there, :]
        d_full[i] = grad
        q_full[i] = queries[i // 2][there, :]
        lines = grad[:, :128].astype(f32).T
        for n in range(6):
            stats[i, n : n + 1, :] = (
                lines[3 * n : 3 * n + 1] + lines[3 * n + 1 : 3 * n + 2] + lines[3 * n + 2 : 3 * n + 3]
            )
        dq_acc[i] = jnp.zeros(dq_acc.shape[1:], f32) if first else dq_in[i]
    for j in range(2 * count):
        there = slice(BLOCK * (j % 2), BLOCK * (j % 2 + 1))
        kv[j, :BLOCK, :] = kv_own[j // 2][there, :]
        kv[j, BLOCK:, :] = kv_oth[j // 2][there, :]

    def one_key_block(j, carry):
        keys = kv[j, :, :WIDE]
        k_turned[...] = keys.astype(f32).T.astype(bf16)
        dk_acc[...] = jnp.zeros(dk_acc.shape, f32)
        dv_acc[...] = jnp.zeros(dv_acc.shape, f32)
        key_span = meta[8 + 2 * group + j]

        def visit(i, masked):
            if masked:
                allowed = allowed_block(parity)
            query = q_full[i]
            grad = d_full[i]
            first_key, mid_key, last_key = (kv[j, :, 128 * n : 128 * (n + 1)] for n in range(3))
            scores = [
                nt(first_key, query[:, :128] * left),
                nt(first_key, query[:, :128] * right),
                nt(mid_key, query[:, 128:]),
            ]
            dprobs = [
                nt(mid_key, grad[:, :128] * right),
                nt(last_key, grad[:, 128:] * left),
                nt(last_key, grad[:, 128:] * right),
            ]
            all_weights = []
            all_dscores = []
            for h in range(GROUP_HEADS):
                weights = jnp.exp2(scores[h] + stats[i, 3 + h : 4 + h, :])
                if masked:
                    weights = jnp.where(allowed, weights, 0.0)
                all_weights.append(weights.astype(bf16))
                all_dscores.append((weights * (dprobs[h] + stats[i, h : h + 1, :])).astype(bf16))
            d_heads = jnp.concatenate(
                [
                    grad * lanes_of(BLOCK, HEAD_DIM * (h + 1), HEAD_DIM * (h + 2))
                    for h in range(GROUP_HEADS)
                ],
                axis=0,
            )
            q_heads = jnp.concatenate(
                [
                    query * lanes_of(BLOCK, HEAD_DIM * h, HEAD_DIM * (h + 1))
                    for h in range(GROUP_HEADS)
                ],
                axis=0,
            )
            dv_acc[...] = dv_acc[...] + dense(jnp.concatenate(all_weights, axis=1), d_heads)
            dk_acc[...] = dk_acc[...] + dense(jnp.concatenate(all_dscores, axis=1), q_heads)
            for h in range(GROUP_HEADS):
                here = slice(HEAD_DIM * h, HEAD_DIM * (h + 1))
                dq_acc[i, here, :] = dq_acc[i, here, :] + dense(k_turned[here, :], all_dscores[h])

        def one_span(i, carry):
            @pl.when(key_span < meta[i])
            def _():
                visit(i, False)

            @pl.when(key_span == meta[i])
            def _():
                visit(i, True)

            return carry

        lax.fori_loop(0, 8, one_span, 0)
        dk = dk_acc[...] * ln_2
        dv = dv_acc[...]
        dkv[j, :, :128] = dk[:, :128].astype(bf16)
        dkv[j, :, 128:256] = jnp.where(wide_lane < 64, dk[:, 128:], dv[:, :128]).astype(bf16)
        dkv[j, :, 256:] = dv[:, 128:].astype(bf16)
        return carry

    lax.fori_loop(0, 2 * count, one_key_block, 0)
    for j in range(2 * count):
        there = slice(BLOCK * (j % 2), BLOCK * (j % 2 + 1))
        dkv_own[j // 2][there, :] = dkv[j, :BLOCK, :]
        dkv_oth[BLOCK * j : BLOCK * (j + 1), :] = dkv[j, BLOCK:, :]
    if last:
        for i in range(8):
            there = slice(BLOCK * (i % 2), BLOCK * (i % 2 + 1))
            filled = jnp.concatenate(
                [dq_acc[i], jnp.zeros((WIDE - GROUP_WIDTH, BLOCK), f32)], axis=0
            )
            dqs[i // 2][there, :] = filled.T.astype(bf16)


def backward_call(group, meta, queries, grads, kv_own, kv_oth, dq_in=None, last=False):
    count = len(kv_own)
    first = dq_in is None
    kv_outs = [((2 * BLOCK, 2 * GROUP_WIDTH), bf16)] * count
    kv_outs.append(((count * 2 * BLOCK, 2 * GROUP_WIDTH), bf16))
    dq_shape = (8, GROUP_WIDTH, BLOCK)
    if last:
        dq_outs, accs = [((2 * BLOCK, WIDE), bf16)] * 4, [pltpu.VMEM(dq_shape, f32)]
    else:
        dq_outs, accs = [(dq_shape, f32)], []
    outs = run(
        lambda *refs: backward_kernel(group, count, first, last, *refs),
        f"attention_backward_{group}",
        kv_outs + dq_outs,
        (meta, *queries, *grads, *kv_own, *kv_oth) + (() if first else (dq_in,)),
        scratch=accs
        + [
            pltpu.VMEM((8, 8, BLOCK), f32),
            pltpu.VMEM((WIDE, 2 * BLOCK), bf16),
            pltpu.VMEM((8, BLOCK, WIDE), bf16),
            pltpu.VMEM((8, BLOCK, WIDE), bf16),
            pltpu.VMEM((2 * count, 2 * BLOCK, 2 * GROUP_WIDTH), bf16),
            pltpu.VMEM((2 * count, 2 * BLOCK, 2 * GROUP_WIDTH), bf16),
            pltpu.VMEM((2 * BLOCK, WIDE), f32),
            pltpu.VMEM((2 * BLOCK, WIDE), f32),
        ],
        cost=pl.CostEstimate(
            flops=10 * count * 10**9, bytes_accessed=10**7, transcendentals=4 * count * 10**6
        ),
    )
    return outs[:count], outs[count], outs[count + 1 :]


def early_kernel(meta, *refs):
    parts, context, cot_far, out, cots, done = refs[:4], *refs[4:]
    core, z = meta[16], meta[17]
    copies = []
    for k in range(RING):
        there = pl.ds(pl.multiple_of((2 * turn(z - k) + core) * 128, 128), 128)
        copies.append(pltpu.make_async_copy(cot_far.at[there, :], cots.at[k], done.at[k]))
    for copy in copies:
        copy.start()
    up = sum(tn(a[256:384, :], a[128:256, :]) for a in parts)
    out_grad = jnp.zeros((GROUP_WIDTH, 768), f32)
    for k in range(RING):
        rows = pl.ds(pl.multiple_of(turn(z - k) * 128, 128), 128)
        out_grad = out_grad + tn(context[rows, :GROUP_WIDTH], parts[k][384:, :])
    for copy in copies:
        copy.wait()
    down = sum(tn(a[:128, :], cots[k]) for k, a in enumerate(parts))
    for i in range(RING):
        made = []
        for c in range(CORES):
            made.append(down[384 * c + 96 * i : 384 * c + 96 * i + 96])
            made.append(out_grad[96 * c + 24 * i : 96 * c + 24 * i + 24])
        for r in range(RING * CORES):
            made.append(up[96 * r + 24 * i : 96 * r + 24 * i + 24])
        out[432 * i : 432 * (i + 1), :] = jnp.concatenate(made, axis=0).astype(bf16)


def cut_up(outs, whole, place):
    rows = outs[0].shape[0]
    for k in range(RING):
        there = pl.ds(pl.multiple_of(turn(place + k - RING) * rows, 8), rows)
        outs[k][...] = whole[there, :].astype(bf16)


def put_together(whole, parts, place):
    rows = parts[0].shape[0]
    for k in range(RING):
        there = pl.ds(pl.multiple_of(turn(place - k) * rows, 8), rows)
        whole[there, :] = parts[k][...].astype(f32)


def early_end_kernel(meta, total, down, out, up):
    whole = total[...].astype(f32)
    for i in range(RING):
        at = 224 * i
        down[96 * i : 96 * (i + 1), :] = whole[at : at + 96]
        out[24 * i : 24 * (i + 1), :] = whole[at + 96 : at + 120]
        for t in range(RING):
            up[24 * i : 24 * (i + 1), 768 * t : 768 * (t + 1)] = whole[
                at + 120 + 24 * t : at + 144 + 24 * t
            ]


def collect_kernel(meta, *refs):
    dqs, dkvs = refs[:4], refs[4:9]
    normed, span_tokens, w_qkv, sums, sum_up, early = refs[9:15]
    dnormeds, lates = refs[15:19], refs[19:23]
    dqkv = refs[23]
    z = meta[17]
    dq = sum(part[...].astype(f32) for part in dqs)
    dqkv[:, 384:] = (dq.astype(bf16).astype(f32) * 0.125).astype(bf16)
    dqkv[:, :384] = sum(part[...].astype(f32) for part in dkvs).astype(bf16)
    grads = dqkv[...]
    dnormed = nt(grads, w_qkv[...])
    for t in range(RING):
        put_by_distance(dnormeds, z, t, dnormed[128 * t : 128 * (t + 1), :].astype(bf16))
    xhat, _ = center_rows(span_tokens[...].astype(f32))
    gain_grad = jnp.sum(dnormed * xhat, axis=0, keepdims=True)
    shift_grad = jnp.sum(dnormed, axis=0, keepdims=True)
    ones = jnp.ones((8, 512), bf16)
    bias = dense(ones, grads)
    row = lax.broadcasted_iota(jnp.int32, (8, 768), 0)
    vec = sums[...]
    vec = jnp.where(row == 0, gain_grad, jnp.where(row == 1, shift_grad, vec))
    weight = tn(normed[...], grads)
    for t in range(RING):
        top = pieces([(vec, 3 * t + n) for n in range(3)] + [None])
        mine = z == t
        from_q = pieces([(bias, 6 + n) for n in range(3)] + [None])
        from_v = pieces([(bias, 3 + n) for n in range(3)] + [None])
        row8 = lax.broadcasted_iota(jnp.int32, (8, WIDE), 0)
        top = jnp.where(mine & (row8 == 2), from_q, jnp.where(mine & (row8 == 3), from_v, top))
        lines = jnp.zeros((8, WIDE), f32)
        up = jnp.broadcast_to(sum_up[:, 768 * t : 768 * (t + 1)], (8, 768))
        for q in range(4):
            line = pieces([(up, 3 * q + n) for n in range(3)] + [None])
            lines = jnp.where(row8 == q, line, lines)
        bottom = jnp.concatenate(
            [jnp.concatenate([top, lines], axis=0), jnp.zeros((16, 512), f32)], axis=1
        )
        mine = weight[GROUP_WIDTH * t : GROUP_WIDTH * (t + 1), :]
        made = []
        for n in range(3):
            block = mine[48 * n : 48 * (n + 1), :]
            side = [(block, 8)] + [(mine[144:, :], 3 * n + m) for m in range(3)]
            made.append(jnp.concatenate([block[:, :512], pieces(side)], axis=1))
        value = jnp.concatenate(made + [bottom], axis=0).astype(bf16)
        put_by_distance([ref.at[:160, :] for ref in lates], z, t, value)
        put_by_distance(
            [ref.at[160:, :] for ref in lates], z, t, early[240 + 48 * t : 288 + 48 * t, :]
        )


def end_norm_kernel(meta, n0, n1, n2, n3, tokens, vec, dmiddle, out):
    dnormed = sum(part[...].astype(f32) for part in (n0, n1, n2, n3))
    xhat, scale = center_rows(tokens[...].astype(f32))
    grad = dnormed * vec[0:1, :]
    out[...] = dmiddle[...] + scale * (
        grad
        - jnp.mean(grad, axis=-1, keepdims=True)
        - xhat * jnp.mean(grad * xhat, axis=-1, keepdims=True)
    )


def late_kernel(meta, *refs):
    parts, early = refs[:4], refs[4]
    keep, send, wide, ups, weight = refs[5:]
    core, z = meta[16], meta[17]
    vec = sum(part[144:160, :640].astype(f32) for part in parts).astype(bf16)
    wide[...] = early[:240, :].astype(f32)
    for k in range(RING):
        place = turn(z - k)
        ups[pl.ds(pl.multiple_of(place * 48, 16), 48), :] = parts[k][160:, :].astype(f32)
        weight[k, :144, :512] = parts[k][:144, :512]
        weight[k, :144, 512:] = pieces([(parts[k][:144, :], 8), None]).astype(bf16)
        tail = [(parts[k][48 * n : 48 * (n + 1), :], 9 + m) for n in range(3) for m in range(3)]
        weight[k, 144:, :] = pieces(tail + [None]).astype(bf16)
        to = pl.ds(pl.multiple_of(place * 96, 32), 96)
        for ref, side in ((keep, core), (send, 1 - core)):
            ref[to, :640] = weight[k, pl.ds(pl.multiple_of(side * 96, 32), 96), :]
            ref[to, 640:] = jnp.zeros((96, 128), bf16)
    for ref, side in ((keep, core), (send, 1 - core)):
        ref[384:400, :640] = vec
        ref[384:400, 640:] = jnp.zeros((16, 128), bf16)
        made = [wide[pl.ds(pl.multiple_of(side * 120, 8), 120), :]]
        for t in range(RING):
            made.append(ups[pl.ds(pl.multiple_of(48 * t + side * 24, 8), 24), :])
        made.append(jnp.zeros((8, 768), f32))
        ref[400:, :] = jnp.concatenate(made, axis=0).astype(bf16)


def late_sum_kernel(meta, keep, got, *refs):
    early, whole = refs[4], refs[5]
    whole[:400, :] = keep[:400, :640].astype(f32) + got[:400, :640].astype(f32)
    whole[400:, :] = jnp.zeros((48, 640), f32)
    cut_up(refs[:4], whole, meta[19])
    early[...] = (keep[400:, :].astype(f32) + got[400:, :].astype(f32)).astype(bf16)


def late_end_kernel(meta, *refs):
    key_grad, value_grad, query_grad = refs[4:7]
    lines, up_line, whole = refs[7:15], refs[15], refs[16]
    put_together(whole, refs[:4], meta[19])
    parts = [whole[96 * t : 96 * (t + 1), :] for t in range(RING)]
    for n, out in enumerate((key_grad, value_grad, query_grad)):
        out[...] = pieces([(parts[t], 3 * n + m) for t in range(RING) for m in range(3)])
    vec = whole[384:400, :WIDE]
    core = meta[16]
    turned = pltpu.roll(vec, WIDE - 96, 1)
    mine = jnp.where(core == 0, vec, turned)
    for n in range(8):
        lines[n][...] = mine[n, :96]
    first = jnp.where(core == 0, vec[8:9, :], vec[10:11, :])
    second = jnp.where(core == 0, vec[9:10, :], vec[11:12, :])
    spread_line = pieces(
        [(first, 0), (first, 1), (first, 2), (second, 0), (second, 1), (second, 2)]
    )
    up_line[...] = spread_line[0, :]


def on_device(
    tokens,
    span_order,
    first_gain,
    first_shift,
    query_weight,
    query_bias,
    key_weight,
    value_weight,
    value_bias,
    out_weight,
    out_bias,
    second_gain,
    second_shift,
    up_weight,
    up_bias,
    down_weight,
    down_bias,
    cotangent,
):
    shard_at = lax.axis_index("shard")
    z, core = shard_at // CORES, shard_at % CORES
    ctx_at = lax.axis_index("ctx")
    y, xq = ctx_at // RING, ctx_at % RING
    rows, width = tokens.shape
    low = ((rows, width), bf16)

    steps = jnp.arange(RING, dtype=jnp.int32)
    groups = jnp.concatenate([((y - steps) % RING) * RING + xq, y * RING + (xq - steps) % RING])
    stored = (2 * groups[:, None] + jnp.arange(2, dtype=jnp.int32)[None, :]).reshape(-1)
    found = stored[:, None] == jnp.arange(span_order.shape[0], dtype=jnp.int32)[None, :]
    spans = jnp.sum(jnp.where(found, span_order[None, :], 0), axis=1)
    meta = jnp.concatenate([spans, jnp.stack([core, z, xq, y]).astype(jnp.int32)])

    vectors = (
        first_gain,
        first_shift,
        query_bias,
        value_bias,
        out_bias,
        second_gain,
        second_shift,
        down_bias,
        up_bias,
    )
    chunks = run(
        arrange_kernel,
        "arrange_weights",
        [((240, width), bf16)] * 4,
        (meta, tokens, key_weight, value_weight, query_weight, *vectors),
        scratch=[pltpu.VMEM((16, 128), f32)],
    )
    arrived = deliver(chunks, move_z)
    out_down = jnp.concatenate([out_weight, down_weight], axis=0)
    arrived, out_down, up_own, cot_own = lax.optimization_barrier(
        (arrived, out_down, up_weight, cotangent)
    )
    arrived_others = [swap_core(part) for part in arrived]
    w_out_down = lax.all_gather(out_down, "shard", axis=0, tiled=True)
    w_up = lax.all_gather(up_own, "shard", axis=0, tiled=True)
    cot_all = lax.all_gather(cot_own, "shard", axis=0, tiled=True)
    span_tokens, normed, queries, kv_own, w_qkv, vec, b_up = run(
        project_kernel,
        "project",
        [
            ((512, width), bf16),
            ((512, width), bf16),
            ((512, WIDE), bf16),
            ((512, 384), bf16),
            ((width, 640), bf16),
            ((16, width), f32),
            ((1, 4 * width), f32),
        ],
        (meta, *arrived, *arrived_others),
        scratch=[pltpu.VMEM((8, 16, 128), bf16)],
    )
    kv_parts = spread(kv_own, move_x)
    queries_all = spread(queries, move_y)
    kv_parts, queries_all = lax.optimization_barrier((kv_parts, queries_all))
    kv_others = [swap_core(part) for part in kv_parts]
    partial = forward_call(meta, queries_all, kv_parts, kv_others)

    context, *context_chunks = run(
        merge_groups_kernel,
        "merge_groups",
        [((512, WIDE), bf16)] + [((128, WIDE), bf16)] * 4,
        (meta, *give_back(partial, move_y)),
    )
    far = pl.BlockSpec(memory_space=pl.ANY)
    middle = run(
        middle_kernel,
        "feed_forward",
        [low, ((rows, width), f32)]
        + [((4 * rows, width), bf16)] * 4
        + [((128, GROUP_WIDTH), bf16)] * 4
        + [((8, width), f32), ((1, 4 * width), f32)],
        (
            meta,
            tokens,
            cotangent,
            *deliver(context_chunks, move_z),
            w_out_down,
            w_up,
            vec,
            b_up,
        ),
        specs=[SM] + [VM] * 6 + [far, far, VM, VM],
        scratch=[
            pltpu.VMEM((width, width), bf16),
            pltpu.VMEM((width, 4 * width), bf16),
            pltpu.VMEM((4 * width, width), bf16),
            pltpu.SemaphoreType.DMA,
            pltpu.SemaphoreType.DMA((2 * RING, 2)),
        ],
    )
    activations, dmiddle = middle[:2]
    early_sent, dcontexts = middle[2:6], middle[6:10]
    sums, sum_up = middle[10:]

    (packed,) = run(
        pack_kernel,
        "pack_context_gradient",
        [((512, WIDE), bf16)],
        (meta, *deliver(dcontexts, move_z), context),
        scratch=[pltpu.VMEM((512, GROUP_WIDTH), bf16)],
    )
    packed, early_sent = lax.optimization_barrier((packed, early_sent))
    grads_all = spread(packed, move_y)
    early_parts = deliver(early_sent, move_z)
    dkv_own, dkv_oth, dq_so_far = backward_call(
        1, meta, queries_all, grads_all, kv_parts[1:], kv_others[1:]
    )

    dkv_oth, dq_so_far, early_parts = lax.optimization_barrier((dkv_oth, dq_so_far, early_parts))
    (early,) = run(
        early_kernel,
        "early_gradients",
        [((1728, width), bf16)],
        (meta, *early_parts, context, cot_all),
        specs=[SM] + [VM] * 5 + [far],
        scratch=[
            pltpu.VMEM((RING, rows, width), bf16),
            pltpu.SemaphoreType.DMA((RING,)),
        ],
    )
    dkv_got = swap_core(dkv_oth)
    dq_so_far, early, dkv_got = lax.optimization_barrier((dq_so_far, early, dkv_got))
    early = lax.psum_scatter(
        early, "ctx", axis_index_groups=COLUMN_GROUPS, scatter_dimension=0, tiled=True
    )
    dkv_sums = [sum_low([dkv_own[k], dkv_got[512 * k : 512 * (k + 1)]]) for k in range(3)]
    dkv_arrived = [move_x(dkv_sums[k], -1 - k) for k in range(3)]
    dkv_own0, dkv_oth0, dqs = backward_call(
        0, meta, queries_all, grads_all, kv_parts[:1], kv_others[:1], *dq_so_far, last=True
    )
    dqs, dkv_oth0, dkv_arrived = lax.optimization_barrier((dqs, dkv_oth0, dkv_arrived))
    dq_arrived = give_back(dqs, move_y)
    dkv_got0 = swap_core(dkv_oth0)

    collected = run(
        collect_kernel,
        "collect",
        [low] * 4 + [((208, width), bf16)] * 4,
        (
            meta,
            *dq_arrived,
            dkv_own0[0],
            dkv_got0,
            *dkv_arrived,
            normed,
            span_tokens,
            w_qkv,
            sums,
            sum_up,
            early,
        ),
        scratch=[pltpu.VMEM((512, 640), bf16)],
    )
    late_parts = deliver(collected[4:], move_z)
    late_keep, late_send = run(
        late_kernel,
        "late",
        [((624, width), bf16)] * 2,
        (meta, *late_parts, early),
        scratch=[
            pltpu.VMEM((240, width), f32),
            pltpu.VMEM((192, width), f32),
            pltpu.VMEM((RING, GROUP_WIDTH, 640), bf16),
        ],
    )
    *late_chunks, early = run(
        late_sum_kernel,
        "late_sum",
        [((112, 640), bf16)] * 4 + [((224, width), bf16)],
        (meta, late_keep, swap_core(late_send)),
        scratch=[pltpu.VMEM((448, 640), f32)],
    )
    late_arrived = deliver(late_chunks, move_y)
    early_parts = spread(early, move_x)
    late_arrived, early_parts = lax.optimization_barrier((late_arrived, early_parts))
    early_total = lax.all_gather(
        sum_low(early_parts), "ctx", axis_index_groups=COLUMN_GROUPS, axis=0, tiled=True
    )
    late_parts = spread(sum_low(late_arrived), move_x)
    late_parts, dnormed_sent = lax.optimization_barrier((late_parts, collected[:4]))
    dnormed_parts = deliver(dnormed_sent, move_z)
    (input_grad,) = run(
        end_norm_kernel,
        "end_norm",
        [((rows, width), f32)],
        (meta, *dnormed_parts, tokens, vec, dmiddle),
    )
    late_sums = spread(sum_low(late_parts), move_y)
    late_sums, input_grad = lax.optimization_barrier((late_sums, input_grad))
    grad_down, grad_out, grad_up = run(
        early_end_kernel,
        "early_end",
        [((384, width), f32), ((96, width), f32), ((96, 4 * width), f32)],
        (meta, early_total),
    )
    key_grad, value_grad, query_grad, *vec_grads = run(
        late_end_kernel,
        "late_end",
        [((96, width), f32)] * 3 + [((96,), f32)] * 8 + [((384,), f32)],
        (meta, *late_sums),
        scratch=[pltpu.VMEM((448, 640), f32)],
    )
    return (
        activations,
        input_grad,
        vec_grads[0],
        vec_grads[1],
        query_grad,
        vec_grads[2],
        key_grad,
        value_grad,
        vec_grads[3],
        grad_out,
        vec_grads[4],
        vec_grads[5],
        vec_grads[6],
        grad_up,
        vec_grads[8],
        grad_down,
        vec_grads[7],
    )


def solution(mesh):
    tokens_spec = P(("ctx", "shard"), None)
    vector_spec = P("shard")
    matrix_spec = P("shard", None)
    return jax.shard_map(
        on_device,
        mesh=mesh,
        in_specs=(
            tokens_spec,
            P(),
            vector_spec,
            vector_spec,
            matrix_spec,
            vector_spec,
            matrix_spec,
            matrix_spec,
            vector_spec,
            matrix_spec,
            vector_spec,
            vector_spec,
            vector_spec,
            matrix_spec,
            vector_spec,
            matrix_spec,
            vector_spec,
            tokens_spec,
        ),
        out_specs=(
            tokens_spec,
            tokens_spec,
            vector_spec,
            vector_spec,
            matrix_spec,
            vector_spec,
            matrix_spec,
            matrix_spec,
            vector_spec,
            matrix_spec,
            vector_spec,
            vector_spec,
            vector_spec,
            matrix_spec,
            vector_spec,
            matrix_spec,
            vector_spec,
        ),
        check_vma=False,
    )
```
